32 devices in a mesh: dp: 4 (over x, core), seq: 8 (over z, y).
Axes of the slice: x: 2, y: 2, z: 4, core: 2. Of those that a mesh axis runs over, the one named last changes fastest.
Arguments:
- frames: bfloat16 [4, 1024, 1024], P('dp', 'seq'), may hold values from -6 to 6
- skip: bfloat16 [4, 1024, 1024], P('dp', 'seq'), may hold values from -6 to 6
- lengths: int32 [4, 8], P('dp'), may hold values from 1 to 897, 1024 in all within a row
- frame_mask: int32 [4, 1024], P('dp', 'seq'), may hold values 0 or 1
- time_step: int32 [4, 8], P('dp'), may hold values from 0 to 31
- w_skip: bfloat16 [2048, 1024], replicated, may hold values from -0.125 to 0.125
- w_ada: bfloat16 [1024, 2048], replicated, may hold values from -0.1875 to 0.1875
- b_ada: bfloat16 [2048], replicated, may hold values from -4 to 4
- w_qkv: bfloat16 [1024, 3072], replicated, may hold values from -0.1875 to 0.1875
- w_out: bfloat16 [1024, 1024], replicated, may hold values from -0.5 to 0.5
- norm_gain: bfloat16 [1024], replicated, may hold values from 0.25 to 1.75
- w_up: bfloat16 [1024, 4096], replicated, may hold values from -0.1875 to 0.1875
- b_up: bfloat16 [4096], replicated, may hold values from -6 to 6
- w_down: bfloat16 [4096, 1024], replicated, may hold values from -0.09375 to 0.09375
- b_down: bfloat16 [1024], replicated, may hold values from -4 to 4
- cotangent: bfloat16 [4, 1024, 1024], P('dp', 'seq'), may hold values from -6 to 6
Outputs:
- result: bfloat16 [4, 1024, 1024], P('dp', 'seq')
- grad_frames: float32 [4, 1024, 1024], P('dp', 'seq')
- grad_skip_in: float32 [4, 1024, 1024], P('dp', 'seq')
- grad_w_skip: float32 [2048, 1024], P('seq')
- grad_w_ada: float32 [1024, 2048], P('seq')
- grad_b_ada: float32 [2048], P('seq')
- grad_w_qkv: float32 [1024, 3072], P('seq')
- grad_w_out: float32 [1024, 1024], P('seq')
- grad_gain: float32 [1024], P('seq')
- grad_w_up: float32 [1024, 4096], P('seq')
- grad_b_up: float32 [4096], P('seq')
- grad_w_down: float32 [4096, 1024], P('seq')
- grad_b_down: float32 [1024], P('seq')
The draws below stay inside these ranges and needn't reach their ends.
Inputs may be any that keep to these rules, and one draw needn't show every extreme that they name: In each row the 8 lengths sum to 1024, and the longest is exactly 897.
All inputs are finite; a program needn't handle non-finite values. No bound on the sum of `frame_mask` on one device may be relied on, other than what follows from the above.
Results may differ from the reference program's by a relative error of at most 0.02.
Values may be sent and summed in bfloat16 or wider, within the bound.
A program may use at most 320 MiB of HBM per device.

```python
import math
import jax
import jax.numpy as jnp
import numpy as np
from jax import lax

D = 1024
HEADS = 16
HEAD = 64
FF = 4096
F_DEV = 128
NU = 8
TSTEPS = 32
LEN = 1024
BATCH = 4


def set_ends(entries, key, low, top_value):
    longest = entries.shape.index(max(entries.shape))
    spots = []
    for shift in (0, 1):
        where = [jax.random.randint(jax.random.fold_in(key, axis), (), 0, length) for axis, length in enumerate(entries.shape)]
        where[longest] = (where[longest] + shift) % entries.shape[longest]
        spots.append(tuple(where))
    return entries.at[spots[0]].set(low).at[spots[1]].set(top_value)


def block_levels(own_key, dims, shards, least, largest):
    level, own = 1.0, jax.random.fold_in(own_key, 6)
    for axis_at, shards_of in shards:
        draws = jnp.exp(jax.random.uniform(jax.random.fold_in(own, axis_at), (shards_of,), jnp.float32, least / len(shards), largest / len(shards)))
        level = level * jnp.repeat(draws, dims[axis_at] // shards_of).reshape([-1 if axis == axis_at else 1 for axis in range(len(dims))])
    return level


def split_up(count, total, most, slope):
    loads = [(1 << 20) // math.isqrt(rank ** slope) + 1 for rank in range(2, count + 1)]
    surplus, counts = total - most - (count - 1), [1] * (count - 1)
    while surplus > 0:
        candidates = [i for i in range(count - 1) if counts[i] < most]
        pool, left = sum([loads[i] for i in candidates]), surplus
        for i in candidates:
            extra = min(most - counts[i], max(1, left * loads[i] // pool), surplus)
            counts[i] = counts[i] + extra
            surplus = surplus - extra
    return np.array([most] + counts)


def ragged(stream_key, count, total, reach, skew):
    if count == 2:
        one = jax.random.randint(stream_key, (), max(1, total - reach), min(reach, total - 1) + 1)
        return jnp.stack([one, total - one])
    sizes = jnp.asarray(split_up(count, total, reach, skew), jnp.int32)
    pairs = (count - 1) // 2
    giver, taker = sizes[1:1 + 2 * pairs:2], sizes[2:2 + 2 * pairs:2]
    margin = jnp.minimum(giver - 1, reach - taker)
    moved = jax.random.randint(jax.random.fold_in(stream_key, 1), (pairs,), 0, 1 << 20) % (margin + 1)
    sizes = sizes.at[1:1 + 2 * pairs:2].set(giver - moved).at[2:2 + 2 * pairs:2].set(taker + moved)
    return sizes[jax.random.permutation(jax.random.fold_in(stream_key, 2), count)]


def centred(own_key, shape, scale, bound, split=(), held_as=jnp.bfloat16):
    gain = block_levels(own_key, shape, split, -0.22, 0.18) if split else 1.0
    drawn = jax.random.normal(own_key, shape, jnp.float32) * scale * gain
    return jnp.minimum(jnp.maximum(drawn, -bound), bound).astype(held_as)


def setup_inputs(seed: int = 0) -> dict:
    keys = jax.random.split(jax.random.key(seed), 17)
    frames = centred(keys[0], (BATCH, LEN, D), 1.0, 6.0, ((0, 4), (1, 8)))
    skip = centred(keys[1], (BATCH, LEN, D), 1.0, 6.0, ((0, 4), (1, 8)))
    lengths = jax.vmap(lambda own: ragged(own, NU, LEN, LEN - F_DEV + 1, 2))(jax.random.split(keys[2], BATCH)).reshape((BATCH, NU)).astype(jnp.int32)
    frame_mask = set_ends((jax.random.randint(keys[3], (BATCH, LEN), 0, 8) < 7).astype(jnp.int32), jax.random.fold_in(keys[3], 1), 0, 1)
    time_step = set_ends(jax.random.randint(keys[4], (BATCH, NU), 0, TSTEPS), jax.random.fold_in(keys[4], 1), 0, TSTEPS - 1).astype(jnp.int32)
    w_skip = centred(keys[5], (2 * D, D), (2 * D) ** -0.5, 0.125)
    w_ada = centred(keys[6], (D, 2 * D), D ** -0.5, 0.1875)
    b_ada = centred(keys[7], (2 * D,), 0.3, 4.0)
    w_qkv = centred(keys[8], (D, 3 * D), D ** -0.5, 0.1875)
    w_out = centred(keys[9], (D, D), (D // 8) ** -0.5, 0.5)
    norm_gain = jnp.clip(1.0 + 0.15 * jax.random.normal(keys[10], (D,), jnp.float32), 0.25, 1.75).astype(jnp.bfloat16)
    w_up = centred(keys[11], (D, FF), D ** -0.5, 0.1875)
    b_up = centred(keys[12], (FF,), 0.5, 6.0)
    w_down = centred(keys[13], (FF, D), FF ** -0.5, 0.09375)
    b_down = centred(keys[14], (D,), 0.3, 4.0)
    cotangent = centred(keys[15], (BATCH, LEN, D), 1.0, 6.0, ((0, 4), (1, 8)))
    return dict(frames=frames, skip=skip, lengths=lengths, frame_mask=frame_mask, time_step=time_step, w_skip=w_skip, w_ada=w_ada, b_ada=b_ada, w_qkv=w_qkv, w_out=w_out, norm_gain=norm_gain, w_up=w_up, b_up=b_up, w_down=w_down, b_down=b_down, cotangent=cotangent)


@jax.custom_vjp
def low(v):
    return lax.optimization_barrier(v.astype(jnp.bfloat16)).astype(jnp.float32)

@jax.custom_vjp
def low_back(v):
    return v

def low_keep(v):
    return (low(v), None)

def low_pass(kept, grad):
    return (grad,)

def back_keep(v):
    return (v, None)

def back_low(kept, grad):
    return (low(grad),)
low.defvjp(low_keep, low_pass)
low_back.defvjp(back_keep, back_low)
precise = lax.Precision.HIGHEST
masked_score = -1e+30

def divisor_below(count_all, upper_limit):
    size_now = min(count_all, upper_limit)
    while count_all % size_now:
        size_now -= 1
    return size_now

def normalize(values):
    centered = values - lax.optimization_barrier(jnp.mean(values, axis=-1, keepdims=True))
    variance = lax.optimization_barrier(jnp.mean(centered * centered, axis=-1, keepdims=True))
    return centered * lax.rsqrt(variance + 1e-06)

def segment_of(lengths, frame_index):
    utter_ends = jnp.cumsum(lengths).astype(jnp.int32)
    return lax.optimization_barrier(jnp.sum((frame_index[:, None] >= utter_ends[None, :]).astype(jnp.int32), axis=1))

def utterance_layout(lengths, frame_index):
    utter_ends = jnp.cumsum(lengths).astype(jnp.int32)
    starts = utter_ends - lengths
    segment = segment_of(lengths, frame_index)
    member = segment[:, None] == jnp.arange(lengths.shape[0], dtype=jnp.int32)[None, :]
    position = frame_index - lax.optimization_barrier(jnp.sum(jnp.where(member, starts[None, :], 0), axis=1))
    return (segment, position, member)

def rotary_tables(position, head_size):
    half_size = head_size // 2
    frequency = jnp.exp(jnp.arange(half_size, dtype=jnp.float32) * (-2.0 * math.log(10000.0) / head_size))
    angles = position.astype(jnp.float32)[:, None] * frequency[None, :]
    return (jnp.cos(angles)[:, None, :], jnp.sin(angles)[:, None, :])

def rotate(values, cos_table, sin_table):
    half_size = values.shape[-1] // 2
    first_half = values[..., :half_size]
    second_half = values[..., half_size:]
    return jnp.concatenate([first_half * cos_table - second_half * sin_table, second_half * cos_table + first_half * sin_table], axis=-1)

def time_embedding(steps, model_width):
    half_size = model_width // 2
    flow_time = steps.astype(jnp.float32) / TSTEPS
    frequency = jnp.exp(jnp.arange(half_size, dtype=jnp.float32) * (-math.log(10000.0) / half_size))
    angles = 1000.0 * flow_time[:, None] * frequency[None, :]
    return jnp.concatenate([jnp.sin(angles), jnp.cos(angles)], axis=1)

def attention_rows(queries, key_rows, value_rows, segment, valid, frame_index):
    count_all, head_count, head_size = queries.shape
    block_rows = divisor_below(count_all, 512)
    block_count = count_all // block_rows

    def attend_block(inputs):
        query_block, segment_block, index_block = inputs
        scores = low_back(jnp.einsum('qhd,khd->hqk', query_block, key_rows, precision=precise) / math.sqrt(head_size))
        allowed = (segment_block[:, None] == segment[None, :]) & ((valid[None, :] > 0) | (index_block[:, None] == frame_index[None, :]))
        scores = jnp.where(allowed[None], scores, masked_score)
        row_top = lax.optimization_barrier(jnp.max(scores, axis=2, keepdims=True))
        weights = jnp.exp(scores - row_top)
        weights = weights / lax.optimization_barrier(jnp.sum(weights, axis=2, keepdims=True))
        return jnp.einsum('hqk,khd->qhd', low(weights), value_rows, precision=precise)
    outputs = lax.map(jax.checkpoint(attend_block), (queries.reshape(block_count, block_rows, head_count, head_size), segment.reshape(block_count, block_rows), frame_index.reshape(block_count, block_rows)))
    return outputs.reshape(count_all, head_count * head_size)

def row_forward(joined, segment, position, member, valid, frame_index, embed_low, w_skip, w_ada, b_ada, w_qkv, w_out, norm_gain, w_up, b_up, w_down, b_down):
    count_all = joined.shape[0]
    model_width = w_out.shape[0]
    residual_in = low_back(jnp.dot(joined, w_skip, precision=precise))
    ada_table = jnp.dot(embed_low, w_ada, precision=precise) + b_ada
    ada_frame = jnp.dot(member.astype(jnp.float32), ada_table, precision=precise)
    first_in = low(normalize(residual_in) * (1.0 + ada_frame[:, :model_width]) + ada_frame[:, model_width:])
    packed = low_back(jnp.dot(first_in, w_qkv, precision=precise))
    cos_table, sin_table = rotary_tables(position, HEAD)
    queries = low(rotate(packed[:, :model_width].reshape(count_all, HEADS, HEAD), cos_table, sin_table))
    key_rows = low(rotate(packed[:, model_width:2 * model_width].reshape(count_all, HEADS, HEAD), cos_table, sin_table))
    value_rows = low(packed[:, 2 * model_width:].reshape(count_all, HEADS, HEAD))
    attn_sum = attention_rows(queries, key_rows, value_rows, segment, valid, frame_index)
    attn_low = low(low_back(attn_sum))
    residual_mid = residual_in + low_back(jnp.dot(attn_low, w_out, precision=precise))
    second_in = low(normalize(residual_mid) * norm_gain)
    upper_sum = low_back(jnp.dot(second_in, w_up, precision=precise) + b_up)
    gated_in = low(jax.nn.gelu(upper_sum, approximate=True))
    lower_sum = low_back(jnp.dot(gated_in, w_down, precision=precise) + b_down)
    return residual_mid + lower_sum

def reference(frames, skip, lengths, frame_mask, time_step, w_skip, w_ada, b_ada, w_qkv, w_out, norm_gain, w_up, b_up, w_down, b_down, cotangent):
    row_count, count_all, model_width = frames.shape
    frame_index = jnp.arange(count_all, dtype=jnp.int32)
    layouts = [utterance_layout(lengths[number], frame_index) for number in range(row_count)]
    embeds = [low(time_embedding(time_step[number], model_width)) for number in range(row_count)]
    floats = tuple((argument.astype(jnp.float32) for argument in (frames, skip, w_skip, w_ada, b_ada, w_qkv, w_out, norm_gain, w_up, b_up, w_down, b_down)))

    def forward(frames_in, skip_in, skip_weight, ada_weight, ada_bias, qkv_weight, out_weight, gain_vector, up_weight, up_bias, down_weight, down_bias):
        outputs = []
        for number in range(row_count):
            segment, position, member = layouts[number]
            joined = jnp.concatenate([frames_in[number], skip_in[number]], axis=1)
            outputs.append(row_forward(joined, segment, position, member, frame_mask[number], frame_index, embeds[number], skip_weight, ada_weight, ada_bias, qkv_weight, out_weight, gain_vector, up_weight, up_bias, down_weight, down_bias))
        return jnp.stack(outputs)
    output, pullback = jax.vjp(forward, *floats)
    grads = pullback(cotangent.astype(jnp.float32))
    return (output.astype(jnp.bfloat16), grads[0], grads[1], grads[2], grads[3], grads[4], grads[5], grads[6], grads[7], grads[8], grads[9], grads[10], grads[11])
```

```python
import math

import jax
import jax.numpy as jnp
from jax import lax
from jax.experimental import pallas as pl
from jax.experimental.pallas import tpu as pltpu
from jax.sharding import PartitionSpec as P

HEADS = 16
HEAD = 64
TSTEPS = 32


precise = lax.Precision.HIGHEST
masked_score = -1e30
contract_rows = (((0,), (0,)), ((), ()))
contract_cols = (((1,), (1,)), ((), ()))


def divisor_below(count_all, upper_limit):
    size_now = min(count_all, upper_limit)
    while count_all % size_now:
        size_now -= 1
    return size_now


def normalize(values):
    centered = values - jnp.mean(values, axis=-1, keepdims=True)
    variance = jnp.mean(centered * centered, axis=-1, keepdims=True)
    return centered * lax.rsqrt(variance + 1e-06)


def segment_of(lengths, frame_index):
    utter_ends = jnp.cumsum(lengths)
    return jnp.sum((frame_index[:, None] >= utter_ends[None, :]).astype(jnp.int32), axis=1)


def utterance_layout(lengths, frame_index):
    utter_ends = jnp.cumsum(lengths)
    starts = utter_ends - lengths
    segment = segment_of(lengths, frame_index)
    member = segment[:, None] == jnp.arange(lengths.shape[0], dtype=jnp.int32)[None, :]
    position = frame_index - jnp.sum(jnp.where(member, starts[None, :], 0), axis=1)
    return (segment, position, member)


def rotary_tables(position, head_size):
    half_size = head_size // 2
    frequency = jnp.exp(
        jnp.arange(half_size, dtype=jnp.float32) * (-2.0 * math.log(10000.0) / head_size)
    )
    angles = position.astype(jnp.float32)[:, None] * frequency[None, :]
    return (jnp.cos(angles)[:, None, :], jnp.sin(angles)[:, None, :])


def rotate(values, cos_table, sin_table):
    half_size = values.shape[-1] // 2
    first_half = values[..., :half_size]
    second_half = values[..., half_size:]
    return jnp.concatenate(
        [
            first_half * cos_table - second_half * sin_table,
            second_half * cos_table + first_half * sin_table,
        ],
        axis=-1,
    )


def rotate_back(values, cos_table, sin_table):
    half_size = values.shape[-1] // 2
    first_half = values[..., :half_size]
    second_half = values[..., half_size:]
    return jnp.concatenate(
        [
            first_half * cos_table + second_half * sin_table,
            second_half * cos_table - first_half * sin_table,
        ],
        axis=-1,
    )


def time_embedding(steps, model_width):
    half_size = model_width // 2
    flow_time = steps.astype(jnp.float32) / TSTEPS
    frequency = jnp.exp(jnp.arange(half_size, dtype=jnp.float32) * (-math.log(10000.0) / half_size))
    angles = 1000.0 * flow_time[:, None] * frequency[None, :]
    return jnp.concatenate([jnp.sin(angles), jnp.cos(angles)], axis=1)


def make_attend(query_low, query_segment, query_index, lengths):
    count_rows, head_count, head_size = query_low.shape
    scale_factor = 1.0 / math.sqrt(head_size)

    def attend(running, key_piece, first_row):
        keys_part, values_part, valid_part = key_piece
        count_keys = keys_part.shape[0]
        block_rows = divisor_below(count_keys, 1024)
        block_count = count_keys // block_rows
        key_blocks = keys_part.reshape(block_count, block_rows, head_count, head_size)
        value_blocks = values_part.reshape(block_count, block_rows, head_count, head_size)
        valid_blocks = valid_part.reshape(block_count, block_rows)
        offsets = first_row + jnp.arange(block_count, dtype=jnp.int32) * block_rows

        def attend_block_step(carried, inputs):
            row_top, row_total, weighted = carried
            key_block, value_block, valid_block, offset = inputs
            key_index = offset + jnp.arange(block_rows, dtype=jnp.int32)
            key_segment = segment_of(lengths, key_index)
            allowed = (query_segment[:, None] == key_segment[None, :]) & (
                (valid_block[None, :] > 0) | (query_index[:, None] == key_index[None, :])
            )
            scores = (
                jnp.einsum("qhd,khd->hqk", query_low, key_block, preferred_element_type=jnp.float32)
                * scale_factor
            )
            scores = jnp.where(allowed[None], scores, masked_score)
            new_top = jnp.maximum(row_top, jnp.max(scores, axis=2))
            weights = jnp.where(allowed[None], jnp.exp(scores - new_top[:, :, None]), 0.0)
            factor = jnp.exp(row_top - new_top)
            row_total = row_total * factor + jnp.sum(weights, axis=2)
            weighted = weighted * jnp.transpose(factor)[:, :, None] + jnp.einsum(
                "hqk,khd->qhd",
                weights.astype(jnp.bfloat16),
                value_block,
                preferred_element_type=jnp.float32,
            )
            return ((new_top, row_total, weighted), None)

        result_state, unused = lax.scan(
            attend_block_step, running, (key_blocks, value_blocks, valid_blocks, offsets)
        )
        return result_state

    return attend


def key_sweep(
    query_low, grad_attn, log_total, row_delta, query_segment, query_index, lengths, key_tuple
):
    keys_all, values_all, valid_all = key_tuple
    count_rows, head_count, head_size = query_low.shape
    scale_factor = 1.0 / math.sqrt(head_size)
    count_keys = keys_all.shape[0]
    block_rows = divisor_below(count_keys, 1024)
    block_count = count_keys // block_rows
    key_blocks = keys_all.reshape(block_count, block_rows, head_count, head_size)
    value_blocks = values_all.reshape(block_count, block_rows, head_count, head_size)
    valid_blocks = valid_all.reshape(block_count, block_rows)
    offsets = jnp.arange(block_count, dtype=jnp.int32) * block_rows
    top_shift = jnp.transpose(log_total)[:, :, None]
    delta_shift = jnp.transpose(row_delta)[:, :, None]

    def key_block_step(grad_query, inputs):
        key_block, value_block, valid_block, offset = inputs
        key_index = offset + jnp.arange(block_rows, dtype=jnp.int32)
        key_segment = segment_of(lengths, key_index)
        allowed = (query_segment[:, None] == key_segment[None, :]) & (
            (valid_block[None, :] > 0) | (query_index[:, None] == key_index[None, :])
        )
        scores = (
            jnp.einsum("qhd,khd->hqk", query_low, key_block, preferred_element_type=jnp.float32)
            * scale_factor
        )
        weights = jnp.where(allowed[None], jnp.exp(scores - top_shift), 0.0)
        grad_weights = jnp.einsum(
            "qhd,khd->hqk", grad_attn, value_block, preferred_element_type=jnp.float32
        )
        grad_scores = (weights * (grad_weights - delta_shift)).astype(jnp.bfloat16)
        grad_query = (
            grad_query
            + jnp.einsum("hqk,khd->qhd", grad_scores, key_block, preferred_element_type=jnp.float32)
            * scale_factor
        )
        grad_key = (
            jnp.einsum("hqk,qhd->khd", grad_scores, query_low, preferred_element_type=jnp.float32)
            * scale_factor
        )
        grad_value = jnp.einsum(
            "hqk,qhd->khd",
            weights.astype(jnp.bfloat16),
            grad_attn,
            preferred_element_type=jnp.float32,
        )
        return (grad_query, (grad_key, grad_value))

    start_grad = jnp.zeros((count_rows, head_count, head_size), jnp.float32)
    return lax.scan(key_block_step, start_grad, (key_blocks, value_blocks, valid_blocks, offsets))


def on_device(
    frames,
    skip,
    lengths,
    frame_mask,
    time_step,
    w_skip,
    w_ada,
    b_ada,
    w_qkv,
    w_out,
    norm_gain,
    w_up,
    b_up,
    w_down,
    b_down,
    cotangent,
):
    local_frames = frames[0]
    local_skip = skip[0]
    row_lengths = lengths[0]
    count_rows, model_width = local_frames.shape
    head_count = HEADS
    head_size = HEAD
    row_base = lax.axis_index("seq") * count_rows
    frame_index = row_base + jnp.arange(count_rows, dtype=jnp.int32)
    segment, position, member = utterance_layout(row_lengths, frame_index)
    member_float = member.astype(jnp.float32)
    embed_low = time_embedding(time_step[0], model_width).astype(jnp.bfloat16)
    ada_table = jnp.dot(embed_low, w_ada, preferred_element_type=jnp.float32) + b_ada.astype(
        jnp.float32
    )
    ada_frame = jnp.dot(member_float, ada_table, precision=precise)
    scale_part = ada_frame[:, :model_width]
    shift_part = ada_frame[:, model_width:]
    joined = jnp.concatenate([local_frames, local_skip], axis=1)
    residual_in = jnp.dot(joined, w_skip, preferred_element_type=jnp.float32)
    norm_first, first_pull = jax.vjp(normalize, residual_in)
    first_low = (norm_first * (1.0 + scale_part) + shift_part).astype(jnp.bfloat16)
    packed = jnp.dot(first_low, w_qkv, preferred_element_type=jnp.float32)
    cos_table, sin_table = rotary_tables(position, head_size)
    query_low = rotate(
        packed[:, :model_width].reshape(count_rows, head_count, head_size), cos_table, sin_table
    ).astype(jnp.bfloat16)
    keys_low = (
        rotate(
            packed[:, model_width : 2 * model_width].reshape(count_rows, head_count, head_size),
            cos_table,
            sin_table,
        )
        .astype(jnp.bfloat16)
        .reshape(count_rows, model_width)
    )
    values_low = packed[:, 2 * model_width :].astype(jnp.bfloat16)
    valid_low = frame_mask[0].astype(jnp.bfloat16)
    attend = make_attend(query_low, segment, frame_index, row_lengths)
    start_state = (
        jnp.full((head_count, count_rows), masked_score, jnp.float32),
        jnp.zeros((head_count, count_rows), jnp.float32),
        jnp.zeros((count_rows, head_count, head_size), jnp.float32),
    )
    gathered = (
        lax.all_gather(keys_low, "seq", axis=0, tiled=True),
        lax.all_gather(values_low, "seq", axis=0, tiled=True),
        lax.all_gather(valid_low, "seq", axis=0, tiled=True),
    )
    row_top, row_total, weighted = attend(start_state, gathered, 0)
    attn_sum = weighted / jnp.transpose(row_total)[:, :, None]
    log_total = jnp.transpose(row_top + jnp.log(row_total))
    attn_low = attn_sum.reshape(count_rows, model_width).astype(jnp.bfloat16)
    residual_mid = residual_in + jnp.dot(attn_low, w_out, preferred_element_type=jnp.float32)
    gain_float = norm_gain.astype(jnp.float32)
    second_float, second_pull = jax.vjp(
        lambda hidden, gain_vector: normalize(hidden) * gain_vector, residual_mid, gain_float
    )
    second_low = second_float.astype(jnp.bfloat16)
    upper_sum = jnp.dot(second_low, w_up, preferred_element_type=jnp.float32) + b_up.astype(
        jnp.float32
    )
    gated_float, gelu_pull = jax.vjp(
        lambda hidden: jax.nn.gelu(hidden, approximate=True), upper_sum
    )
    gated_low = gated_float.astype(jnp.bfloat16)
    output = (
        residual_mid
        + jnp.dot(gated_low, w_down, preferred_element_type=jnp.float32)
        + b_down.astype(jnp.float32)
    )
    grad_out = cotangent[0]
    grad_out_float = grad_out.astype(jnp.float32)
    grad_down = lax.dot_general(
        gated_low, grad_out, contract_rows, preferred_element_type=jnp.float32
    )
    grad_down_bias = jnp.sum(grad_out_float, axis=0)
    grad_gated = lax.dot_general(
        grad_out, w_down, contract_cols, preferred_element_type=jnp.float32
    )
    grad_upper = gelu_pull(grad_gated)[0].astype(jnp.bfloat16)
    grad_up = lax.dot_general(
        second_low, grad_upper, contract_rows, preferred_element_type=jnp.float32
    )
    grad_up_bias = jnp.sum(grad_upper.astype(jnp.float32), axis=0)
    grad_second = lax.dot_general(
        grad_upper, w_up, contract_cols, preferred_element_type=jnp.float32
    )
    grad_mid_norm, grad_gain = second_pull(grad_second)
    grad_mid = grad_out_float + grad_mid_norm
    grad_branch = grad_mid.astype(jnp.bfloat16)
    grad_out_weight = lax.dot_general(
        attn_low, grad_branch, contract_rows, preferred_element_type=jnp.float32
    )
    grad_attn = (
        lax.dot_general(grad_branch, w_out, contract_cols, preferred_element_type=jnp.float32)
        .astype(jnp.bfloat16)
        .reshape(count_rows, head_count, head_size)
    )
    row_delta = jnp.sum(grad_attn.astype(jnp.float32) * attn_sum, axis=2)
    grad_query, key_parts = key_sweep(
        query_low, grad_attn, log_total, row_delta, segment, frame_index, row_lengths, gathered
    )
    grad_key_all, grad_value_all = key_parts
    total_keys = grad_key_all.shape[0] * grad_key_all.shape[1]
    grad_key, grad_value = (
        lax.psum_scatter(
            grad_key_all.reshape(total_keys, model_width), "seq", scatter_dimension=0, tiled=True
        ),
        lax.psum_scatter(
            grad_value_all.reshape(total_keys, model_width), "seq", scatter_dimension=0, tiled=True
        ),
    )
    grad_key = rotate_back(
        grad_key.reshape(count_rows, head_count, head_size), cos_table, sin_table
    ).reshape(count_rows, model_width)
    grad_query = rotate_back(grad_query, cos_table, sin_table).reshape(count_rows, model_width)
    grad_packed = jnp.concatenate([grad_query, grad_key, grad_value], axis=1).astype(jnp.bfloat16)
    grad_qkv = lax.dot_general(
        first_low, grad_packed, contract_rows, preferred_element_type=jnp.float32
    )
    grad_first = lax.dot_general(
        grad_packed, w_qkv, contract_cols, preferred_element_type=jnp.float32
    )
    grad_ada_frame = jnp.concatenate([grad_first * norm_first, grad_first], axis=1)
    grad_ada_table = lax.dot_general(member_float, grad_ada_frame, contract_rows, precision=precise)
    grad_ada = lax.dot_general(
        embed_low.astype(jnp.float32), grad_ada_table, contract_rows, precision=precise
    )
    grad_ada_bias = jnp.sum(grad_ada_table, axis=0)
    grad_in = (grad_mid + first_pull(grad_first * (1.0 + scale_part))[0]).astype(jnp.bfloat16)
    grad_skip_weight = lax.dot_general(
        joined, grad_in, contract_rows, preferred_element_type=jnp.float32
    )
    grad_joined = lax.dot_general(
        grad_in, w_skip, contract_cols, preferred_element_type=jnp.float32
    )
    (
        share_skip,
        share_ada,
        share_ada_bias,
        share_qkv,
        share_out,
        share_gain,
        share_up,
        share_up_bias,
        share_down,
        share_down_bias,
    ) = (
        lax.psum_scatter(grad_skip_weight, "seq", scatter_dimension=0, tiled=True),
        lax.psum_scatter(grad_ada, "seq", scatter_dimension=0, tiled=True),
        lax.psum_scatter(grad_ada_bias, "seq", scatter_dimension=0, tiled=True),
        lax.psum_scatter(grad_qkv, "seq", scatter_dimension=0, tiled=True),
        lax.psum_scatter(grad_out_weight, "seq", scatter_dimension=0, tiled=True),
        lax.psum_scatter(grad_gain, "seq", scatter_dimension=0, tiled=True),
        lax.psum_scatter(grad_up, "seq", scatter_dimension=0, tiled=True),
        lax.psum_scatter(grad_up_bias, "seq", scatter_dimension=0, tiled=True),
        lax.psum_scatter(grad_down, "seq", scatter_dimension=0, tiled=True),
        lax.psum_scatter(grad_down_bias, "seq", scatter_dimension=0, tiled=True),
    )
    (
        total_skip,
        total_ada,
        total_ada_bias,
        total_qkv,
        total_out,
        total_gain,
        total_up,
        total_up_bias,
        total_down,
        total_down_bias,
    ) = (
        lax.psum(share_skip.astype(jnp.bfloat16), "dp").astype(jnp.float32),
        lax.psum(share_ada.astype(jnp.bfloat16), "dp").astype(jnp.float32),
        lax.psum(share_ada_bias.astype(jnp.bfloat16), "dp").astype(jnp.float32),
        lax.psum(share_qkv.astype(jnp.bfloat16), "dp").astype(jnp.float32),
        lax.psum(share_out.astype(jnp.bfloat16), "dp").astype(jnp.float32),
        lax.psum(share_gain.astype(jnp.bfloat16), "dp").astype(jnp.float32),
        lax.psum(share_up.astype(jnp.bfloat16), "dp").astype(jnp.float32),
        lax.psum(share_up_bias.astype(jnp.bfloat16), "dp").astype(jnp.float32),
        lax.psum(share_down.astype(jnp.bfloat16), "dp").astype(jnp.float32),
        lax.psum(share_down_bias.astype(jnp.bfloat16), "dp").astype(jnp.float32),
    )
    return (
        output.astype(jnp.bfloat16)[None],
        grad_joined[:, :model_width][None],
        grad_joined[:, model_width:][None],
        total_skip,
        total_ada,
        total_ada_bias,
        total_qkv,
        total_out,
        total_gain,
        total_up,
        total_up_bias,
        total_down,
        total_down_bias,
    )


STEPS = (1, 2, 6)
RELATIVE = (0, 6, 2, 4, 1, 7, 3, 5)


def swap(values, axis_name, mask):
    size = lax.axis_size(axis_name)
    return lax.ppermute(values, axis_name, [(i, i ^ mask) for i in range(size)])


def block_of(values, index, width):
    return lax.dynamic_slice_in_dim(values, index * width, width, axis=1)


def relative_columns(values, seq_index):
    width = values.shape[1] // len(RELATIVE)
    return jnp.concatenate([block_of(values, seq_index ^ mask, width) for mask in RELATIVE], axis=1)


def share_rows(values):
    pair = jnp.concatenate([values, swap(values, "dp", 2)], axis=0)
    return jnp.concatenate([pair, swap(pair, "dp", 1)], axis=0)


def share_quarters(quarter_of, dp_index):
    own = quarter_of(dp_index)
    across = swap(quarter_of(dp_index ^ 2), "dp", 2)
    core = swap(quarter_of(dp_index ^ 1), "dp", 1)
    far = swap(quarter_of(dp_index ^ 3), "dp", 3)
    return jnp.concatenate([own, across, core, far], axis=0)


def column_quarters(values, dp_index):
    width = values.shape[1] // 4
    return share_quarters(lambda index: block_of(values, index, width), dp_index)


def row_product(left, right):
    return lax.dot_general(left, right, contract_rows, preferred_element_type=jnp.float32)


def sum_over_seq(left, right):
    half = left.shape[1] // 2
    send = row_product(left[:, half:], right).astype(jnp.bfloat16)
    arrived = swap(send, "seq", STEPS[0])
    total = row_product(left[:, :half], right) + arrived.astype(jnp.float32)
    for mask in STEPS[1:]:
        half = half // 2
        arrived = swap(total[half:].astype(jnp.bfloat16), "seq", mask)
        total = total[:half] + arrived.astype(jnp.float32)
    return total.astype(jnp.bfloat16)


def gather_quarters(part, dp_index, axis):
    across = swap(part, "dp", 2)
    pair = jnp.stack([part, across])
    other = swap(pair, "dp", 1)
    order = jnp.concatenate([pair, other], axis=0)
    place = jnp.array([0, 2, 1, 3], jnp.int32)
    parts = [
        lax.dynamic_index_in_dim(order, place[dp_index ^ number], 0, keepdims=False)
        for number in range(4)
    ]
    return jnp.concatenate(parts, axis=axis).astype(jnp.float32)


def partner(values):
    half_size = HEAD // 2
    lane = lax.broadcasted_iota(jnp.int32, values.shape, 1) % HEAD
    return jnp.where(
        lane < half_size, jnp.roll(values, -half_size, axis=1), jnp.roll(values, half_size, axis=1)
    )


def partner_rolled(values):
    half_size = HEAD // 2
    lane = lax.broadcasted_iota(jnp.int32, values.shape, 1) % HEAD
    return jnp.where(
        lane < half_size,
        pltpu.roll(values, values.shape[1] - half_size, 1),
        pltpu.roll(values, half_size, 1),
    )


def wide_tables(position, width):
    lane = jnp.arange(width, dtype=jnp.int32) % HEAD
    pair = (lane % (HEAD // 2)).astype(jnp.float32)
    frequency = jnp.exp(pair * (-2.0 * math.log(10000.0) / HEAD))
    angles = position.astype(jnp.float32)[:, None] * frequency[None, :]
    sign = jnp.where(lane < HEAD // 2, -1.0, 1.0)[None, :]
    return jnp.cos(angles), jnp.sin(angles) * sign


def head_mask(values, head):
    lane = lax.broadcasted_iota(jnp.int32, values.shape, 1)
    return jnp.where(lane // HEAD == head, values, jnp.zeros_like(values))


def attend_heads(query_segment, key_segment, key_valid, packed_ref, key_ref, weight_ref, out_ref):
    rows = packed_ref.shape[0]
    width = out_ref.shape[1]
    keys = key_ref[:, width : 2 * width]
    values = key_ref[:, 2 * width :]
    row_index = pl.program_id(0) * rows + lax.broadcasted_iota(
        jnp.int32, (rows, keys.shape[0]), 0
    )
    key_index = lax.broadcasted_iota(jnp.int32, (rows, keys.shape[0]), 1)
    allowed = (query_segment[...] == key_segment[...]) & (
        (key_valid[...] > 0) | (row_index == key_index)
    )
    total = jnp.zeros((rows, width), jnp.float32)
    for head in range(width // HEAD):
        query = head_mask(packed_ref[:, :width], head)
        scores = lax.dot_general(query, keys, contract_cols, preferred_element_type=jnp.float32)
        scores = jnp.where(allowed, scores * (1.0 / math.sqrt(HEAD)), masked_score)
        top = jnp.max(scores, axis=1, keepdims=True)
        weights = jnp.exp(scores - top)
        weights = (weights / jnp.sum(weights, axis=1, keepdims=True)).astype(jnp.bfloat16)
        weight_ref[head] = weights
        total += jnp.dot(weights, head_mask(values, head), preferred_element_type=jnp.float32)
    out_ref[...] = total


def attend_heads_back(
    packed_ref, key_ref, weight_ref, out_ref, grad_ref, cos_ref, sin_ref, all_cos, all_sin,
    query_out, key_out, value_out, key_total, value_total,
):
    width = out_ref.shape[1]
    scale_factor = 1.0 / math.sqrt(HEAD)
    query = packed_ref[:, :width]
    keys = key_ref[:, width : 2 * width]
    values = key_ref[:, 2 * width :]
    grad = grad_ref[...]
    product = grad.astype(jnp.float32) * out_ref[...]

    @pl.when(pl.program_id(0) == 0)
    def _():
        key_total[...] = jnp.zeros_like(key_total)
        value_total[...] = jnp.zeros_like(value_total)

    grad_query = jnp.zeros((query.shape[0], width), jnp.float32)
    for head in range(width // HEAD):
        weights = weight_ref[head]
        grad_head = head_mask(grad, head)
        delta = jnp.sum(head_mask(product, head), axis=1, keepdims=True)
        grad_weights = lax.dot_general(
            grad_head, values, contract_cols, preferred_element_type=jnp.float32
        )
        grad_scores = (weights.astype(jnp.float32) * (grad_weights - delta)).astype(jnp.bfloat16)
        grad_query += jnp.dot(grad_scores, head_mask(keys, head), preferred_element_type=jnp.float32)
        key_total[...] += row_product(grad_scores, head_mask(query, head))
        value_total[...] += row_product(weights, grad_head)
    grad_query = grad_query * scale_factor
    query_out[...] = (
        grad_query * cos_ref[...] - partner_rolled(grad_query) * sin_ref[...]
    ).astype(jnp.bfloat16)

    @pl.when(pl.program_id(0) == pl.num_programs(0) - 1)
    def _():
        grad_key = key_total[...] * scale_factor
        key_out[...] = (
            grad_key * all_cos[...] - partner_rolled(grad_key) * all_sin[...]
        ).astype(jnp.bfloat16)
        value_out[...] = value_total[...].astype(jnp.bfloat16)


def attention(packed, segment, valid):
    count_all = packed.shape[0]
    width = packed.shape[1] // 3
    heads = width // HEAD
    rows = 256
    whole = lambda shape: pl.BlockSpec(shape, lambda i: (0,) * len(shape))
    return pl.pallas_call(
        attend_heads,
        grid=(count_all // rows,),
        in_specs=[
            pl.BlockSpec((rows, 1), lambda i: (i, 0)),
            whole((1, count_all)),
            whole((1, count_all)),
            pl.BlockSpec((rows, 3 * width), lambda i: (i, 0)),
            whole((count_all, 3 * width)),
        ],
        out_specs=(
            pl.BlockSpec((heads, rows, count_all), lambda i: (0, i, 0)),
            pl.BlockSpec((rows, width), lambda i: (i, 0)),
        ),
        out_shape=(
            jax.ShapeDtypeStruct((heads, count_all, count_all), jnp.bfloat16),
            jax.ShapeDtypeStruct((count_all, width), jnp.float32),
        ),
        compiler_params=pltpu.CompilerParams(vmem_limit_bytes=40 * 2**20),
        name="attention",
    )(segment[:, None], segment[None, :], valid[None, :], packed, packed)


def attention_back(packed, weights, attn_sum, grad_attn, cos_table, sin_table):
    count_all = packed.shape[0]
    width = packed.shape[1] // 3
    heads = width // HEAD
    rows = 256
    whole = lambda shape: pl.BlockSpec(shape, lambda i: (0,) * len(shape))
    part = lambda columns: pl.BlockSpec((rows, columns), lambda i: (i, 0))
    return pl.pallas_call(
        attend_heads_back,
        grid=(count_all // rows,),
        in_specs=[
            part(3 * width),
            whole((count_all, 3 * width)),
            pl.BlockSpec((heads, rows, count_all), lambda i: (0, i, 0)),
            part(width),
            part(width),
            part(width),
            part(width),
            whole((count_all, width)),
            whole((count_all, width)),
        ],
        out_specs=(part(width), whole((count_all, width)), whole((count_all, width))),
        out_shape=(jax.ShapeDtypeStruct((count_all, width), jnp.bfloat16),) * 3,
        scratch_shapes=[pltpu.VMEM((count_all, width), jnp.float32)] * 2,
        compiler_params=pltpu.CompilerParams(vmem_limit_bytes=40 * 2**20),
        name="attention_back",
    )(packed, packed, weights, attn_sum, grad_attn, cos_table, sin_table, cos_table, sin_table)


def norm_parts(values):
    centered = values - jnp.mean(values, axis=-1, keepdims=True)
    variance = jnp.mean(centered * centered, axis=-1, keepdims=True)
    factor = lax.rsqrt(variance + 1e-06)
    return centered * factor, factor


def norm_back(grad, normal, factor):
    mean_grad = jnp.mean(grad, axis=-1, keepdims=True)
    mean_product = jnp.mean(grad * normal, axis=-1, keepdims=True)
    return factor * (grad - mean_grad - normal * mean_product)


def by_heads(
    frames,
    skip,
    lengths,
    frame_mask,
    time_step,
    w_skip,
    w_ada,
    b_ada,
    w_qkv,
    w_out,
    norm_gain,
    w_up,
    b_up,
    w_down,
    b_down,
    cotangent,
):
    row_lengths = lengths[0]
    count_rows, width = frames.shape[1:]
    seq_size = lax.axis_size("seq")
    seq_index = lax.axis_index("seq")
    dp_index = lax.axis_index("dp")
    count_all = count_rows * seq_size
    head_width = width // seq_size
    joined = jnp.concatenate([frames[0], skip[0]], axis=1)
    grad_out = cotangent[0]
    joined_all = share_rows(relative_columns(joined, seq_index))
    grad_out_all = share_rows(grad_out)
    steps_all = share_rows(time_step)
    grad_gated = lax.dot_general(
        grad_out, w_down, contract_cols, preferred_element_type=jnp.float32
    )

    all_index = jnp.arange(count_all, dtype=jnp.int32)
    all_segment, all_position, unused = utterance_layout(row_lengths, all_index)
    segment = lax.dynamic_slice_in_dim(all_segment, seq_index * count_rows, count_rows)
    position = lax.dynamic_slice_in_dim(all_position, seq_index * count_rows, count_rows)
    member = segment[:, None] == jnp.arange(lengths.shape[1], dtype=jnp.int32)[None, :]
    member_float = member.astype(jnp.float32)
    embed_low = time_embedding(time_step[0], width).astype(jnp.bfloat16)
    ada_table = jnp.dot(embed_low, w_ada, preferred_element_type=jnp.float32) + b_ada.astype(
        jnp.float32
    )
    ada_frame = jnp.dot(member_float, ada_table, precision=precise)
    scale_part = ada_frame[:, :width]
    shift_part = ada_frame[:, width:]
    residual_in = jnp.dot(joined, w_skip, preferred_element_type=jnp.float32)
    norm_first, factor_first = norm_parts(residual_in)
    first_low = (norm_first * (1.0 + scale_part) + shift_part).astype(jnp.bfloat16)
    packed = jnp.dot(first_low, w_qkv, preferred_element_type=jnp.float32)
    cos_own, sin_own = wide_tables(position, 2 * width)
    turned = packed[:, : 2 * width]
    turned = (turned * cos_own + partner(turned) * sin_own).astype(jnp.bfloat16)
    values_low = packed[:, 2 * width :].astype(jnp.bfloat16)
    split = jnp.concatenate([turned, values_low], axis=1).reshape(
        count_rows, 3, seq_size, head_width
    )
    split = jnp.transpose(split, (2, 0, 1, 3)).reshape(seq_size, count_rows, 3 * head_width)
    mask_rows = jnp.zeros((seq_size, 16, 3 * head_width), jnp.bfloat16)
    mask_rows = mask_rows.at[:, 0, :count_rows].set(frame_mask.astype(jnp.bfloat16))
    received = lax.all_to_all(jnp.concatenate([split, mask_rows], axis=1), "seq", 0, 0)
    row_packed = received[:, :count_rows].reshape(count_all, 3 * head_width)
    row_valid = received[:, count_rows, :count_rows].reshape(count_all).astype(jnp.int32)
    first_all = share_rows(relative_columns(first_low, seq_index))

    weights, attn_heads = attention(row_packed, all_segment, row_valid)
    attn_back = lax.all_to_all(
        attn_heads.astype(jnp.bfloat16).reshape(seq_size, count_rows, head_width), "seq", 0, 0
    )
    attn_low = jnp.transpose(attn_back, (1, 0, 2)).reshape(count_rows, width)
    residual_mid = residual_in + jnp.dot(attn_low, w_out, preferred_element_type=jnp.float32)
    gain_float = norm_gain.astype(jnp.float32)
    norm_second, factor_second = norm_parts(residual_mid)
    second_low = (norm_second * gain_float).astype(jnp.bfloat16)
    attn_low_all = share_rows(relative_columns(attn_low, seq_index))
    second_all = share_rows(relative_columns(second_low, seq_index))
    upper_sum = jnp.dot(second_low, w_up, preferred_element_type=jnp.float32) + b_up.astype(
        jnp.float32
    )
    root = math.sqrt(2.0 / math.pi)
    bent = jnp.tanh(root * (upper_sum + 0.044715 * upper_sum * upper_sum * upper_sum))
    gated_low = (0.5 * upper_sum * (1.0 + bent)).astype(jnp.bfloat16)
    slope = 0.5 * (1.0 + bent) + 0.5 * upper_sum * (1.0 - bent * bent) * root * (
        1.0 + 3.0 * 0.044715 * upper_sum * upper_sum
    )
    grad_upper = (grad_gated * slope).astype(jnp.bfloat16)

    hidden = gated_low.shape[1]
    own_hidden = hidden // seq_size
    part_hidden = own_hidden // 4

    def gated_quarter(index):
        return jnp.concatenate(
            [
                lax.dynamic_slice_in_dim(
                    gated_low,
                    (seq_index ^ mask) * own_hidden + index * part_hidden,
                    part_hidden,
                    axis=1,
                )
                for mask in RELATIVE
            ],
            axis=1,
        )

    gated_all = share_quarters(gated_quarter, dp_index)
    part_down = sum_over_seq(gated_all, grad_out_all)
    upper_all = column_quarters(grad_upper, dp_index)
    part_up = sum_over_seq(second_all, upper_all)
    output = (
        residual_mid
        + jnp.dot(gated_low, w_down, preferred_element_type=jnp.float32)
        + b_down.astype(jnp.float32)
    )
    grad_out_float = grad_out.astype(jnp.float32)
    grad_second = lax.dot_general(
        grad_upper, w_up, contract_cols, preferred_element_type=jnp.float32
    )
    sum_gain = jnp.sum(grad_second * norm_second, axis=0)
    grad_mid = grad_out_float + norm_back(grad_second * gain_float, norm_second, factor_second)
    grad_branch = grad_mid.astype(jnp.bfloat16)
    branch_all = column_quarters(grad_branch, dp_index)
    part_out = sum_over_seq(attn_low_all, branch_all)
    grad_attn = lax.dot_general(
        grad_branch, w_out, contract_cols, preferred_element_type=jnp.float32
    ).astype(jnp.bfloat16)
    grad_attn = jnp.transpose(grad_attn.reshape(count_rows, seq_size, head_width), (1, 0, 2))
    grad_heads = lax.all_to_all(grad_attn, "seq", 0, 0).reshape(count_all, head_width)
    cos_all, sin_all = wide_tables(all_position, head_width)
    grad_parts = attention_back(row_packed, weights, attn_heads, grad_heads, cos_all, sin_all)
    grad_split = jnp.concatenate(
        [part.reshape(seq_size, count_rows, head_width) for part in grad_parts], axis=2
    )
    grad_back = lax.all_to_all(grad_split, "seq", 0, 0)
    grad_packed = jnp.transpose(
        grad_back.reshape(seq_size, count_rows, 3, head_width), (1, 2, 0, 3)
    ).reshape(count_rows, 3 * width)
    grad_first = lax.dot_general(
        grad_packed, w_qkv, contract_cols, preferred_element_type=jnp.float32
    )
    packed_all = column_quarters(grad_packed, dp_index)
    grad_in = (
        grad_mid + norm_back(grad_first * (1.0 + scale_part), norm_first, factor_first)
    ).astype(jnp.bfloat16)
    in_all = column_quarters(grad_in, dp_index)
    part_qkv = sum_over_seq(first_all, packed_all)
    part_skip = sum_over_seq(joined_all, in_all)
    grad_joined = lax.dot_general(
        grad_in, w_skip, contract_cols, preferred_element_type=jnp.float32
    )

    place = jnp.array([0, 2, 1, 3], jnp.int32)
    grad_ada_frame = jnp.concatenate([grad_first * norm_first, grad_first], axis=1)
    ada_sums = lax.dot_general(member_float, grad_ada_frame, contract_rows, precision=precise)
    vector_sums = jnp.concatenate(
        [
            jnp.sum(grad_upper.astype(jnp.float32), axis=0),
            sum_gain,
            jnp.sum(grad_out_float, axis=0),
        ]
    ).reshape(-1, ada_sums.shape[1])
    small = jnp.concatenate([ada_sums, vector_sums], axis=0)
    for mask in STEPS:
        small = small + swap(small, "seq", mask)
    small_all = jnp.stack([small, swap(small, "dp", 2)])
    small_all = jnp.concatenate([small_all, swap(small_all, "dp", 1)], axis=0)
    small_all = jnp.stack(
        [lax.dynamic_index_in_dim(small_all, place[dp_index ^ q], 0, False) for q in range(4)]
    )
    steps_all = jnp.stack(
        [lax.dynamic_index_in_dim(steps_all, place[dp_index ^ q], 0, False) for q in range(4)]
    )
    count_utter = lengths.shape[1]
    ada_all = small_all[:, :count_utter].reshape(-1, small.shape[1])
    vectors = jnp.sum(small_all[:, count_utter:], axis=0).reshape(-1)
    embed_all = time_embedding(steps_all.reshape(-1), width).astype(jnp.bfloat16)
    own_embed = block_of(embed_all, seq_index, width // seq_size).astype(jnp.float32)
    total_ada = lax.dot_general(own_embed, ada_all, contract_rows, precision=precise)
    total_ada_bias = lax.dynamic_slice_in_dim(
        jnp.sum(ada_all, axis=0), seq_index * (2 * width // seq_size), 2 * width // seq_size
    )
    total_up_bias = lax.dynamic_slice_in_dim(vectors, seq_index * own_hidden, own_hidden)
    total_gain = lax.dynamic_slice_in_dim(
        vectors[hidden:], seq_index * head_width, head_width
    )
    total_down_bias = lax.dynamic_slice_in_dim(
        vectors[hidden + width :], seq_index * head_width, head_width
    )
    return (
        output.astype(jnp.bfloat16)[None],
        grad_joined[:, :width][None],
        grad_joined[:, width:][None],
        gather_quarters(part_skip, dp_index, 1),
        total_ada,
        total_ada_bias,
        gather_quarters(part_qkv, dp_index, 1),
        gather_quarters(part_out, dp_index, 1),
        total_gain,
        gather_quarters(part_up, dp_index, 1),
        total_up_bias,
        gather_quarters(part_down, dp_index, 0),
        total_down_bias,
    )


def solution(mesh):
    placed = (
        P("dp", "seq", None),
        P("dp", "seq", None),
        P("dp", None),
        P("dp", "seq"),
        P("dp", None),
        P(),
        P(),
        P(),
        P(),
        P(),
        P(),
        P(),
        P(),
        P(),
        P(),
        P("dp", "seq", None),
    )
    split_heads = mesh.shape["dp"] == 4 and mesh.shape["seq"] == len(RELATIVE)
    return jax.shard_map(
        by_heads if split_heads else on_device,
        mesh=mesh,
        in_specs=placed,
        out_specs=(
            P("dp", "seq", None),
            P("dp", "seq", None),
            P("dp", "seq", None),
            P("seq", None),
            P("seq", None),
            P("seq"),
            P("seq", None),
            P("seq", None),
            P("seq"),
            P("seq", None),
            P("seq"),
            P("seq", None),
            P("seq"),
        ),
        check_vma=False,
    )
```

```python
import math

import jax
import jax.numpy as jnp
from jax import lax
from jax.experimental import pallas as pl
from jax.experimental.pallas import tpu as pltpu
from jax.sharding import PartitionSpec as P

HEADS = 16
HEAD = 64
TSTEPS = 32


precise = lax.Precision.HIGHEST
masked_score = -1e30
contract_rows = (((0,), (0,)), ((), ()))
contract_cols = (((1,), (1,)), ((), ()))


def divisor_below(count_all, upper_limit):
    size_now = min(count_all, upper_limit)
    while count_all % size_now:
        size_now -= 1
    return size_now


def normalize(values):
    centered = values - jnp.mean(values, axis=-1, keepdims=True)
    variance = jnp.mean(centered * centered, axis=-1, keepdims=True)
    return centered * lax.rsqrt(variance + 1e-06)


def segment_of(lengths, frame_index):
    utter_ends = jnp.cumsum(lengths)
    return jnp.sum((frame_index[:, None] >= utter_ends[None, :]).astype(jnp.int32), axis=1)


def utterance_layout(lengths, frame_index):
    utter_ends = jnp.cumsum(lengths)
    starts = utter_ends - lengths
    segment = segment_of(lengths, frame_index)
    member = segment[:, None] == jnp.arange(lengths.shape[0], dtype=jnp.int32)[None, :]
    position = frame_index - jnp.sum(jnp.where(member, starts[None, :], 0), axis=1)
    return (segment, position, member)


def rotary_tables(position, head_size):
    half_size = head_size // 2
    frequency = jnp.exp(
        jnp.arange(half_size, dtype=jnp.float32) * (-2.0 * math.log(10000.0) / head_size)
    )
    angles = position.astype(jnp.float32)[:, None] * frequency[None, :]
    return (jnp.cos(angles)[:, None, :], jnp.sin(angles)[:, None, :])


def rotate(values, cos_table, sin_table):
    half_size = values.shape[-1] // 2
    first_half = values[..., :half_size]
    second_half = values[..., half_size:]
    return jnp.concatenate(
        [
            first_half * cos_table - second_half * sin_table,
            second_half * cos_table + first_half * sin_table,
        ],
        axis=-1,
    )


def rotate_back(values, cos_table, sin_table):
    half_size = values.shape[-1] // 2
    first_half = values[..., :half_size]
    second_half = values[..., half_size:]
    return jnp.concatenate(
        [
            first_half * cos_table + second_half * sin_table,
            second_half * cos_table - first_half * sin_table,
        ],
        axis=-1,
    )


def time_embedding(steps, model_width):
    half_size = model_width // 2
    flow_time = steps.astype(jnp.float32) / TSTEPS
    frequency = jnp.exp(jnp.arange(half_size, dtype=jnp.float32) * (-math.log(10000.0) / half_size))
    angles = 1000.0 * flow_time[:, None] * frequency[None, :]
    return jnp.concatenate([jnp.sin(angles), jnp.cos(angles)], axis=1)


def make_attend(query_low, query_segment, query_index, lengths):
    count_rows, head_count, head_size = query_low.shape
    scale_factor = 1.0 / math.sqrt(head_size)

    def attend(running, key_piece, first_row):
        keys_part, values_part, valid_part = key_piece
        count_keys = keys_part.shape[0]
        block_rows = divisor_below(count_keys, 1024)
        block_count = count_keys // block_rows
        key_blocks = keys_part.reshape(block_count, block_rows, head_count, head_size)
        value_blocks = values_part.reshape(block_count, block_rows, head_count, head_size)
        valid_blocks = valid_part.reshape(block_count, block_rows)
        offsets = first_row + jnp.arange(block_count, dtype=jnp.int32) * block_rows

        def attend_block_step(carried, inputs):
            row_top, row_total, weighted = carried
            key_block, value_block, valid_block, offset = inputs
            key_index = offset + jnp.arange(block_rows, dtype=jnp.int32)
            key_segment = segment_of(lengths, key_index)
            allowed = (query_segment[:, None] == key_segment[None, :]) & (
                (valid_block[None, :] > 0) | (query_index[:, None] == key_index[None, :])
            )
            scores = (
                jnp.einsum("qhd,khd->hqk", query_low, key_block, preferred_element_type=jnp.float32)
                * scale_factor
            )
            scores = jnp.where(allowed[None], scores, masked_score)
            new_top = jnp.maximum(row_top, jnp.max(scores, axis=2))
            weights = jnp.where(allowed[None], jnp.exp(scores - new_top[:, :, None]), 0.0)
            factor = jnp.exp(row_top - new_top)
            row_total = row_total * factor + jnp.sum(weights, axis=2)
            weighted = weighted * jnp.transpose(factor)[:, :, None] + jnp.einsum(
                "hqk,khd->qhd",
                weights.astype(jnp.bfloat16),
                value_block,
                preferred_element_type=jnp.float32,
            )
            return ((new_top, row_total, weighted), None)

        result_state, unused = lax.scan(
            attend_block_step, running, (key_blocks, value_blocks, valid_blocks, offsets)
        )
        return result_state

    return attend


def key_sweep(
    query_low, grad_attn, log_total, row_delta, query_segment, query_index, lengths, key_tuple
):
    keys_all, values_all, valid_all = key_tuple
    count_rows, head_count, head_size = query_low.shape
    scale_factor = 1.0 / math.sqrt(head_size)
    count_keys = keys_all.shape[0]
    block_rows = divisor_below(count_keys, 1024)
    block_count = count_keys // block_rows
    key_blocks = keys_all.reshape(block_count, block_rows, head_count, head_size)
    value_blocks = values_all.reshape(block_count, block_rows, head_count, head_size)
    valid_blocks = valid_all.reshape(block_count, block_rows)
    offsets = jnp.arange(block_count, dtype=jnp.int32) * block_rows
    top_shift = jnp.transpose(log_total)[:, :, None]
    delta_shift = jnp.transpose(row_delta)[:, :, None]

    def key_block_step(grad_query, inputs):
        key_block, value_block, valid_block, offset = inputs
        key_index = offset + jnp.arange(block_rows, dtype=jnp.int32)
        key_segment = segment_of(lengths, key_index)
        allowed = (query_segment[:, None] == key_segment[None, :]) & (
            (valid_block[None, :] > 0) | (query_index[:, None] == key_index[None, :])
        )
        scores = (
            jnp.einsum("qhd,khd->hqk", query_low, key_block, preferred_element_type=jnp.float32)
            * scale_factor
        )
        weights = jnp.where(allowed[None], jnp.exp(scores - top_shift), 0.0)
        grad_weights = jnp.einsum(
            "qhd,khd->hqk", grad_attn, value_block, preferred_element_type=jnp.float32
        )
        grad_scores = (weights * (grad_weights - delta_shift)).astype(jnp.bfloat16)
        grad_query = (
            grad_query
            + jnp.einsum("hqk,khd->qhd", grad_scores, key_block, preferred_element_type=jnp.float32)
            * scale_factor
        )
        grad_key = (
            jnp.einsum("hqk,qhd->khd", grad_scores, query_low, preferred_element_type=jnp.float32)
            * scale_factor
        )
        grad_value = jnp.einsum(
            "hqk,qhd->khd",
            weights.astype(jnp.bfloat16),
            grad_attn,
            preferred_element_type=jnp.float32,
        )
        return (grad_query, (grad_key, grad_value))

    start_grad = jnp.zeros((count_rows, head_count, head_size), jnp.float32)
    return lax.scan(key_block_step, start_grad, (key_blocks, value_blocks, valid_blocks, offsets))


def on_device(
    frames,
    skip,
    lengths,
    frame_mask,
    time_step,
    w_skip,
    w_ada,
    b_ada,
    w_qkv,
    w_out,
    norm_gain,
    w_up,
    b_up,
    w_down,
    b_down,
    cotangent,
):
    local_frames = frames[0]
    local_skip = skip[0]
    row_lengths = lengths[0]
    count_rows, model_width = local_frames.shape
    head_count = HEADS
    head_size = HEAD
    row_base = lax.axis_index("seq") * count_rows
    frame_index = row_base + jnp.arange(count_rows, dtype=jnp.int32)
    segment, position, member = utterance_layout(row_lengths, frame_index)
    member_float = member.astype(jnp.float32)
    embed_low = time_embedding(time_step[0], model_width).astype(jnp.bfloat16)
    ada_table = jnp.dot(embed_low, w_ada, preferred_element_type=jnp.float32) + b_ada.astype(
        jnp.float32
    )
    ada_frame = jnp.dot(member_float, ada_table, precision=precise)
    scale_part = ada_frame[:, :model_width]
    shift_part = ada_frame[:, model_width:]
    joined = jnp.concatenate([local_frames, local_skip], axis=1)
    residual_in = jnp.dot(joined, w_skip, preferred_element_type=jnp.float32)
    norm_first, first_pull = jax.vjp(normalize, residual_in)
    first_low = (norm_first * (1.0 + scale_part) + shift_part).astype(jnp.bfloat16)
    packed = jnp.dot(first_low, w_qkv, preferred_element_type=jnp.float32)
    cos_table, sin_table = rotary_tables(position, head_size)
    query_low = rotate(
        packed[:, :model_width].reshape(count_rows, head_count, head_size), cos_table, sin_table
    ).astype(jnp.bfloat16)
    keys_low = (
        rotate(
            packed[:, model_width : 2 * model_width].reshape(count_rows, head_count, head_size),
            cos_table,
            sin_table,
        )
        .astype(jnp.bfloat16)
        .reshape(count_rows, model_width)
    )
    values_low = packed[:, 2 * model_width :].astype(jnp.bfloat16)
    valid_low = frame_mask[0].astype(jnp.bfloat16)
    attend = make_attend(query_low, segment, frame_index, row_lengths)
    start_state = (
        jnp.full((head_count, count_rows), masked_score, jnp.float32),
        jnp.zeros((head_count, count_rows), jnp.float32),
        jnp.zeros((count_rows, head_count, head_size), jnp.float32),
    )
    gathered = (
        lax.all_gather(keys_low, "seq", axis=0, tiled=True),
        lax.all_gather(values_low, "seq", axis=0, tiled=True),
        lax.all_gather(valid_low, "seq", axis=0, tiled=True),
    )
    row_top, row_total, weighted = attend(start_state, gathered, 0)
    attn_sum = weighted / jnp.transpose(row_total)[:, :, None]
    log_total = jnp.transpose(row_top + jnp.log(row_total))
    attn_low = attn_sum.reshape(count_rows, model_width).astype(jnp.bfloat16)
    residual_mid = residual_in + jnp.dot(attn_low, w_out, preferred_element_type=jnp.float32)
    gain_float = norm_gain.astype(jnp.float32)
    second_float, second_pull = jax.vjp(
        lambda hidden, gain_vector: normalize(hidden) * gain_vector, residual_mid, gain_float
    )
    second_low = second_float.astype(jnp.bfloat16)
    upper_sum = jnp.dot(second_low, w_up, preferred_element_type=jnp.float32) + b_up.astype(
        jnp.float32
    )
    gated_float, gelu_pull = jax.vjp(
        lambda hidden: jax.nn.gelu(hidden, approximate=True), upper_sum
    )
    gated_low = gated_float.astype(jnp.bfloat16)
    output = (
        residual_mid
        + jnp.dot(gated_low, w_down, preferred_element_type=jnp.float32)
        + b_down.astype(jnp.float32)
    )
    grad_out = cotangent[0]
    grad_out_float = grad_out.astype(jnp.float32)
    grad_down = lax.dot_general(
        gated_low, grad_out, contract_rows, preferred_element_type=jnp.float32
    )
    grad_down_bias = jnp.sum(grad_out_float, axis=0)
    grad_gated = lax.dot_general(
        grad_out, w_down, contract_cols, preferred_element_type=jnp.float32
    )
    grad_upper = gelu_pull(grad_gated)[0].astype(jnp.bfloat16)
    grad_up = lax.dot_general(
        second_low, grad_upper, contract_rows, preferred_element_type=jnp.float32
    )
    grad_up_bias = jnp.sum(grad_upper.astype(jnp.float32), axis=0)
    grad_second = lax.dot_general(
        grad_upper, w_up, contract_cols, preferred_element_type=jnp.float32
    )
    grad_mid_norm, grad_gain = second_pull(grad_second)
    grad_mid = grad_out_float + grad_mid_norm
    grad_branch = grad_mid.astype(jnp.bfloat16)
    grad_out_weight = lax.dot_general(
        attn_low, grad_branch, contract_rows, preferred_element_type=jnp.float32
    )
    grad_attn = (
        lax.dot_general(grad_branch, w_out, contract_cols, preferred_element_type=jnp.float32)
        .astype(jnp.bfloat16)
        .reshape(count_rows, head_count, head_size)
    )
    row_delta = jnp.sum(grad_attn.astype(jnp.float32) * attn_sum, axis=2)
    grad_query, key_parts = key_sweep(
        query_low, grad_attn, log_total, row_delta, segment, frame_index, row_lengths, gathered
    )
    grad_key_all, grad_value_all = key_parts
    total_keys = grad_key_all.shape[0] * grad_key_all.shape[1]
    grad_key, grad_value = (
        lax.psum_scatter(
            grad_key_all.reshape(total_keys, model_width), "seq", scatter_dimension=0, tiled=True
        ),
        lax.psum_scatter(
            grad_value_all.reshape(total_keys, model_width), "seq", scatter_dimension=0, tiled=True
        ),
    )
    grad_key = rotate_back(
        grad_key.reshape(count_rows, head_count, head_size), cos_table, sin_table
    ).reshape(count_rows, model_width)
    grad_query = rotate_back(grad_query, cos_table, sin_table).reshape(count_rows, model_width)
    grad_packed = jnp.concatenate([grad_query, grad_key, grad_value], axis=1).astype(jnp.bfloat16)
    grad_qkv = lax.dot_general(
        first_low, grad_packed, contract_rows, preferred_element_type=jnp.float32
    )
    grad_first = lax.dot_general(
        grad_packed, w_qkv, contract_cols, preferred_element_type=jnp.float32
    )
    grad_ada_frame = jnp.concatenate([grad_first * norm_first, grad_first], axis=1)
    grad_ada_table = lax.dot_general(member_float, grad_ada_frame, contract_rows, precision=precise)
    grad_ada = lax.dot_general(
        embed_low.astype(jnp.float32), grad_ada_table, contract_rows, precision=precise
    )
    grad_ada_bias = jnp.sum(grad_ada_table, axis=0)
    grad_in = (grad_mid + first_pull(grad_first * (1.0 + scale_part))[0]).astype(jnp.bfloat16)
    grad_skip_weight = lax.dot_general(
        joined, grad_in, contract_rows, preferred_element_type=jnp.float32
    )
    grad_joined = lax.dot_general(
        grad_in, w_skip, contract_cols, preferred_element_type=jnp.float32
    )
    (
        share_skip,
        share_ada,
        share_ada_bias,
        share_qkv,
        share_out,
        share_gain,
        share_up,
        share_up_bias,
        share_down,
        share_down_bias,
    ) = (
        lax.psum_scatter(grad_skip_weight, "seq", scatter_dimension=0, tiled=True),
        lax.psum_scatter(grad_ada, "seq", scatter_dimension=0, tiled=True),
        lax.psum_scatter(grad_ada_bias, "seq", scatter_dimension=0, tiled=True),
        lax.psum_scatter(grad_qkv, "seq", scatter_dimension=0, tiled=True),
        lax.psum_scatter(grad_out_weight, "seq", scatter_dimension=0, tiled=True),
        lax.psum_scatter(grad_gain, "seq", scatter_dimension=0, tiled=True),
        lax.psum_scatter(grad_up, "seq", scatter_dimension=0, tiled=True),
        lax.psum_scatter(grad_up_bias, "seq", scatter_dimension=0, tiled=True),
        lax.psum_scatter(grad_down, "seq", scatter_dimension=0, tiled=True),
        lax.psum_scatter(grad_down_bias, "seq", scatter_dimension=0, tiled=True),
    )
    (
        total_skip,
        total_ada,
        total_ada_bias,
        total_qkv,
        total_out,
        total_gain,
        total_up,
        total_up_bias,
        total_down,
        total_down_bias,
    ) = (
        lax.psum(share_skip.astype(jnp.bfloat16), "dp").astype(jnp.float32),
        lax.psum(share_ada.astype(jnp.bfloat16), "dp").astype(jnp.float32),
        lax.psum(share_ada_bias.astype(jnp.bfloat16), "dp").astype(jnp.float32),
        lax.psum(share_qkv.astype(jnp.bfloat16), "dp").astype(jnp.float32),
        lax.psum(share_out.astype(jnp.bfloat16), "dp").astype(jnp.float32),
        lax.psum(share_gain.astype(jnp.bfloat16), "dp").astype(jnp.float32),
        lax.psum(share_up.astype(jnp.bfloat16), "dp").astype(jnp.float32),
        lax.psum(share_up_bias.astype(jnp.bfloat16), "dp").astype(jnp.float32),
        lax.psum(share_down.astype(jnp.bfloat16), "dp").astype(jnp.float32),
        lax.psum(share_down_bias.astype(jnp.bfloat16), "dp").astype(jnp.float32),
    )
    return (
        output.astype(jnp.bfloat16)[None],
        grad_joined[:, :model_width][None],
        grad_joined[:, model_width:][None],
        total_skip,
        total_ada,
        total_ada_bias,
        total_qkv,
        total_out,
        total_gain,
        total_up,
        total_up_bias,
        total_down,
        total_down_bias,
    )


RELATIVE = (0, 6, 2, 4, 1, 7, 3, 5)
STEPS = (1, 2, 6)
MESH = pl.DeviceIdType.MESH
MIB = 2**20
FAR_FIRST = (4, 5, 2, 3, 6, 7, 1)
ROOT = math.sqrt(2.0 / math.pi)


def bit(value, place):
    return lax.rem(lax.div(value, jnp.int32(1 << place)), jnp.int32(2))


def flip(value, mask):
    out = value
    for place in range(3):
        if (mask >> place) & 1:
            out = out + (1 << place) * (1 - 2 * bit(value, place))
    return out


def exclusive(value, other):
    return sum(
        (1 << place) * lax.rem(bit(value, place) + bit(other, place), jnp.int32(2))
        for place in range(3)
    )


def relative_block(seq_index, number):
    step_y, step_a, step_b = bit(number, 2), bit(number, 1), bit(number, 0)
    two = jnp.int32(2)
    return (
        lax.rem(bit(seq_index, 0) + step_y, two)
        + 2 * lax.rem(bit(seq_index, 1) + step_a + step_b, two)
        + 4 * lax.rem(bit(seq_index, 2) + step_b, two)
    )


def columns(start, size):
    return pl.ds(pl.multiple_of(start, 128), size)


class Links:
    def __init__(self, send_sems, recv_sems, load_sems):
        self.send_sems, self.recv_sems, self.load_sems = send_sems, recv_sems, load_sems
        self.used, self.loads, self.sent = 0, 0, []
        self.dp_index, self.seq_index = lax.axis_index("dp"), lax.axis_index("seq")

    def peer(self, axis, mask):
        if axis == "dp":
            return (flip(self.dp_index, mask), self.seq_index)
        return (self.dp_index, flip(self.seq_index, mask))

    def barrier(self):
        semaphore = pltpu.get_barrier_semaphore()
        for axis, count in (("seq", 8), ("dp", 4)):
            for mask in range(1, count):
                pl.semaphore_signal(
                    semaphore, inc=1, device_id=self.peer(axis, mask), device_id_type=MESH
                )
        pl.semaphore_wait(semaphore, 10)

    def send(self, source, target, axis, mask):
        number = self.used
        self.used += 1
        copy = pltpu.make_async_remote_copy(
            src_ref=source,
            dst_ref=target,
            send_sem=self.send_sems.at[number],
            recv_sem=self.recv_sems.at[number],
            device_id=self.peer(axis, mask),
            device_id_type=MESH,
        )
        copy.start()
        self.sent.append(copy)
        return copy

    def load(self, source, target):
        copy = pltpu.make_async_copy(source, target, self.load_sems.at[self.loads])
        self.loads += 1
        copy.start()
        return copy

    def settle(self, copy):
        copy.wait()
        self.sent = [other for other in self.sent if other is not copy]

    def drain(self):
        for copy in self.sent:
            copy.wait_send()


def share_start(links, slots):
    return links.send(slots.at[0], slots.at[2], "dp", 2), links.send(
        slots.at[0], slots.at[1], "dp", 1
    )


def share_forward(links, slots, copies):
    copies[0].wait_recv()
    last = links.send(slots.at[2], slots.at[3], "dp", 1)
    return copies[1], last


def arrived(copies):
    for copy in copies:
        copy.wait_recv()


def turn_sine_cosine(angles):
    turns = jnp.floor(angles * (0.5 / math.pi) + 0.5)
    rest = angles - turns * 6.28125
    rest = rest - turns * (2.0 * math.pi - 6.28125)
    return jnp.sin(rest), jnp.cos(rest)


def utterance_ends(lengths_ref):
    ends, total = [], jnp.int32(0)
    for number in range(lengths_ref.shape[1]):
        total = total + lengths_ref[0, number]
        ends.append(total)
    return ends


def segments(ends, index):
    return sum((index >= end).astype(jnp.int32) for end in ends)


def rotary(ends, first_row, rows, width):
    index = first_row + lax.broadcasted_iota(jnp.int32, (rows, width), 0)
    start = jnp.zeros_like(index)
    for end in ends:
        start = jnp.where(index >= end, end, start)
    lane = lax.broadcasted_iota(jnp.int32, (rows, width), 1) % HEAD
    pair = (lane % (HEAD // 2)).astype(jnp.float32)
    angles = (index - start).astype(jnp.float32) * jnp.exp(
        pair * (-2.0 * math.log(10000.0) / HEAD)
    )
    sine, cosine = turn_sine_cosine(angles)
    return cosine, jnp.where(lane < HEAD // 2, -sine, sine)


def partner(values):
    half_size = HEAD // 2
    lane = lax.broadcasted_iota(jnp.int32, values.shape, 1) % HEAD
    return jnp.where(
        lane < half_size,
        pltpu.roll(values, values.shape[1] - half_size, 1),
        pltpu.roll(values, half_size, 1),
    )


def head_mask(values, head):
    lane = lax.broadcasted_iota(jnp.int32, values.shape, 1)
    return jnp.where(lane // HEAD == head, values, jnp.zeros_like(values))


def norm_parts(values):
    centered = values - jnp.mean(values, axis=-1, keepdims=True)
    variance = jnp.mean(centered * centered, axis=-1, keepdims=True)
    factor = lax.rsqrt(variance + 1e-06)
    return centered * factor, factor


def norm_back(grad, normal, factor):
    mean_grad = jnp.mean(grad, axis=-1, keepdims=True)
    mean_product = jnp.mean(grad * normal, axis=-1, keepdims=True)
    return factor * (grad - mean_grad - normal * mean_product)


def product(left, right):
    return jnp.dot(left, right, preferred_element_type=jnp.float32)


def product_cols(left, right):
    return lax.dot_general(left, right, contract_cols, preferred_element_type=jnp.float32)


def product_rows(left, right):
    return lax.dot_general(left, right, contract_rows, preferred_element_type=jnp.float32)


def first_kernel(
    lengths, steps, frame_mask, frames, skip, cotangent, b_ada, w_skip, w_ada, w_qkv, w_down,
    joined_all, cot_all, first_all, embed_all, residual, scale, grad_gated, packed, weights,
    attn_sum, attn_low,
    skip_buf, ada_buf, qkv_buf, down_buf, joined_own, first_own, table, packed_send, attn_send,
    masks, weight_buf, send_sems, recv_sems, load_sems,
):
    links = Links(send_sems, recv_sems, load_sems)
    seq_index, dp_index = links.seq_index, links.dp_index
    rows, width = frames.shape
    load_skip = links.load(w_skip, skip_buf)
    load_ada = links.load(w_ada, ada_buf)
    load_qkv = links.load(w_qkv, qkv_buf)
    load_down = links.load(w_down, down_buf)

    block = 2 * width // 8
    for number in range(8):
        place = relative_block(seq_index, jnp.int32(number))
        inside = columns(lax.rem(place, jnp.int32(4)) * block, block)
        chosen = jnp.where(place < 4, frames[:, inside], skip[:, inside])
        joined_own[:, number * block : (number + 1) * block] = chosen
    masks[0] = jnp.broadcast_to(frame_mask[...], masks.shape[1:])

    ends = utterance_ends(lengths)
    utter = lax.broadcasted_iota(jnp.int32, (16, width), 0)
    flow = jnp.zeros((16, width), jnp.float32)
    for number in range(steps.shape[1]):
        flow = jnp.where(utter == number, steps[0, number].astype(jnp.float32), flow)
    lane = lax.broadcasted_iota(jnp.int32, (16, width), 1)
    half = width // 2
    frequency = jnp.exp(
        (lane % half).astype(jnp.float32) * (-math.log(10000.0) / half)
    )
    sine, cosine = turn_sine_cosine(1000.0 * (flow / TSTEPS) * frequency)
    embed = jnp.where(lane < half, sine, cosine).astype(jnp.bfloat16)
    table_embed = embed

    links.barrier()
    own_copies = [
        links.load(joined_own, joined_all.at[0]),
        links.load(cotangent, cot_all.at[0]),
    ]
    mask_copies = [links.send(masks.at[0], masks.at[m], "seq", m) for m in range(1, 8)]
    cot_copies = [
        links.send(cotangent, cot_all.at[m], "dp", m) for m in (1, 2)
    ]
    joined_copies = [links.send(joined_own, joined_all.at[m], "dp", m) for m in (1, 2)]

    load_skip.wait()
    residual[...] = product(frames[...], skip_buf[:width]) + product(skip[...], skip_buf[width:])
    load_ada.wait()
    table[...] = product(table_embed, ada_buf[...]) + b_ada[...].astype(jnp.float32)
    first_row = seq_index * rows
    normal, unused = norm_parts(residual[...])
    row_index = first_row + lax.broadcasted_iota(jnp.int32, (rows, 1), 0)
    own_segment = segments(ends, row_index)
    spread_scale = jnp.zeros((rows, width), jnp.float32)
    spread_shift = jnp.zeros((rows, width), jnp.float32)
    for number in range(len(ends)):
        member = own_segment == number
        spread_scale = jnp.where(member, table[number : number + 1, :width], spread_scale)
        spread_shift = jnp.where(member, table[number : number + 1, width:], spread_shift)
    scale[...] = spread_scale
    first_low = (normal * (1.0 + spread_scale) + spread_shift).astype(jnp.bfloat16)
    first_own[0] = first_low
    for number in range(8):
        place = relative_block(seq_index, jnp.int32(number))
        first_own[1, :, number * 128 : (number + 1) * 128] = first_own[0, :, columns(place * 128, 128)]
    own_copies.append(links.load(first_own.at[1], first_all.at[0]))
    first_copies = [links.send(first_own.at[1], first_all.at[m], "dp", m) for m in (1, 2)]

    cos_own, sin_own = rotary(ends, first_row, rows, 256)
    load_qkv.wait()
    packed_copies = {}
    for far in (2, 1, 3, 0):
        pair = flip(lax.div(seq_index, jnp.int32(2)), far)
        parts = []
        for kind in range(3):
            part = product(first_low, qkv_buf[:, columns(kind * width + pair * 256, 256)])
            if kind < 2:
                part = part * cos_own + partner(part) * sin_own
            parts.append(part.astype(jnp.bfloat16))
        for odd in range(2):
            for kind in range(3):
                packed_send[pair * 2 + odd, :, kind * 128 : (kind + 1) * 128] = parts[kind][
                    :, odd * 128 : (odd + 1) * 128
                ]
        for mask in (2 * far, 2 * far + 1):
            if mask:
                packed_copies[mask] = links.send(
                    packed_send.at[flip(seq_index, mask)], packed.at[seq_index], "seq", mask
                )
    packed[seq_index] = packed_send[seq_index]

    forwards = []
    for slots, copies in ((cot_all, cot_copies), (joined_all, joined_copies)):
        copies[1].wait_recv()
        forwards.append(links.send(slots.at[2], slots.at[3], "dp", 1))
    load_down.wait()

    def gated_step(step, carried):
        part = columns(step * 512, 512)
        grad_gated[:, part] = product_cols(cotangent[...], down_buf[part, :])
        return carried

    lax.fori_loop(0, down_buf.shape[0] // 512, gated_step, 0)
    embed_own = first_own.at[2, :16]
    embed_own[...] = embed
    own_copies.append(links.load(embed_own, embed_all.at[0]))
    embed_copies = [links.send(embed_own, embed_all.at[m], "dp", m) for m in range(1, 4)]
    first_copies[1].wait_recv()
    forwards.append(links.send(first_all.at[2], first_all.at[3], "dp", 1))

    arrived(mask_copies)
    arrived(packed_copies.values())
    key_index = lax.broadcasted_iota(jnp.int32, (1, 8 * rows), 1)
    key_segment = segments(ends, key_index)
    key_valid = jnp.concatenate(
        [
            masks[exclusive(seq_index, jnp.int32(number))][:1]
            for number in range(8)
        ],
        axis=1,
    )

    def attend(place):
        query = packed[place, :, :128]
        row_index = place * rows + lax.broadcasted_iota(jnp.int32, (rows, 1), 0)
        allowed = (segments(ends, row_index) == key_segment) & (
            (key_valid > 0) | (row_index == key_index)
        )
        keys = packed[:, :, 128:256].reshape(8 * rows, 128)
        values = packed[:, :, 256:].reshape(8 * rows, 128)
        total = jnp.zeros((rows, 128), jnp.float32)
        here = pl.ds(pl.multiple_of(place * rows, rows), rows)
        for head in range(2):
            scores = product_cols(head_mask(query, head), keys) * (1.0 / math.sqrt(HEAD))
            scores = jnp.where(allowed, scores, masked_score)
            raised = jnp.exp(scores - jnp.max(scores, axis=1, keepdims=True))
            low = (raised / jnp.sum(raised, axis=1, keepdims=True)).astype(jnp.bfloat16)
            weight_buf[here, head * 1024 : (head + 1) * 1024] = low
            total = total + product(low, head_mask(values, head))
        attn_sum[here, :] = total
        attn_send[place] = total.astype(jnp.bfloat16)

    base = links.used

    def attn_copy(mask):
        target = exclusive(seq_index, mask)
        return pltpu.make_async_remote_copy(
            src_ref=attn_send.at[target],
            dst_ref=attn_low.at[seq_index],
            send_sem=send_sems.at[base + mask],
            recv_sem=recv_sems.at[base + mask],
            device_id=(dp_index, target),
            device_id_type=MESH,
        )

    def attend_step(step, carried):
        mask = 7 - step
        attend(exclusive(seq_index, mask))
        attn_copy(mask).start()
        return carried

    lax.fori_loop(0, 7, attend_step, 0)
    attend(seq_index)
    save = links.load(weight_buf, weights)
    own = pltpu.make_async_copy(
        attn_send.at[seq_index], attn_low.at[seq_index], load_sems.at[links.loads]
    )
    own.start()
    arrived(cot_copies[:1] + joined_copies[:1] + first_copies[:1] + embed_copies + forwards)
    links.drain()
    for mask in range(1, 8):
        attn_copy(jnp.int32(mask)).wait()
    save.wait()
    own.wait()
    for copy in own_copies:
        copy.wait()


def second_kernel(
    lengths, b_up, b_down, gain, joined_in, cot_in, first_in, residual_in, scale_in, gated_in,
    packed_in, weights_in, attn_sum_in, attn_low_in, w_out, w_up, w_down, w_qkv, w_skip,
    result, grad_frames, grad_skip, sum_skip, sum_qkv, sum_out, sum_up, sum_down, small_all,
    out_buf, up_buf, down_buf, weight_buf, attn_sum, packed, attn_low, joined_all, cot_all,
    first_all, attn_all, second_all, gated_all, upper_all, branch_all, packed_all, in_all,
    residual, scale, grad_gated, second_low, gated, gated_parts, upper_parts, residual_mid, normal_mid, grad_mid,
    branch, grad_send, grad_heads, back_send, back_recv, grad_packed, grad_in, key_total, value_total,
    small, small_recv,
    down_send, down_recv, down_a, down_b, up_send, up_recv, up_a, up_b, out_send, out_recv, out_a, out_b,
    qkv_send, qkv_recv, qkv_a, qkv_b, skip_send, skip_recv, skip_a, skip_b,
    send_sems, recv_sems, load_sems,
):
    links = Links(send_sems, recv_sems, load_sems)
    seq_index, dp_index = links.seq_index, links.dp_index
    rows, width = residual.shape
    hidden = grad_gated.shape[1]
    float32, bfloat16 = jnp.float32, jnp.bfloat16
    load_attn = links.load(attn_low_in, attn_low)
    load_out = links.load(w_out, out_buf)
    load_residual = links.load(residual_in, residual)
    load_up = links.load(w_up, up_buf)
    load_gated = links.load(gated_in, grad_gated)
    load_cot = links.load(cot_in, cot_all)
    load_down = links.load(w_down, down_buf)
    load_packed = links.load(packed_in, packed)
    load_sum = links.load(attn_sum_in, attn_sum)
    load_weights = links.load(weights_in, weight_buf)
    load_scale = links.load(scale_in, scale)
    load_first = links.load(first_in, first_all)
    load_joined = links.load(joined_in, joined_all)
    links.barrier()

    def relative(source, target):
        for number in range(8):
            place = relative_block(seq_index, jnp.int32(number))
            target[0, :, number * 128 : (number + 1) * 128] = source[:, columns(place * 128, 128)]

    load_attn.wait()
    for number in range(8):
        place = relative_block(seq_index, jnp.int32(number))
        attn_all[0, :, number * 128 : (number + 1) * 128] = attn_low[place]
    attn_copies = share_start(links, attn_all)
    load_out.wait()
    load_residual.wait()
    joined_attn = jnp.concatenate([attn_low[number] for number in range(8)], axis=1)
    residual_mid[...] = residual[...] + product(joined_attn, out_buf[...])
    normal, factor_mid = norm_parts(residual_mid[...])
    normal_mid[...] = normal
    gain_float = gain[...].astype(float32)
    second_low[...] = (normal * gain_float).astype(bfloat16)
    relative(second_low, second_all)
    second_copies = share_start(links, second_all)
    small[8:] = jnp.zeros((8, small.shape[1]), float32)
    load_up.wait()
    load_gated.wait()

    def up_step(step, carried):
        number = lax.rem(step + 4, jnp.int32(8))
        place = relative_block(seq_index, number)
        part = columns(place * 512, 512)
        upper = product(second_low[...], up_buf[:, part]) + b_up[:, part].astype(float32)
        square = upper * upper
        bent = jnp.tanh(ROOT * (upper + 0.044715 * upper * square))
        low = (0.5 * upper * (1.0 + bent)).astype(bfloat16)
        slope = 0.5 * (1.0 + bent) + 0.5 * upper * (1.0 - bent * bent) * ROOT * (
            1.0 + 3.0 * 0.044715 * square
        )
        grad_upper = (grad_gated[:, part] * slope).astype(bfloat16)
        gated[:, part] = low
        for quarter in range(4):
            gated_parts[quarter, :, columns(number * 128, 128)] = low[
                :, quarter * 128 : (quarter + 1) * 128
            ]
        upper_parts[lax.div(place, jnp.int32(2)), :, columns(bit(place, 0) * 512, 512)] = grad_upper
        small[
            pl.ds(8 + lax.div(place, jnp.int32(4)), 1),
            columns(lax.rem(place, jnp.int32(4)) * 512, 512),
        ] = jnp.sum(grad_upper.astype(float32), axis=0, keepdims=True)
        return carried

    lax.fori_loop(0, 8, up_step, 0)
    gated_copies = [
        links.send(gated_parts.at[flip(dp_index, m)], gated_all.at[m], "dp", m) for m in (3, 2, 1)
    ]
    upper_copies = [
        links.send(upper_parts.at[flip(dp_index, m)], upper_all.at[m], "dp", m) for m in (3, 2, 1)
    ]
    gated_all[0] = gated_parts[dp_index]
    upper_all[0] = upper_parts[dp_index]
    attn_copies = share_forward(links, attn_all, attn_copies)
    second_copies = share_forward(links, second_all, second_copies)

    key_total[...] = jnp.zeros_like(key_total)
    value_total[...] = jnp.zeros_like(value_total)

    def second_step(step, total):
        return total + product_cols(
            upper_parts[lax.div(step, jnp.int32(2)), :, columns(bit(step, 0) * 512, 512)],
            up_buf[:, columns(step * 512, 512)],
        )

    grad_second = lax.fori_loop(0, 8, second_step, jnp.zeros((rows, width), float32))
    load_qkv = links.load(w_qkv, up_buf.at[:, : 3 * width])
    load_cot.wait()
    grad_out = cot_all[0].astype(float32)
    normal = normal_mid[...]
    small[10:11, :width] = jnp.sum(grad_second * normal, axis=0, keepdims=True)
    small[10:11, width:] = jnp.sum(grad_out, axis=0, keepdims=True)
    grad_mid[...] = grad_out + norm_back(grad_second * gain_float, normal, factor_mid)
    branch[...] = grad_mid[...].astype(bfloat16)
    branch_copies = [
        links.send(branch.at[:, columns(flip(dp_index, m) * 256, 256)], branch_all.at[m], "dp", m)
        for m in (3, 2, 1)
    ]
    branch_all[0] = branch[:, columns(dp_index * 256, 256)]
    grad_attn = product_cols(branch[...], out_buf[...]).astype(bfloat16)
    for number in range(8):
        grad_send[number] = grad_attn[:, number * 128 : (number + 1) * 128]
    head_copies = [
        links.send(grad_send.at[flip(seq_index, m)], grad_heads.at[seq_index], "seq", m)
        for m in FAR_FIRST
    ]
    grad_heads[seq_index] = grad_send[seq_index]

    def piece(left, right, start, size):
        return product_rows(
            left[:, :, columns(start, size)].reshape(4 * rows, size),
            right[...].reshape(4 * rows, right.shape[2]),
        )

    class Sum:
        def __init__(self, left, right, send, recv, recv_a, recv_b):
            self.left, self.right, self.out, self.into = left, right, send, recv
            self.into_a, self.into_b = recv_a, recv_b
            self.half = send.shape[0]
            self.size = self.half // 4

        def begin(self):
            def step(number, carried):
                start = pl.multiple_of(number * 256, 256)
                self.out[pl.ds(start, 256), :] = piece(
                    self.left, self.right, self.half + start, 256
                ).astype(bfloat16)
                return carried

            lax.fori_loop(0, self.half // 256, step, 0)
            self.copy = links.send(self.out, self.into, "seq", STEPS[0])

        def part(self, low, high):
            def step(number, carried):
                start = pl.multiple_of(number * 256, 256)
                here = pl.ds(start, 256)
                self.out[here, :] = (
                    piece(self.left, self.right, start, 256) + self.into[here, :].astype(float32)
                ).astype(bfloat16)
                return carried

            lax.fori_loop(low // 256, high // 256, step, 0)

        def second(self):
            links.settle(self.copy)
            self.part(2 * self.size, 4 * self.size)
            self.copy = links.send(
                self.out.at[2 * self.size :], self.into_a, "seq", STEPS[1]
            )
            self.part(0, 2 * self.size)

        def third(self):
            self.copy.wait_recv()
            both = pl.ds(0, 2 * self.size)
            self.into[both, :] = (
                self.out[both, :].astype(float32) + self.into_a[...].astype(float32)
            ).astype(bfloat16)
            self.copy = links.send(
                self.into.at[self.size : 2 * self.size], self.into_b, "seq", STEPS[2]
            )

        def last(self, target, spread):
            self.copy.wait_recv()
            own = pl.ds(0, self.size)
            self.out[own, :] = (
                self.into[own, :].astype(float32) + self.into_b[...].astype(float32)
            ).astype(bfloat16)

            def place(index):
                if spread == 0:
                    return target.at[pl.ds(index * self.size, self.size), :]
                size = self.out.shape[1]
                return target.at[:, columns(index * size, size)]

            self.target = place
            ready = self.out.at[: self.size]
            self.across = links.send(ready, place(dp_index), "dp", 2)
            self.core = links.send(ready, place(dp_index), "dp", 1)
            self.own = links.load(ready, place(dp_index))

        def spread(self):
            self.across.wait_recv()
            other = self.target(flip(dp_index, 2))
            self.far = links.send(other, other, "dp", 1)

        def finish(self):
            self.own.wait()
            arrived([self.core, self.far])

    down = Sum(gated_all, cot_all, down_send, down_recv, down_a, down_b)
    up = Sum(second_all, upper_all, up_send, up_recv, up_a, up_b)
    out = Sum(attn_all, branch_all, out_send, out_recv, out_a, out_b)
    qkv = Sum(first_all, packed_all, qkv_send, qkv_recv, qkv_a, qkv_b)
    skip = Sum(joined_all, in_all, skip_send, skip_recv, skip_a, skip_b)

    arrived(gated_copies)
    down.begin()
    arrived(upper_copies)
    arrived(second_copies)
    up.begin()
    load_down.wait()

    def down_step(step, total):
        part = columns(step * 512, 512)
        return total + product(gated[:, part], down_buf[part, :])

    lower = lax.fori_loop(
        0, 8, down_step, residual_mid[...] + b_down[...].astype(float32)
    )
    result[...] = lower.astype(bfloat16)
    load_skip = links.load(w_skip, down_buf.at[: 2 * width])
    arrived(branch_copies)
    arrived(attn_copies)
    out.begin()

    ends = utterance_ends(lengths)
    load_packed.wait()
    load_sum.wait()
    load_weights.wait()
    arrived(head_copies)
    shrink = 1.0 / math.sqrt(HEAD)

    def back_step(place, carried):
        here = pl.ds(pl.multiple_of(place * rows, rows), rows)
        grad = grad_heads[place]
        query = packed[place, :, :128]
        keys = packed[:, :, 128:256].reshape(8 * rows, 128)
        values = packed[:, :, 256:].reshape(8 * rows, 128)
        both = grad.astype(float32) * attn_sum[here, :]
        total = jnp.zeros((rows, 128), float32)
        for head in range(2):
            low = weight_buf[here, head * 1024 : (head + 1) * 1024]
            grad_head = head_mask(grad, head)
            delta = jnp.sum(head_mask(both, head), axis=1, keepdims=True)
            grad_scores = (
                low.astype(float32) * (product_cols(grad_head, values) - delta)
            ).astype(bfloat16)
            total = total + product(grad_scores, head_mask(keys, head))
            key_total[...] += product_rows(grad_scores, head_mask(query, head))
            value_total[...] += product_rows(low, grad_head)
        total = total * shrink
        cosine, sine = rotary(ends, place * rows, rows, 128)
        back_send[place, :, :128] = (total * cosine - partner(total) * sine).astype(bfloat16)
        return carried

    lax.fori_loop(0, 8, back_step, 0)

    def key_step(place, carried):
        here = pl.ds(pl.multiple_of(place * rows, rows), rows)
        total = key_total[here, :] * shrink
        cosine, sine = rotary(ends, place * rows, rows, 128)
        back_send[place, :, 128:256] = (total * cosine - partner(total) * sine).astype(bfloat16)
        back_send[place, :, 256:] = value_total[here, :].astype(bfloat16)
        return carried

    lax.fori_loop(0, 8, key_step, 0)
    back_copies = [
        links.send(back_send.at[flip(seq_index, m)], back_recv.at[seq_index], "seq", m)
        for m in FAR_FIRST
    ]
    back_recv[seq_index] = back_send[seq_index]
    down.second()
    up.second()
    out.second()

    arrived(back_copies)
    for number in range(8):
        for kind in range(3):
            grad_packed[:, kind * width + number * 128 : kind * width + (number + 1) * 128] = (
                back_recv[number, :, kind * 128 : (kind + 1) * 128]
            )
    packed_copies = [
        links.send(
            grad_packed.at[:, columns(flip(dp_index, m) * 768, 768)], packed_all.at[m], "dp", m
        )
        for m in (3, 2, 1)
    ]
    packed_all[0] = grad_packed[:, columns(dp_index * 768, 768)]
    load_qkv.wait()

    def first_step(step, total):
        part = columns(step * 512, 512)
        return total + product_cols(grad_packed[:, part], up_buf[:, part])

    grad_first = lax.fori_loop(0, 6, first_step, jnp.zeros((rows, width), float32))
    normal, factor = norm_parts(residual[...])
    load_scale.wait()
    grad_in[...] = (
        grad_mid[...] + norm_back(grad_first * (1.0 + scale[...]), normal, factor)
    ).astype(bfloat16)
    in_copies = [
        links.send(grad_in.at[:, columns(flip(dp_index, m) * 256, 256)], in_all.at[m], "dp", m)
        for m in (3, 2, 1)
    ]
    in_all[0] = grad_in[:, columns(dp_index * 256, 256)]
    row_index = seq_index * rows + lax.broadcasted_iota(jnp.int32, (rows, 1), 0)
    own_segment = segments(ends, row_index)
    scaled = grad_first * normal
    for number in range(len(ends)):
        member = own_segment == number
        small[number : number + 1, :width] = jnp.sum(
            jnp.where(member, scaled, 0.0), axis=0, keepdims=True
        )
        small[number : number + 1, width:] = jnp.sum(
            jnp.where(member, grad_first, 0.0), axis=0, keepdims=True
        )
    small_copy = links.send(small, small_recv.at[0], "seq", STEPS[0])
    load_first.wait()
    arrived(packed_copies)
    qkv.begin()
    load_joined.wait()
    arrived(in_copies)
    skip.begin()
    down.third()
    up.third()
    out.third()
    load_skip.wait()
    for target, start in ((grad_frames, 0), (grad_skip, width)):
        target[...] = product_cols(grad_in[...], down_buf[start : start + width, :])
    links.settle(small_copy)
    small[...] = small[...] + small_recv[0]
    small_copy = links.send(small, small_recv.at[1], "seq", STEPS[1])
    down.last(sum_down, 0)
    up.last(sum_up, 1)
    out.last(sum_out, 1)
    qkv.second()
    skip.second()
    links.settle(small_copy)
    small[...] = small[...] + small_recv[1]
    small_copy = links.send(small, small_recv.at[2], "seq", STEPS[2])
    down.spread()
    up.spread()
    out.spread()
    qkv.third()
    skip.third()
    links.settle(small_copy)
    small[...] = small[...] + small_recv[2]
    small_across = links.send(small, small_all.at[dp_index], "dp", 2)
    small_core = links.send(small, small_all.at[dp_index], "dp", 1)
    small_far = links.send(small, small_all.at[dp_index], "dp", 3)
    small_own = links.load(small, small_all.at[dp_index])
    qkv.last(sum_qkv, 1)
    skip.last(sum_skip, 1)
    qkv.spread()
    skip.spread()
    small_own.wait()
    arrived([small_across, small_core, small_far])
    for each in (down, up, out, qkv, skip):
        each.finish()
    links.drain()


def two_kernels(
    frames, skip, lengths, frame_mask, time_step, w_skip, w_ada, b_ada, w_qkv, w_out, norm_gain,
    w_up, b_up, w_down, b_down, cotangent,
):
    rows, width = frames.shape[1:]
    hidden = b_up.shape[0]
    seq_index = lax.axis_index("seq")
    float32, bfloat16 = jnp.float32, jnp.bfloat16
    shape = jax.ShapeDtypeStruct
    vmem = pl.BlockSpec(memory_space=pltpu.VMEM)
    smem = pl.BlockSpec(memory_space=pltpu.SMEM)
    anywhere = pl.BlockSpec(memory_space=pl.ANY)
    dma = pltpu.SemaphoreType.DMA

    first_outs = (
        (shape((4, rows, 2 * width), bfloat16), anywhere),
        (shape((4, rows, width), bfloat16), anywhere),
        (shape((4, rows, width), bfloat16), anywhere),
        (shape((4, 16, width), bfloat16), anywhere),
        (shape((rows, width), float32), vmem),
        (shape((rows, width), float32), vmem),
        (shape((rows, hidden), float32), vmem),
        (shape((8, rows, 384), bfloat16), vmem),
        (shape((8 * rows, 2048), bfloat16), anywhere),
        (shape((8 * rows, 128), float32), vmem),
        (shape((8, rows, 128), bfloat16), anywhere),
    )
    (
        joined_all, cot_all, first_all, embed_all, residual, scale, grad_gated, packed, weights,
        attn_sum, attn_low,
    ) = pl.pallas_call(
        first_kernel,
        out_shape=tuple(item[0] for item in first_outs),
        in_specs=[smem, smem, vmem, vmem, vmem, vmem, vmem, anywhere, anywhere, anywhere, anywhere],
        out_specs=tuple(item[1] for item in first_outs),
        scratch_shapes=[
            pltpu.VMEM(w_skip.shape, bfloat16),
            pltpu.VMEM(w_ada.shape, bfloat16),
            pltpu.VMEM(w_qkv.shape, bfloat16),
            pltpu.VMEM(w_down.shape, bfloat16),
            pltpu.VMEM((rows, 2 * width), bfloat16),
            pltpu.VMEM((3, rows, width), bfloat16),
            pltpu.VMEM((16, 2 * width), float32),
            pltpu.VMEM((8, rows, 384), bfloat16),
            pltpu.VMEM((8, rows, 128), bfloat16),
            pltpu.VMEM((8, 8, rows), jnp.int32),
            pltpu.VMEM((8 * rows, 2048), bfloat16),
            dma((48,)),
            dma((48,)),
            dma((12,)),
        ],
        compiler_params=pltpu.CompilerParams(
            collective_id=0, has_side_effects=True, vmem_limit_bytes=58 * MIB
        ),
        name="first",
    )(
        lengths, time_step, frame_mask, frames[0], skip[0], cotangent[0], b_ada[None], w_skip,
        w_ada, w_qkv, w_down,
    )

    sums = ((1024, 1024), (1024, 1024), (1024, 256), (1024, 768), (2048, 256))
    sum_scratch = []
    for tall, wide in sums:
        sum_scratch += [pltpu.VMEM((tall // part, wide), bfloat16) for part in (2, 2, 4, 8)]
    second_outs = (
        (shape((rows, width), bfloat16), vmem),
        (shape((rows, width), float32), vmem),
        (shape((rows, width), float32), vmem),
        (shape((2 * width // 8, width), bfloat16), anywhere),
        (shape((width // 8, 3 * width), bfloat16), anywhere),
        (shape((width // 8, width), bfloat16), anywhere),
        (shape((width // 8, hidden), bfloat16), anywhere),
        (shape((hidden // 8, width), bfloat16), anywhere),
        (shape((4, 16, 2 * width), float32), anywhere),
    )
    low = lambda *size: pltpu.VMEM(size, bfloat16)
    full = lambda *size: pltpu.VMEM(size, float32)
    (
        result, grad_frames, grad_skip, sum_skip, sum_qkv, sum_out, sum_up, sum_down, small_all,
    ) = pl.pallas_call(
        second_kernel,
        out_shape=tuple(item[0] for item in second_outs),
        in_specs=[smem, vmem, vmem, vmem] + [anywhere] * 15,
        out_specs=tuple(item[1] for item in second_outs),
        scratch_shapes=[
            low(*w_out.shape), low(*w_up.shape), low(*w_down.shape), low(8 * rows, 2048),
            full(8 * rows, 128), low(8, rows, 384), low(8, rows, 128),
            low(4, rows, 2 * width), low(4, rows, width), low(4, rows, width),
            low(4, rows, width), low(4, rows, width), low(4, rows, width), low(4, rows, width),
            low(4, rows, 256), low(4, rows, 768), low(4, rows, 256),
            full(rows, width), full(rows, width), full(rows, hidden), low(rows, width),
            low(rows, hidden), low(4, rows, width), low(4, rows, width),
            full(rows, width), full(rows, width), full(rows, width),
            low(rows, width), low(8, rows, 128), low(8, rows, 128), low(8, rows, 384), low(8, rows, 384),
            low(rows, 3 * width), low(rows, width), full(8 * rows, 128), full(8 * rows, 128),
            full(16, 2 * width), full(3, 16, 2 * width),
            *sum_scratch,
            dma((90,)), dma((90,)), dma((24,)),
        ],
        compiler_params=pltpu.CompilerParams(
            collective_id=1, has_side_effects=True, vmem_limit_bytes=60 * MIB
        ),
        name="second",
    )(
        lengths, b_up[None], b_down[None], norm_gain[None], joined_all, cot_all, first_all,
        residual, scale, grad_gated, packed, weights, attn_sum, attn_low, w_out, w_up, w_down,
        w_qkv, w_skip,
    )

    dp_index = lax.axis_index("dp")
    embed_ordered = jnp.stack(
        [lax.dynamic_index_in_dim(embed_all, dp_index ^ number, 0, False) for number in range(4)]
    )
    count_utter = lengths.shape[1]
    ada_all = small_all[:, :count_utter].reshape(-1, 2 * width)
    vectors = jnp.sum(small_all[:, count_utter:], axis=0)
    own_embed = lax.dynamic_slice_in_dim(embed_ordered, seq_index * 128, 128, axis=2)
    own_embed = own_embed[:, :count_utter].reshape(-1, 128).astype(float32)
    total_ada = lax.dot_general(own_embed, ada_all, contract_rows, precision=precise)
    bias = lambda values, size: lax.dynamic_slice_in_dim(values, seq_index * size, size)
    wide = lambda values: values.astype(float32)
    return (
        result[None],
        grad_frames[None],
        grad_skip[None],
        wide(sum_skip),
        total_ada,
        bias(jnp.sum(ada_all, axis=0), 256),
        wide(sum_qkv),
        wide(sum_out),
        bias(vectors[2, :width], 128),
        wide(sum_up),
        bias(vectors[:2].reshape(-1), 512),
        wide(sum_down),
        bias(vectors[2, width:], 128),
    )


def solution(mesh):
    placed = (
        P("dp", "seq", None),
        P("dp", "seq", None),
        P("dp", None),
        P("dp", "seq"),
        P("dp", None),
        P(),
        P(),
        P(),
        P(),
        P(),
        P(),
        P(),
        P(),
        P(),
        P(),
        P("dp", "seq", None),
    )
    split_heads = mesh.shape["dp"] == 4 and mesh.shape["seq"] == len(RELATIVE)
    return jax.shard_map(
        two_kernels if split_heads else on_device,
        mesh=mesh,
        in_specs=placed,
        out_specs=(
            P("dp", "seq", None),
            P("dp", "seq", None),
            P("dp", "seq", None),
            P("seq", None),
            P("seq", None),
            P("seq"),
            P("seq", None),
            P("seq", None),
            P("seq"),
            P("seq", None),
            P("seq"),
            P("seq", None),
            P("seq"),
        ),
        check_vma=False,
    )
```

```python
import math

import jax
import jax.numpy as jnp
from jax import lax
from jax.experimental import pallas as pl
from jax.experimental.pallas import tpu as pltpu
from jax.sharding import PartitionSpec as P

HEADS = 16
HEAD = 64
TSTEPS = 32


precise = lax.Precision.HIGHEST
masked_score = -1e30
contract_rows = (((0,), (0,)), ((), ()))
contract_cols = (((1,), (1,)), ((), ()))


def divisor_below(count_all, upper_limit):
    size_now = min(count_all, upper_limit)
    while count_all % size_now:
        size_now -= 1
    return size_now


def normalize(values):
    centered = values - jnp.mean(values, axis=-1, keepdims=True)
    variance = jnp.mean(centered * centered, axis=-1, keepdims=True)
    return centered * lax.rsqrt(variance + 1e-06)


def segment_of(lengths, frame_index):
    utter_ends = jnp.cumsum(lengths)
    return jnp.sum((frame_index[:, None] >= utter_ends[None, :]).astype(jnp.int32), axis=1)


def utterance_layout(lengths, frame_index):
    utter_ends = jnp.cumsum(lengths)
    starts = utter_ends - lengths
    segment = segment_of(lengths, frame_index)
    member = segment[:, None] == jnp.arange(lengths.shape[0], dtype=jnp.int32)[None, :]
    position = frame_index - jnp.sum(jnp.where(member, starts[None, :], 0), axis=1)
    return (segment, position, member)


def rotary_tables(position, head_size):
    half_size = head_size // 2
    frequency = jnp.exp(
        jnp.arange(half_size, dtype=jnp.float32) * (-2.0 * math.log(10000.0) / head_size)
    )
    angles = position.astype(jnp.float32)[:, None] * frequency[None, :]
    return (jnp.cos(angles)[:, None, :], jnp.sin(angles)[:, None, :])


def rotate(values, cos_table, sin_table):
    half_size = values.shape[-1] // 2
    first_half = values[..., :half_size]
    second_half = values[..., half_size:]
    return jnp.concatenate(
        [
            first_half * cos_table - second_half * sin_table,
            second_half * cos_table + first_half * sin_table,
        ],
        axis=-1,
    )


def rotate_back(values, cos_table, sin_table):
    half_size = values.shape[-1] // 2
    first_half = values[..., :half_size]
    second_half = values[..., half_size:]
    return jnp.concatenate(
        [
            first_half * cos_table + second_half * sin_table,
            second_half * cos_table - first_half * sin_table,
        ],
        axis=-1,
    )


def time_embedding(steps, model_width):
    half_size = model_width // 2
    flow_time = steps.astype(jnp.float32) / TSTEPS
    frequency = jnp.exp(jnp.arange(half_size, dtype=jnp.float32) * (-math.log(10000.0) / half_size))
    angles = 1000.0 * flow_time[:, None] * frequency[None, :]
    return jnp.concatenate([jnp.sin(angles), jnp.cos(angles)], axis=1)


def make_attend(query_low, query_segment, query_index, lengths):
    count_rows, head_count, head_size = query_low.shape
    scale_factor = 1.0 / math.sqrt(head_size)

    def attend(running, key_piece, first_row):
        keys_part, values_part, valid_part = key_piece
        count_keys = keys_part.shape[0]
        block_rows = divisor_below(count_keys, 1024)
        block_count = count_keys // block_rows
        key_blocks = keys_part.reshape(block_count, block_rows, head_count, head_size)
        value_blocks = values_part.reshape(block_count, block_rows, head_count, head_size)
        valid_blocks = valid_part.reshape(block_count, block_rows)
        offsets = first_row + jnp.arange(block_count, dtype=jnp.int32) * block_rows

        def attend_block_step(carried, inputs):
            row_top, row_total, weighted = carried
            key_block, value_block, valid_block, offset = inputs
            key_index = offset + jnp.arange(block_rows, dtype=jnp.int32)
            key_segment = segment_of(lengths, key_index)
            allowed = (query_segment[:, None] == key_segment[None, :]) & (
                (valid_block[None, :] > 0) | (query_index[:, None] == key_index[None, :])
            )
            scores = (
                jnp.einsum("qhd,khd->hqk", query_low, key_block, preferred_element_type=jnp.float32)
                * scale_factor
            )
            scores = jnp.where(allowed[None], scores, masked_score)
            new_top = jnp.maximum(row_top, jnp.max(scores, axis=2))
            weights = jnp.where(allowed[None], jnp.exp(scores - new_top[:, :, None]), 0.0)
            factor = jnp.exp(row_top - new_top)
            row_total = row_total * factor + jnp.sum(weights, axis=2)
            weighted = weighted * jnp.transpose(factor)[:, :, None] + jnp.einsum(
                "hqk,khd->qhd",
                weights.astype(jnp.bfloat16),
                value_block,
                preferred_element_type=jnp.float32,
            )
            return ((new_top, row_total, weighted), None)

        result_state, unused = lax.scan(
            attend_block_step, running, (key_blocks, value_blocks, valid_blocks, offsets)
        )
        return result_state

    return attend


def key_sweep(
    query_low, grad_attn, log_total, row_delta, query_segment, query_index, lengths, key_tuple
):
    keys_all, values_all, valid_all = key_tuple
    count_rows, head_count, head_size = query_low.shape
    scale_factor = 1.0 / math.sqrt(head_size)
    count_keys = keys_all.shape[0]
    block_rows = divisor_below(count_keys, 1024)
    block_count = count_keys // block_rows
    key_blocks = keys_all.reshape(block_count, block_rows, head_count, head_size)
    value_blocks = values_all.reshape(block_count, block_rows, head_count, head_size)
    valid_blocks = valid_all.reshape(block_count, block_rows)
    offsets = jnp.arange(block_count, dtype=jnp.int32) * block_rows
    top_shift = jnp.transpose(log_total)[:, :, None]
    delta_shift = jnp.transpose(row_delta)[:, :, None]

    def key_block_step(grad_query, inputs):
        key_block, value_block, valid_block, offset = inputs
        key_index = offset + jnp.arange(block_rows, dtype=jnp.int32)
        key_segment = segment_of(lengths, key_index)
        allowed = (query_segment[:, None] == key_segment[None, :]) & (
            (valid_block[None, :] > 0) | (query_index[:, None] == key_index[None, :])
        )
        scores = (
            jnp.einsum("qhd,khd->hqk", query_low, key_block, preferred_element_type=jnp.float32)
            * scale_factor
        )
        weights = jnp.where(allowed[None], jnp.exp(scores - top_shift), 0.0)
        grad_weights = jnp.einsum(
            "qhd,khd->hqk", grad_attn, value_block, preferred_element_type=jnp.float32
        )
        grad_scores = (weights * (grad_weights - delta_shift)).astype(jnp.bfloat16)
        grad_query = (
            grad_query
            + jnp.einsum("hqk,khd->qhd", grad_scores, key_block, preferred_element_type=jnp.float32)
            * scale_factor
        )
        grad_key = (
            jnp.einsum("hqk,qhd->khd", grad_scores, query_low, preferred_element_type=jnp.float32)
            * scale_factor
        )
        grad_value = jnp.einsum(
            "hqk,qhd->khd",
            weights.astype(jnp.bfloat16),
            grad_attn,
            preferred_element_type=jnp.float32,
        )
        return (grad_query, (grad_key, grad_value))

    start_grad = jnp.zeros((count_rows, head_count, head_size), jnp.float32)
    return lax.scan(key_block_step, start_grad, (key_blocks, value_blocks, valid_blocks, offsets))


def on_device(
    frames,
    skip,
    lengths,
    frame_mask,
    time_step,
    w_skip,
    w_ada,
    b_ada,
    w_qkv,
    w_out,
    norm_gain,
    w_up,
    b_up,
    w_down,
    b_down,
    cotangent,
):
    local_frames = frames[0]
    local_skip = skip[0]
    row_lengths = lengths[0]
    count_rows, model_width = local_frames.shape
    head_count = HEADS
    head_size = HEAD
    row_base = lax.axis_index("seq") * count_rows
    frame_index = row_base + jnp.arange(count_rows, dtype=jnp.int32)
    segment, position, member = utterance_layout(row_lengths, frame_index)
    member_float = member.astype(jnp.float32)
    embed_low = time_embedding(time_step[0], model_width).astype(jnp.bfloat16)
    ada_table = jnp.dot(embed_low, w_ada, preferred_element_type=jnp.float32) + b_ada.astype(
        jnp.float32
    )
    ada_frame = jnp.dot(member_float, ada_table, precision=precise)
    scale_part = ada_frame[:, :model_width]
    shift_part = ada_frame[:, model_width:]
    joined = jnp.concatenate([local_frames, local_skip], axis=1)
    residual_in = jnp.dot(joined, w_skip, preferred_element_type=jnp.float32)
    norm_first, first_pull = jax.vjp(normalize, residual_in)
    first_low = (norm_first * (1.0 + scale_part) + shift_part).astype(jnp.bfloat16)
    packed = jnp.dot(first_low, w_qkv, preferred_element_type=jnp.float32)
    cos_table, sin_table = rotary_tables(position, head_size)
    query_low = rotate(
        packed[:, :model_width].reshape(count_rows, head_count, head_size), cos_table, sin_table
    ).astype(jnp.bfloat16)
    keys_low = (
        rotate(
            packed[:, model_width : 2 * model_width].reshape(count_rows, head_count, head_size),
            cos_table,
            sin_table,
        )
        .astype(jnp.bfloat16)
        .reshape(count_rows, model_width)
    )
    values_low = packed[:, 2 * model_width :].astype(jnp.bfloat16)
    valid_low = frame_mask[0].astype(jnp.bfloat16)
    attend = make_attend(query_low, segment, frame_index, row_lengths)
    start_state = (
        jnp.full((head_count, count_rows), masked_score, jnp.float32),
        jnp.zeros((head_count, count_rows), jnp.float32),
        jnp.zeros((count_rows, head_count, head_size), jnp.float32),
    )
    gathered = (
        lax.all_gather(keys_low, "seq", axis=0, tiled=True),
        lax.all_gather(values_low, "seq", axis=0, tiled=True),
        lax.all_gather(valid_low, "seq", axis=0, tiled=True),
    )
    row_top, row_total, weighted = attend(start_state, gathered, 0)
    attn_sum = weighted / jnp.transpose(row_total)[:, :, None]
    log_total = jnp.transpose(row_top + jnp.log(row_total))
    attn_low = attn_sum.reshape(count_rows, model_width).astype(jnp.bfloat16)
    residual_mid = residual_in + jnp.dot(attn_low, w_out, preferred_element_type=jnp.float32)
    gain_float = norm_gain.astype(jnp.float32)
    second_float, second_pull = jax.vjp(
        lambda hidden, gain_vector: normalize(hidden) * gain_vector, residual_mid, gain_float
    )
    second_low = second_float.astype(jnp.bfloat16)
    upper_sum = jnp.dot(second_low, w_up, preferred_element_type=jnp.float32) + b_up.astype(
        jnp.float32
    )
    gated_float, gelu_pull = jax.vjp(
        lambda hidden: jax.nn.gelu(hidden, approximate=True), upper_sum
    )
    gated_low = gated_float.astype(jnp.bfloat16)
    output = (
        residual_mid
        + jnp.dot(gated_low, w_down, preferred_element_type=jnp.float32)
        + b_down.astype(jnp.float32)
    )
    grad_out = cotangent[0]
    grad_out_float = grad_out.astype(jnp.float32)
    grad_down = lax.dot_general(
        gated_low, grad_out, contract_rows, preferred_element_type=jnp.float32
    )
    grad_down_bias = jnp.sum(grad_out_float, axis=0)
    grad_gated = lax.dot_general(
        grad_out, w_down, contract_cols, preferred_element_type=jnp.float32
    )
    grad_upper = gelu_pull(grad_gated)[0].astype(jnp.bfloat16)
    grad_up = lax.dot_general(
        second_low, grad_upper, contract_rows, preferred_element_type=jnp.float32
    )
    grad_up_bias = jnp.sum(grad_upper.astype(jnp.float32), axis=0)
    grad_second = lax.dot_general(
        grad_upper, w_up, contract_cols, preferred_element_type=jnp.float32
    )
    grad_mid_norm, grad_gain = second_pull(grad_second)
    grad_mid = grad_out_float + grad_mid_norm
    grad_branch = grad_mid.astype(jnp.bfloat16)
    grad_out_weight = lax.dot_general(
        attn_low, grad_branch, contract_rows, preferred_element_type=jnp.float32
    )
    grad_attn = (
        lax.dot_general(grad_branch, w_out, contract_cols, preferred_element_type=jnp.float32)
        .astype(jnp.bfloat16)
        .reshape(count_rows, head_count, head_size)
    )
    row_delta = jnp.sum(grad_attn.astype(jnp.float32) * attn_sum, axis=2)
    grad_query, key_parts = key_sweep(
        query_low, grad_attn, log_total, row_delta, segment, frame_index, row_lengths, gathered
    )
    grad_key_all, grad_value_all = key_parts
    total_keys = grad_key_all.shape[0] * grad_key_all.shape[1]
    grad_key, grad_value = (
        lax.psum_scatter(
            grad_key_all.reshape(total_keys, model_width), "seq", scatter_dimension=0, tiled=True
        ),
        lax.psum_scatter(
            grad_value_all.reshape(total_keys, model_width), "seq", scatter_dimension=0, tiled=True
        ),
    )
    grad_key = rotate_back(
        grad_key.reshape(count_rows, head_count, head_size), cos_table, sin_table
    ).reshape(count_rows, model_width)
    grad_query = rotate_back(grad_query, cos_table, sin_table).reshape(count_rows, model_width)
    grad_packed = jnp.concatenate([grad_query, grad_key, grad_value], axis=1).astype(jnp.bfloat16)
    grad_qkv = lax.dot_general(
        first_low, grad_packed, contract_rows, preferred_element_type=jnp.float32
    )
    grad_first = lax.dot_general(
        grad_packed, w_qkv, contract_cols, preferred_element_type=jnp.float32
    )
    grad_ada_frame = jnp.concatenate([grad_first * norm_first, grad_first], axis=1)
    grad_ada_table = lax.dot_general(member_float, grad_ada_frame, contract_rows, precision=precise)
    grad_ada = lax.dot_general(
        embed_low.astype(jnp.float32), grad_ada_table, contract_rows, precision=precise
    )
    grad_ada_bias = jnp.sum(grad_ada_table, axis=0)
    grad_in = (grad_mid + first_pull(grad_first * (1.0 + scale_part))[0]).astype(jnp.bfloat16)
    grad_skip_weight = lax.dot_general(
        joined, grad_in, contract_rows, preferred_element_type=jnp.float32
    )
    grad_joined = lax.dot_general(
        grad_in, w_skip, contract_cols, preferred_element_type=jnp.float32
    )
    (
        share_skip,
        share_ada,
        share_ada_bias,
        share_qkv,
        share_out,
        share_gain,
        share_up,
        share_up_bias,
        share_down,
        share_down_bias,
    ) = (
        lax.psum_scatter(grad_skip_weight, "seq", scatter_dimension=0, tiled=True),
        lax.psum_scatter(grad_ada, "seq", scatter_dimension=0, tiled=True),
        lax.psum_scatter(grad_ada_bias, "seq", scatter_dimension=0, tiled=True),
        lax.psum_scatter(grad_qkv, "seq", scatter_dimension=0, tiled=True),
        lax.psum_scatter(grad_out_weight, "seq", scatter_dimension=0, tiled=True),
        lax.psum_scatter(grad_gain, "seq", scatter_dimension=0, tiled=True),
        lax.psum_scatter(grad_up, "seq", scatter_dimension=0, tiled=True),
        lax.psum_scatter(grad_up_bias, "seq", scatter_dimension=0, tiled=True),
        lax.psum_scatter(grad_down, "seq", scatter_dimension=0, tiled=True),
        lax.psum_scatter(grad_down_bias, "seq", scatter_dimension=0, tiled=True),
    )
    (
        total_skip,
        total_ada,
        total_ada_bias,
        total_qkv,
        total_out,
        total_gain,
        total_up,
        total_up_bias,
        total_down,
        total_down_bias,
    ) = (
        lax.psum(share_skip.astype(jnp.bfloat16), "dp").astype(jnp.float32),
        lax.psum(share_ada.astype(jnp.bfloat16), "dp").astype(jnp.float32),
        lax.psum(share_ada_bias.astype(jnp.bfloat16), "dp").astype(jnp.float32),
        lax.psum(share_qkv.astype(jnp.bfloat16), "dp").astype(jnp.float32),
        lax.psum(share_out.astype(jnp.bfloat16), "dp").astype(jnp.float32),
        lax.psum(share_gain.astype(jnp.bfloat16), "dp").astype(jnp.float32),
        lax.psum(share_up.astype(jnp.bfloat16), "dp").astype(jnp.float32),
        lax.psum(share_up_bias.astype(jnp.bfloat16), "dp").astype(jnp.float32),
        lax.psum(share_down.astype(jnp.bfloat16), "dp").astype(jnp.float32),
        lax.psum(share_down_bias.astype(jnp.bfloat16), "dp").astype(jnp.float32),
    )
    return (
        output.astype(jnp.bfloat16)[None],
        grad_joined[:, :model_width][None],
        grad_joined[:, model_width:][None],
        total_skip,
        total_ada,
        total_ada_bias,
        total_qkv,
        total_out,
        total_gain,
        total_up,
        total_up_bias,
        total_down,
        total_down_bias,
    )


RELATIVE = (0, 6, 2, 4, 1, 7, 3, 5)
PAIRS = (0, 3, 1, 2)
MESH = pl.DeviceIdType.MESH
MIB = 2**20
FAR_FIRST = (4, 5, 2, 3, 6, 7, 1)
GROUP = ((2, 0), (0, 1), (2, 1), (3, 0), (3, 1), (1, 1), (1, 0))
ROOT = math.sqrt(2.0 / math.pi)


def bit(value, place):
    return lax.rem(lax.div(value, jnp.int32(1 << place)), jnp.int32(2))


def flip(value, mask):
    out = value
    for place in range(3):
        if (mask >> place) & 1:
            out = out + (1 << place) * (1 - 2 * bit(value, place))
    return out


def exclusive(value, other):
    return sum(
        (1 << place) * lax.rem(bit(value, place) + bit(other, place), jnp.int32(2))
        for place in range(3)
    )


def columns(start, size):
    return pl.ds(pl.multiple_of(start, 128), size)


class Links:
    def __init__(self, send_sems, recv_sems, load_sems):
        self.send_sems, self.recv_sems, self.load_sems = send_sems, recv_sems, load_sems
        self.used, self.loads, self.sent = 0, 0, []
        self.dp_index, self.seq_index = lax.axis_index("dp"), lax.axis_index("seq")

    def peer(self, dp_mask, seq_mask):
        return (flip(self.dp_index, dp_mask), flip(self.seq_index, seq_mask))

    def barrier(self):
        semaphore = pltpu.get_barrier_semaphore()
        masks = [(0, mask) for mask in range(2, 8)] + list(GROUP)
        for mask in masks:
            pl.semaphore_signal(
                semaphore, inc=1, device_id=self.peer(*mask), device_id_type=MESH
            )
        return lambda: pl.semaphore_wait(semaphore, len(masks))

    def send(self, source, target, dp_mask, seq_mask):
        number = self.used
        self.used += 1
        copy = pltpu.make_async_remote_copy(
            src_ref=source,
            dst_ref=target,
            send_sem=self.send_sems.at[number],
            recv_sem=self.recv_sems.at[number],
            device_id=self.peer(dp_mask, seq_mask),
            device_id_type=MESH,
        )
        copy.start()
        self.sent.append(copy)
        return copy

    def load(self, source, target):
        copy = pltpu.make_async_copy(source, target, self.load_sems.at[self.loads])
        self.loads += 1
        copy.start()
        return copy

    def settle(self, copy):
        copy.wait()
        self.sent = [other for other in self.sent if other is not copy]

    def sent_done(self, copies):
        for copy in copies:
            copy.wait_send()
        self.sent = [other for other in self.sent if not any(other is copy for copy in copies)]

    def drain(self):
        for copy in self.sent:
            copy.wait_send()


class Share:
    def __init__(self, links, slots, near, far):
        self.links, self.slots = links, slots
        self.across = links.send(near, slots.at[2], 2, 0)
        self.beside = links.send(far, slots.at[4], 0, 1)
        self.corner = links.send(far, slots.at[6], 2, 1)
        self.waits = [links.send(near, slots.at[1], 1, 0)]

    def forward(self):
        for copy, slot in ((self.across, 2), (self.beside, 4), (self.corner, 6)):
            copy.wait_recv()
            self.waits.append(
                self.links.send(self.slots.at[slot], self.slots.at[slot + 1], 1, 0)
            )

    def wait(self):
        arrived(self.waits)


def arrived(copies):
    for copy in copies:
        copy.wait_recv()


def turn_sine_cosine(angles):
    turns = jnp.floor(angles * (0.5 / math.pi) + 0.5)
    rest = angles - turns * 6.28125
    rest = rest - turns * (2.0 * math.pi - 6.28125)
    return jnp.sin(rest), jnp.cos(rest)


def utterance_ends(lengths_ref):
    ends, total = [], jnp.int32(0)
    for number in range(lengths_ref.shape[1]):
        total = total + lengths_ref[0, number]
        ends.append(total)
    return ends


def segments(ends, index):
    return sum((index >= end).astype(jnp.int32) for end in ends)


def rotary(ends, first_row, rows, width):
    index = first_row + lax.broadcasted_iota(jnp.int32, (rows, width), 0)
    start = jnp.zeros_like(index)
    for end in ends:
        start = jnp.where(index >= end, end, start)
    lane = lax.broadcasted_iota(jnp.int32, (rows, width), 1) % HEAD
    pair = (lane % (HEAD // 2)).astype(jnp.float32)
    angles = (index - start).astype(jnp.float32) * jnp.exp(
        pair * (-2.0 * math.log(10000.0) / HEAD)
    )
    sine, cosine = turn_sine_cosine(angles)
    return cosine, jnp.where(lane < HEAD // 2, -sine, sine)


def partner(values):
    half_size = HEAD // 2
    lane = lax.broadcasted_iota(jnp.int32, values.shape, 1) % HEAD
    return jnp.where(
        lane < half_size,
        pltpu.roll(values, values.shape[1] - half_size, 1),
        pltpu.roll(values, half_size, 1),
    )


def head_mask(values, head):
    lane = lax.broadcasted_iota(jnp.int32, values.shape, 1)
    return jnp.where(lane // HEAD == head, values, jnp.zeros_like(values))


def norm_parts(values):
    centered = values - jnp.mean(values, axis=-1, keepdims=True)
    variance = jnp.mean(centered * centered, axis=-1, keepdims=True)
    factor = lax.rsqrt(variance + 1e-06)
    return centered * factor, factor


def norm_back(grad, normal, factor):
    mean_grad = jnp.mean(grad, axis=-1, keepdims=True)
    mean_product = jnp.mean(grad * normal, axis=-1, keepdims=True)
    return factor * (grad - mean_grad - normal * mean_product)


def product(left, right):
    return jnp.dot(left, right, preferred_element_type=jnp.float32)


def product_cols(left, right):
    return lax.dot_general(left, right, contract_cols, preferred_element_type=jnp.float32)


def product_rows(left, right):
    return lax.dot_general(left, right, contract_rows, preferred_element_type=jnp.float32)


def gelu_parts(upper):
    square = upper * upper
    bent = jnp.tanh(ROOT * (upper + 0.044715 * upper * square))
    value = 0.5 * upper * (1.0 + bent)
    slope = 0.5 * (1.0 + bent) + 0.5 * upper * (1.0 - bent * bent) * ROOT * (
        1.0 + 3.0 * 0.044715 * square
    )
    return value, slope


class Sum:
    def __init__(self, links, left, right, total, into_a, into_b, place=None):
        self.links, self.left, self.right, self.total = links, left, right, total
        self.into_a, self.into_b, self.place = into_a, into_b, place
        self.size = total.shape[0] // 4

    def fill(self, low, high):
        depth = self.left.shape[0] * self.left.shape[1]

        def step(number, carried):
            start = pl.multiple_of(number * 256, 256)
            source = start if self.place is None else self.place(number)
            self.total[pl.ds(start, 256), :] = product_rows(
                self.left[:, :, columns(source, 256)].reshape(depth, 256),
                self.right[...].reshape(depth, self.right.shape[2]),
            ).astype(jnp.bfloat16)
            return carried

        lax.fori_loop(low // 256, high // 256, step, 0)

    def begin(self):
        self.fill(2 * self.size, 4 * self.size)
        self.copy = self.links.send(self.total.at[2 * self.size :], self.into_a, 0, 2)

    def keep(self):
        self.fill(0, 2 * self.size)

    def second(self):
        self.links.settle(self.copy)
        both = pl.ds(0, 2 * self.size)
        self.total[both, :] = (
            self.total[both, :].astype(jnp.float32) + self.into_a[...].astype(jnp.float32)
        ).astype(jnp.bfloat16)
        self.copy = self.links.send(
            self.total.at[self.size : 2 * self.size], self.into_b, 0, 6
        )

    def third(self):
        self.copy.wait_recv()
        self.ready = self.total.at[2 * self.size : 3 * self.size]
        self.ready[...] = (
            self.total[: self.size, :].astype(jnp.float32) + self.into_b[...].astype(jnp.float32)
        ).astype(jnp.bfloat16)

    def gather(self, ready, place):
        self.target = place
        own = place(self.links.dp_index)
        self.across = self.links.send(ready, own, 2, 0)
        self.core = self.links.send(ready, own, 1, 0)
        self.own = self.links.load(ready, own)

    def spread(self):
        self.across.wait_recv()
        other = self.target(flip(self.links.dp_index, 2))
        self.far = self.links.send(other, other, 1, 0)

    def finish(self):
        self.own.wait()
        arrived([self.core, self.far])


def layer_kernel(
    lengths, steps, frame_mask, frames, skip, cotangent, biases, w_skip, w_ada, w_qkv, w_out, w_up,
    w_down,
    result, grad_frames, grad_skip, sum_skip, sum_qkv, sum_out, sum_up, sum_down, small_all,
    embed_all,
    out_buf, up_buf, down_buf, weight_buf,
    joined_all, cot_all, first_all, attn_all, second_all, gated_all, upper_all, branch_all,
    packed_all, in_all,
    first_own, embed_own, masks, table, packed_send, packed, attn_send, attn_low,
    attn_sum, residual, scale, grad_gated, second_low, gated, upper_parts, residual_mid, normal_mid,
    grad_mid, branch, grad_heads, back_recv, grad_packed, grad_in, key_total,
    value_total, small, small_send, small_recv, up_ready,
    down_sum, down_a, down_b, up_sum, up_a, up_b, out_sum, out_a, out_b, qkv_sum, qkv_a, qkv_b,
    skip_sum, skip_a, skip_b,
    send_sems, recv_sems, load_sems,
):
    links = Links(send_sems, recv_sems, load_sems)
    seq_index, dp_index = links.seq_index, links.dp_index
    rows, width = frames.shape
    hidden = grad_gated.shape[1]
    float32, bfloat16 = jnp.float32, jnp.bfloat16
    odd = bit(seq_index, 0)
    enter = links.barrier()
    load_skip = links.load(w_skip, down_buf.at[: 2 * width])
    load_ada = links.load(w_ada, weight_buf)
    load_qkv = links.load(w_qkv, up_buf.at[:, : 3 * width])
    load_out = links.load(w_out, out_buf)
    load_down_high = links.load(w_down.at[2 * width :], down_buf.at[2 * width :])

    def relative(source, target, size):
        for number, mask in enumerate(RELATIVE):
            target[:, number * size : (number + 1) * size] = source(flip(seq_index, mask))

    def joined_block(place):
        inside = columns(lax.rem(place, jnp.int32(4)) * 256, 256)
        return jnp.where(place < 4, frames[:, inside], skip[:, inside])

    joined_own = grad_packed.at[:, width:]
    relative(joined_block, joined_own, 256)
    joined_all[0] = joined_own[:, :width]
    cot_all[0] = cotangent[...]
    masks[0] = jnp.broadcast_to(frame_mask[...], masks.shape[1:])
    ends = utterance_ends(lengths)
    utter = lax.broadcasted_iota(jnp.int32, embed_own.shape, 0)
    flow = jnp.zeros(embed_own.shape, float32)
    for number in range(steps.shape[1]):
        flow = jnp.where(utter == number, steps[0, number].astype(float32), flow)
    lane = lax.broadcasted_iota(jnp.int32, embed_own.shape, 1)
    half = width // 2
    frequency = jnp.exp((lane % half).astype(float32) * (-math.log(10000.0) / half))
    sine, cosine = turn_sine_cosine(1000.0 * (flow / TSTEPS) * frequency)
    embed = jnp.where(lane < half, sine, cosine)
    embed_own[...] = jnp.where(utter < steps.shape[1], embed, 0.0).astype(bfloat16)
    enter()
    mask_copies = [links.send(masks.at[0], masks.at[m], 0, m) for m in range(1, 8)]
    cot_share = Share(links, cot_all, cot_all.at[0], cot_all.at[0])
    load_skip.wait()
    residual[...] = product(frames[...], down_buf[:width]) + product(
        skip[...], down_buf[width : 2 * width]
    )
    load_down_low = links.load(w_down.at[: 2 * width], down_buf.at[: 2 * width])
    load_ada.wait()
    table[...] = product(embed_own[...], weight_buf[...]) + biases[:, : 2 * width].astype(float32)
    first_row = seq_index * rows
    normal, unused = norm_parts(residual[...])
    row_index = first_row + lax.broadcasted_iota(jnp.int32, (rows, 1), 0)
    own_segment = segments(ends, row_index)
    spread_scale = jnp.zeros((rows, width), float32)
    spread_shift = jnp.zeros((rows, width), float32)
    for number in range(len(ends)):
        member = own_segment == number
        spread_scale = jnp.where(member, table[number : number + 1, :width], spread_scale)
        spread_shift = jnp.where(member, table[number : number + 1, width:], spread_shift)
    scale[...] = spread_scale
    second_low[...] = (normal * (1.0 + spread_scale) + spread_shift).astype(bfloat16)
    cos_own, sin_own = rotary(ends, first_row, rows, 256)
    load_qkv.wait()
    packed_copies = []
    for far in (2, 1, 3, 0):
        pair = flip(lax.div(seq_index, jnp.int32(2)), far)
        parts = []
        for kind in range(3):
            part = product(second_low[...], up_buf[:, columns(kind * width + pair * 256, 256)])
            if kind < 2:
                part = part * cos_own + partner(part) * sin_own
            parts.append(part.astype(bfloat16))
        for side in range(2):
            for kind in range(3):
                packed_send[pair * 2 + side, :, kind * 128 : (kind + 1) * 128] = parts[kind][
                    :, side * 128 : (side + 1) * 128
                ]
        for mask in (2 * far, 2 * far + 1):
            if mask:
                packed_copies.append(
                    links.send(
                        packed_send.at[flip(seq_index, mask)], packed.at[seq_index], 0, mask
                    )
                )
    packed[seq_index] = packed_send[seq_index]
    load_up = links.load(w_up, up_buf)
    relative(lambda place: second_low[:, columns(place * 128, 128)], first_own, 128)
    first_all[0] = first_own[:, : width // 2]
    joined_share = Share(links, joined_all, joined_all.at[0], joined_own.at[:, width:])
    first_share = Share(links, first_all, first_all.at[0], first_own.at[:, width // 2 :])
    embed_copies = [links.send(embed_own, embed_all.at[dp_index], m, 0) for m in (1, 2, 3)]
    embed_load = links.load(embed_own, embed_all.at[dp_index])
    load_down_low.wait()
    load_down_high.wait()

    def gated_step(step, carried):
        part = columns(step * 512, 512)
        grad_gated[:, part] = product_cols(cotangent[...], down_buf[part, :])
        return carried

    lax.fori_loop(0, hidden // 512, gated_step, 0)
    cot_share.forward()
    arrived(mask_copies)
    arrived(packed_copies)
    key_index = lax.broadcasted_iota(jnp.int32, (1, 8 * rows), 1)
    key_segment = segments(ends, key_index)
    key_valid = jnp.concatenate(
        [masks[exclusive(seq_index, jnp.int32(number))][:1] for number in range(8)], axis=1
    )

    def attend(place):
        query = packed[place, :, :128]
        row_index = place * rows + lax.broadcasted_iota(jnp.int32, (rows, 1), 0)
        allowed = (segments(ends, row_index) == key_segment) & (
            (key_valid > 0) | (row_index == key_index)
        )
        keys = packed[:, :, 128:256].reshape(8 * rows, 128)
        values = packed[:, :, 256:].reshape(8 * rows, 128)
        total = jnp.zeros((rows, 128), float32)
        here = pl.ds(pl.multiple_of(place * rows, rows), rows)
        for head in range(2):
            scores = product_cols(head_mask(query, head), keys) * (1.0 / math.sqrt(HEAD))
            scores = jnp.where(allowed, scores, masked_score)
            raised = jnp.exp(scores - jnp.max(scores, axis=1, keepdims=True))
            low = (raised / jnp.sum(raised, axis=1, keepdims=True)).astype(bfloat16)
            weight_buf[here, head * 1024 : (head + 1) * 1024] = low
            total = total + product(low, head_mask(values, head))
        attn_sum[here, :] = total
        attn_send[place] = total.astype(bfloat16)

    base = links.used
    links.used += 8

    def attn_copy(mask):
        target = exclusive(seq_index, mask)
        return pltpu.make_async_remote_copy(
            src_ref=attn_send.at[target],
            dst_ref=attn_low.at[seq_index],
            send_sem=send_sems.at[base + mask],
            recv_sem=recv_sems.at[base + mask],
            device_id=(dp_index, target),
            device_id_type=MESH,
        )

    def attend_step(step, carried):
        mask = 7 - step
        attend(exclusive(seq_index, mask))
        attn_copy(mask).start()
        return carried

    lax.fori_loop(0, 7, attend_step, 0)
    attend(seq_index)
    attn_low[seq_index] = attn_send[seq_index]
    joined_share.forward()
    first_share.forward()
    load_out.wait()
    for mask in range(1, 8):
        attn_copy(jnp.int32(mask)).wait()
    joined_attn = jnp.concatenate([attn_low[number] for number in range(8)], axis=1)
    residual_mid[...] = residual[...] + product(joined_attn, out_buf[...])
    normal, factor_mid = norm_parts(residual_mid[...])
    normal_mid[...] = normal
    gain_float = biases[:, 7 * width : 8 * width].astype(float32)
    second_all[0] = (normal * gain_float).astype(bfloat16)
    second_share = Share(links, second_all, second_all.at[0], second_all.at[0])
    small[8:] = jnp.zeros((8, small.shape[1]), float32)
    load_up.wait()

    def up_step(step, carried):
        part = columns(step * 512, 512)
        upper = product(second_all[0], up_buf[:, part]) + biases[
            :, columns(2 * width + step * 512, 512)
        ].astype(float32)
        value, slope = gelu_parts(upper)
        grad_upper = (grad_gated[:, part] * slope).astype(bfloat16)
        gated[:, part] = value.astype(bfloat16)
        upper_parts[:, part] = grad_upper
        small[
            pl.ds(8 + lax.div(step, jnp.int32(4)), 1),
            columns(lax.rem(step, jnp.int32(4)) * 512, 512),
        ] = jnp.sum(grad_upper.astype(float32), axis=0, keepdims=True)
        return carried

    lax.fori_loop(0, hidden // 512, up_step, 0)

    def second_step(step, total):
        part = columns(step * 512, 512)
        return total + product_cols(upper_parts[:, part], up_buf[:, part])

    grad_second = lax.fori_loop(
        0, hidden // 512, second_step, jnp.zeros((rows, width), float32)
    )
    grad_out = cotangent[...].astype(float32)
    normal = normal_mid[...]
    small[10:11, :width] = jnp.sum(grad_second * normal, axis=0, keepdims=True)
    small[10:11, width:] = jnp.sum(grad_out, axis=0, keepdims=True)
    grad_mid[...] = grad_out + norm_back(grad_second * gain_float, normal, factor_mid)
    branch[...] = grad_mid[...].astype(bfloat16)
    grad_attn = product_cols(branch[...], out_buf[...]).astype(bfloat16)
    grad_send = attn_send
    for number in range(8):
        grad_send[number] = grad_attn[:, number * 128 : (number + 1) * 128]
    head_copies = [
        links.send(grad_send.at[flip(seq_index, m)], grad_heads.at[seq_index], 0, m)
        for m in FAR_FIRST
    ]
    grad_heads[seq_index] = grad_send[seq_index]

    def quarters(source, slots):
        size = slots.shape[2]
        slots[0] = source[:, columns(dp_index * size, size)]
        return [
            links.send(
                source.at[:, columns(flip(dp_index, m) * size, size)], slots.at[4 * v + m], m, v
            )
            for m, v in GROUP
        ]

    second_share.forward()
    branch_copies = quarters(branch, branch_all)
    attn_own = grad_packed.at[:, :width]
    relative(lambda place: attn_low[place], attn_own, 128)
    attn_all[0] = attn_own[:, : width // 2]
    attn_share = Share(links, attn_all, attn_all.at[0], attn_own.at[:, width // 2 :])

    def down_step(step, total):
        part = columns(step * 512, 512)
        return total + product(gated[:, part], down_buf[part, :])

    lower = lax.fori_loop(
        0,
        hidden // 512,
        down_step,
        residual_mid[...] + biases[:, 6 * width : 7 * width].astype(float32),
    )
    second_low[...] = lower.astype(bfloat16)
    out_loads = [links.load(second_low, result)]
    second_share.wait()
    cot_share.wait()
    for first in (0, 2):
        units, spots = [], []
        for number in (first, first + 1):
            place = flip(seq_index, RELATIVE[number])
            units.append(columns(place * 512 + dp_index * 128, 128))
            spots.append(lax.div(place, jnp.int32(2)))
        weight_up = jnp.concatenate([up_buf[:, unit] for unit in units], axis=1)
        weight_down = jnp.concatenate([down_buf[unit, :] for unit in units], axis=0)
        bias = jnp.concatenate(
            [
                biases[:, columns(2 * width + flip(seq_index, RELATIVE[number]) * 512 + dp_index * 128, 128)]
                for number in (first, first + 1)
            ],
            axis=1,
        ).astype(float32)

        def again_step(step, carried):
            both = pl.ds(2 * step, 2)
            upper = product(second_all[both].reshape(2 * rows, width), weight_up) + bias
            value, slope = gelu_parts(upper)
            grad = product_cols(cot_all[both].reshape(2 * rows, width), weight_down)
            gated_all[both, :, first * 128 : (first + 2) * 128] = value.astype(bfloat16).reshape(
                2, rows, 256
            )
            grad_upper = (grad * slope).astype(bfloat16).reshape(2, rows, 256)
            for side in range(2):
                upper_all[both, :, columns(spots[side] * 128, 128)] = grad_upper[
                    :, :, side * 128 : (side + 1) * 128
                ]
            return carried

        lax.fori_loop(0, 4, again_step, 0)
    load_qkv = links.load(w_qkv, up_buf.at[:, : 3 * width])
    load_skip = links.load(w_skip, down_buf.at[: 2 * width])

    def pair_place(number):
        base_pair = lax.div(seq_index, jnp.int32(2))
        step_a, step_b = lax.div(number, jnp.int32(2)), lax.rem(number, jnp.int32(2))
        two = jnp.int32(2)
        low_bit = lax.rem(bit(base_pair, 0) + step_a + step_b, two)
        high_bit = lax.rem(bit(base_pair, 1) + step_b, two)
        return (2 * high_bit + low_bit) * 256

    down = Sum(links, gated_all, cot_all, down_sum, down_a, down_b)
    up = Sum(links, second_all, upper_all, up_sum, up_a, up_b, pair_place)
    out = Sum(links, attn_all, branch_all, out_sum, out_a, out_b)
    qkv = Sum(links, first_all, packed_all, qkv_sum, qkv_a, qkv_b)
    skip_in = Sum(links, joined_all, in_all, skip_sum, skip_a, skip_b)
    down.begin()
    up.begin()
    arrived(head_copies)
    links.sent_done(packed_copies)
    back_send = packed_send
    shrink = 1.0 / math.sqrt(HEAD)
    key_total[...] = jnp.zeros_like(key_total)
    value_total[...] = jnp.zeros_like(value_total)

    def back_step(place, carried):
        here = pl.ds(pl.multiple_of(place * rows, rows), rows)
        grad = grad_heads[place]
        query = packed[place, :, :128]
        keys = packed[:, :, 128:256].reshape(8 * rows, 128)
        values = packed[:, :, 256:].reshape(8 * rows, 128)
        both = grad.astype(float32) * attn_sum[here, :]
        total = jnp.zeros((rows, 128), float32)
        for head in range(2):
            low = weight_buf[here, head * 1024 : (head + 1) * 1024]
            grad_head = head_mask(grad, head)
            delta = jnp.sum(head_mask(both, head), axis=1, keepdims=True)
            grad_scores = (
                low.astype(float32) * (product_cols(grad_head, values) - delta)
            ).astype(bfloat16)
            total = total + product(grad_scores, head_mask(keys, head))
            key_total[...] += product_rows(grad_scores, head_mask(query, head))
            value_total[...] += product_rows(low, grad_head)
        total = total * shrink
        cosine, sine = rotary(ends, place * rows, rows, 128)
        back_send[place, :, :128] = (total * cosine - partner(total) * sine).astype(bfloat16)
        return carried

    lax.fori_loop(0, 8, back_step, 0)

    def key_step(place, carried):
        here = pl.ds(pl.multiple_of(place * rows, rows), rows)
        total = key_total[here, :] * shrink
        cosine, sine = rotary(ends, place * rows, rows, 128)
        back_send[place, :, 128:256] = (total * cosine - partner(total) * sine).astype(bfloat16)
        back_send[place, :, 256:] = value_total[here, :].astype(bfloat16)
        return carried

    lax.fori_loop(0, 8, key_step, 0)
    back_copies = [
        links.send(back_send.at[flip(seq_index, m)], back_recv.at[seq_index], 0, m)
        for m in FAR_FIRST
    ]
    back_recv[seq_index] = back_send[seq_index]
    down.keep()
    up.keep()
    attn_share.forward()
    arrived(branch_copies)
    attn_share.wait()
    out.begin()
    out.keep()
    arrived(back_copies)
    for share in (joined_share, attn_share):
        links.sent_done([share.beside, share.corner])
    for number in range(8):
        for kind in range(3):
            grad_packed[:, kind * width + number * 128 : kind * width + (number + 1) * 128] = (
                back_recv[number, :, kind * 128 : (kind + 1) * 128]
            )
    packed_copies = quarters(grad_packed, packed_all)
    load_qkv.wait()

    def first_step(step, total):
        part = columns(step * 512, 512)
        return total + product_cols(grad_packed[:, part], up_buf[:, part])

    grad_first = lax.fori_loop(0, 6, first_step, jnp.zeros((rows, width), float32))
    normal, factor = norm_parts(residual[...])
    grad_in[...] = (
        grad_mid[...] + norm_back(grad_first * (1.0 + scale[...]), normal, factor)
    ).astype(bfloat16)
    in_copies = quarters(grad_in, in_all)
    scaled = grad_first * normal
    for number in range(len(ends)):
        member = own_segment == number
        small[number : number + 1, :width] = jnp.sum(
            jnp.where(member, scaled, 0.0), axis=0, keepdims=True
        )
        small[number : number + 1, width:] = jnp.sum(
            jnp.where(member, grad_first, 0.0), axis=0, keepdims=True
        )

    def small_start(number, mask):
        small_send[number] = small[...].astype(bfloat16)
        return links.send(small_send.at[number], small_recv.at[number], 0, mask)

    def small_add(copy, number):
        copy.wait_recv()
        small[...] = small_send[number].astype(float32) + small_recv[number].astype(float32)

    small_copy = small_start(0, 1)
    down.second()
    up.second()
    first_share.wait()
    arrived(packed_copies)
    qkv.begin()
    joined_share.wait()
    arrived(in_copies)
    skip_in.begin()
    small_add(small_copy, 0)
    small_copy = small_start(1, 2)
    out.second()
    qkv.keep()
    skip_in.keep()
    load_skip.wait()
    for held, target, start in ((residual, grad_frames, 0), (normal_mid, grad_skip, width)):
        held[...] = product_cols(grad_in[...], down_buf[start : start + width, :])
        out_loads.append(links.load(held, target))
    by_rows = lambda target, size: lambda index: target.at[pl.ds(index * size, size), :]
    by_cols = lambda target, size: lambda index: target.at[:, columns(index * size, size)]
    down.third()
    down.gather(down.ready, by_rows(sum_down, 128))
    up.third()
    up_ready[odd] = up.ready[pl.ds(pl.multiple_of(odd * 128, 128), 128), :]
    up_other = links.send(
        up.ready.at[pl.ds(pl.multiple_of((1 - odd) * 128, 128), 128), :], up_ready.at[odd], 0, 1
    )
    small_add(small_copy, 1)
    small_copy = small_start(2, 6)
    out.third()
    out.gather(out.ready, by_cols(sum_out, 256))
    up_other.wait_recv()
    up.gather(up_ready, lambda index: sum_up.at[index])
    qkv.second()
    skip_in.second()
    small_add(small_copy, 2)
    small_send[3] = small[...].astype(bfloat16)
    small_copies = [
        links.send(small_send.at[3], small_all.at[dp_index], m, 0) for m in (3, 2, 1)
    ]
    small_load = links.load(small_send.at[3], small_all.at[dp_index])
    down.spread()
    out.spread()
    up.spread()
    qkv.third()
    qkv.gather(qkv.ready, by_cols(sum_qkv, 768))
    skip_in.third()
    skip_in.gather(skip_in.ready, by_cols(sum_skip, 256))
    qkv.spread()
    skip_in.spread()
    small_load.wait()
    embed_load.wait()
    for load in out_loads:
        load.wait()
    arrived(small_copies + embed_copies)
    for each in (down, up, out, qkv, skip_in):
        each.finish()
    links.drain()


def widen_kernel(
    result_in, frames_in, skip_in, sum_skip, sum_qkv, sum_out, sum_up, sum_down, small_all, embed_all,
    result, grad_frames, grad_skip, out_skip, out_ada, out_ada_bias, out_qkv, out_out, out_gain,
    out_up, out_up_bias, out_down, out_down_bias,
    low_result, low_frames, low_skip, low_w_skip, low_qkv, low_out, low_up, low_down, low_small, low_embed,
    full_skip, full_ada, full_qkv, full_out, full_up, full_down, in_sems, out_sems,
):
    float32 = jnp.float32
    seq_index = lax.axis_index("seq")
    sources = (sum_up, sum_down, sum_qkv, sum_skip, small_all, embed_all, sum_out, result_in, frames_in, skip_in)
    inside = (low_up, low_down, low_qkv, low_w_skip, low_small, low_embed, low_out, low_result, low_frames, low_skip)
    loads = [
        pltpu.make_async_copy(source, target, in_sems.at[number])
        for number, (source, target) in enumerate(zip(sources, inside, strict=True))
    ]
    for load in loads:
        load.start()
    stores = []

    def store(source, target):
        copy = pltpu.make_async_copy(source, target, out_sems.at[len(stores)])
        copy.start()
        stores.append(copy)

    loads[0].wait()
    for quarter in range(4):
        for side in range(2):
            for level in range(4):
                start = (2 * level + side) * 512 + quarter * 128
                full_up[:, start : start + 128] = low_up[
                    quarter, side, :, level * 128 : (level + 1) * 128
                ].astype(float32)
    store(full_up, out_up)
    for number, low, full, out in (
        (1, low_down, full_down, out_down),
        (2, low_qkv, full_qkv, out_qkv),
        (3, low_w_skip, full_skip, out_skip),
    ):
        loads[number].wait()
        full[...] = low[...].astype(float32)
        store(full, out)
    loads[4].wait()
    loads[5].wait()
    size = full_ada.shape[0]
    own = low_embed[:, :, columns(seq_index * size, size)].reshape(-1, size)
    full_ada[...] = product_rows(own, low_small[...].reshape(own.shape[0], full_ada.shape[1]))
    store(full_ada, out_ada)
    loads[6].wait()
    full_out[...] = low_out[...].astype(float32)
    store(full_out, out_out)
    for number, low, out in ((7, low_result, result), (8, low_frames, grad_frames), (9, low_skip, grad_skip)):
        loads[number].wait()
        store(low, out)
    wide = low_small.shape[2]
    spot = columns(seq_index * 256, 256)
    bias = jnp.zeros((1, 256), float32)
    for number in range(4):
        bias = bias + jnp.sum(low_small[number, :8, spot].astype(float32), axis=0, keepdims=True)
    out_ada_bias[...] = bias
    upper = jnp.zeros((1, 512), float32)
    gain = jnp.zeros((1, 128), float32)
    down_bias = jnp.zeros((1, 128), float32)
    high = lax.div(seq_index, jnp.int32(4))
    for number in range(4):
        both = low_small[number, 8:, columns(lax.rem(seq_index, jnp.int32(4)) * 512, 512)].astype(float32)
        upper = upper + jnp.where(high == 0, both[:1], both[1:2])
        gain = gain + low_small[number, 8:, columns(seq_index * 128, 128)].astype(float32)[2:3]
        down_bias = down_bias + low_small[number, 8:, columns(wide // 2 + seq_index * 128, 128)].astype(float32)[2:3]
    out_up_bias[...] = upper
    out_gain[...] = gain
    out_down_bias[...] = down_bias
    for copy in stores:
        copy.wait()


def one_kernel(
    frames, skip, lengths, frame_mask, time_step, w_skip, w_ada, b_ada, w_qkv, w_out, norm_gain,
    w_up, b_up, w_down, b_down, cotangent,
):
    rows, width = frames.shape[1:]
    hidden = b_up.shape[0]
    float32, bfloat16 = jnp.float32, jnp.bfloat16
    shape = jax.ShapeDtypeStruct
    vmem = pl.BlockSpec(memory_space=pltpu.VMEM)
    smem = pl.BlockSpec(memory_space=pltpu.SMEM)
    anywhere = pl.BlockSpec(memory_space=pl.ANY)
    dma = pltpu.SemaphoreType.DMA
    low = lambda *size: pltpu.VMEM(size, bfloat16)
    full = lambda *size: pltpu.VMEM(size, float32)
    biases = jnp.concatenate([b_ada, b_up, b_down, norm_gain])[None]
    sums = ((512, 1024), (1024, 512), (512, 256), (512, 768), (1024, 256))
    sum_scratch = [low(tall // part, wide) for tall, wide in sums for part in (1, 2, 4)]
    outs = (
        (shape((rows, width), bfloat16), anywhere),
        (shape((rows, width), float32), anywhere),
        (shape((rows, width), float32), anywhere),
        (shape((2 * width // 8, width), bfloat16), anywhere),
        (shape((width // 8, 3 * width), bfloat16), anywhere),
        (shape((width // 8, width), bfloat16), anywhere),
        (shape((4, 2, width // 8, hidden // 8), bfloat16), anywhere),
        (shape((hidden // 8, width), bfloat16), anywhere),
        (shape((4, 16, 2 * width), bfloat16), anywhere),
        (shape((4, 16, width), bfloat16), anywhere),
    )
    parts = pl.pallas_call(
        layer_kernel,
        out_shape=tuple(item[0] for item in outs),
        in_specs=[smem, smem] + [vmem] * 5 + [anywhere] * 6,
        out_specs=tuple(item[1] for item in outs),
        scratch_shapes=[
            low(*w_out.shape), low(*w_up.shape), low(*w_down.shape), low(8 * rows, 2 * width),
            low(8, rows, width), low(8, rows, width), low(8, rows, width // 2), low(8, rows, width // 2),
            low(8, rows, width), low(8, rows, 512), low(8, rows, 512), low(8, rows, 256),
            low(8, rows, 768), low(8, rows, 256),
            low(rows, width), low(16, width), pltpu.VMEM((8, 8, rows), jnp.int32),
            full(16, 2 * width), low(8, rows, 384), low(8, rows, 384), low(8, rows, 128), low(8, rows, 128),
            full(8 * rows, 128), full(rows, width), full(rows, width), full(rows, hidden), low(rows, width),
            low(rows, hidden), low(rows, hidden), full(rows, width), full(rows, width),
            full(rows, width), low(rows, width), low(8, rows, 128), low(8, rows, 384), low(rows, 3 * width), low(rows, width), full(8 * rows, 128),
            full(8 * rows, 128), full(16, 2 * width), low(4, 16, 2 * width), low(3, 16, 2 * width),
            low(2, rows, 512),
            *sum_scratch,
            dma((128,)), dma((128,)), dma((24,)),
        ],
        compiler_params=pltpu.CompilerParams(
            collective_id=0, has_side_effects=True, vmem_limit_bytes=60 * MIB
        ),
        name="layer",
    )(
        lengths, time_step, frame_mask, frames[0], skip[0], cotangent[0], biases, w_skip, w_ada,
        w_qkv, w_out, w_up, w_down,
    )

    last_outs = (
        (shape((rows, width), bfloat16), anywhere),
        (shape((rows, width), float32), anywhere),
        (shape((rows, width), float32), anywhere),
        (shape((2 * width // 8, width), float32), anywhere),
        (shape((width // 8, 2 * width), float32), anywhere),
        (shape((1, 2 * width // 8), float32), vmem),
        (shape((width // 8, 3 * width), float32), anywhere),
        (shape((width // 8, width), float32), anywhere),
        (shape((1, width // 8), float32), vmem),
        (shape((width // 8, hidden), float32), anywhere),
        (shape((1, hidden // 8), float32), vmem),
        (shape((hidden // 8, width), float32), anywhere),
        (shape((1, width // 8), float32), vmem),
    )
    scratch = [pltpu.VMEM(item[0].shape, item[0].dtype) for item in outs]
    scratch += [full(*last_outs[number][0].shape) for number in (3, 4, 6, 7, 9, 11)]
    widened = pl.pallas_call(
        widen_kernel,
        out_shape=tuple(item[0] for item in last_outs),
        in_specs=[pl.BlockSpec(memory_space=pltpu.HBM)] * len(outs),
        out_specs=tuple(item[1] for item in last_outs),
        scratch_shapes=[*scratch, dma((10,)), dma((12,))],
        compiler_params=pltpu.CompilerParams(vmem_limit_bytes=40 * MIB),
        name="widen",
    )(*parts)
    return tuple(
        item[None] if number < 3 else item.reshape(-1) if item.shape[0] == 1 else item
        for number, item in enumerate(widened)
    )


def solution(mesh):
    placed = (
        P("dp", "seq", None),
        P("dp", "seq", None),
        P("dp", None),
        P("dp", "seq"),
        P("dp", None),
        P(),
        P(),
        P(),
        P(),
        P(),
        P(),
        P(),
        P(),
        P(),
        P(),
        P("dp", "seq", None),
    )
    split_heads = mesh.shape["dp"] == 4 and mesh.shape["seq"] == len(RELATIVE)
    return jax.shard_map(
        one_kernel if split_heads else on_device,
        mesh=mesh,
        in_specs=placed,
        out_specs=(
            P("dp", "seq", None),
            P("dp", "seq", None),
            P("dp", "seq", None),
            P("seq", None),
            P("seq", None),
            P("seq"),
            P("seq", None),
            P("seq", None),
            P("seq"),
            P("seq", None),
            P("seq"),
            P("seq", None),
            P("seq"),
        ),
        check_vma=False,
    )
```

```python
import math

import jax
import jax.numpy as jnp
from jax import lax
from jax.experimental import pallas as pl
from jax.experimental.pallas import tpu as pltpu
from jax.sharding import PartitionSpec as P

HEADS = 16
HEAD = 64
TSTEPS = 32


precise = lax.Precision.HIGHEST
masked_score = -1e30
contract_rows = (((0,), (0,)), ((), ()))
contract_cols = (((1,), (1,)), ((), ()))


def divisor_below(count_all, upper_limit):
    size_now = min(count_all, upper_limit)
    while count_all % size_now:
        size_now -= 1
    return size_now


def normalize(values):
    centered = values - jnp.mean(values, axis=-1, keepdims=True)
    variance = jnp.mean(centered * centered, axis=-1, keepdims=True)
    return centered * lax.rsqrt(variance + 1e-06)


def segment_of(lengths, frame_index):
    utter_ends = jnp.cumsum(lengths)
    return jnp.sum((frame_index[:, None] >= utter_ends[None, :]).astype(jnp.int32), axis=1)


def utterance_layout(lengths, frame_index):
    utter_ends = jnp.cumsum(lengths)
    starts = utter_ends - lengths
    segment = segment_of(lengths, frame_index)
    member = segment[:, None] == jnp.arange(lengths.shape[0], dtype=jnp.int32)[None, :]
    position = frame_index - jnp.sum(jnp.where(member, starts[None, :], 0), axis=1)
    return (segment, position, member)


def rotary_tables(position, head_size):
    half_size = head_size // 2
    frequency = jnp.exp(
        jnp.arange(half_size, dtype=jnp.float32) * (-2.0 * math.log(10000.0) / head_size)
    )
    angles = position.astype(jnp.float32)[:, None] * frequency[None, :]
    return (jnp.cos(angles)[:, None, :], jnp.sin(angles)[:, None, :])


def rotate(values, cos_table, sin_table):
    half_size = values.shape[-1] // 2
    first_half = values[..., :half_size]
    second_half = values[..., half_size:]
    return jnp.concatenate(
        [
            first_half * cos_table - second_half * sin_table,
            second_half * cos_table + first_half * sin_table,
        ],
        axis=-1,
    )


def rotate_back(values, cos_table, sin_table):
    half_size = values.shape[-1] // 2
    first_half = values[..., :half_size]
    second_half = values[..., half_size:]
    return jnp.concatenate(
        [
            first_half * cos_table + second_half * sin_table,
            second_half * cos_table - first_half * sin_table,
        ],
        axis=-1,
    )


def time_embedding(steps, model_width):
    half_size = model_width // 2
    flow_time = steps.astype(jnp.float32) / TSTEPS
    frequency = jnp.exp(jnp.arange(half_size, dtype=jnp.float32) * (-math.log(10000.0) / half_size))
    angles = 1000.0 * flow_time[:, None] * frequency[None, :]
    return jnp.concatenate([jnp.sin(angles), jnp.cos(angles)], axis=1)


def make_attend(query_low, query_segment, query_index, lengths):
    count_rows, head_count, head_size = query_low.shape
    scale_factor = 1.0 / math.sqrt(head_size)

    def attend(running, key_piece, first_row):
        keys_part, values_part, valid_part = key_piece
        count_keys = keys_part.shape[0]
        block_rows = divisor_below(count_keys, 1024)
        block_count = count_keys // block_rows
        key_blocks = keys_part.reshape(block_count, block_rows, head_count, head_size)
        value_blocks = values_part.reshape(block_count, block_rows, head_count, head_size)
        valid_blocks = valid_part.reshape(block_count, block_rows)
        offsets = first_row + jnp.arange(block_count, dtype=jnp.int32) * block_rows

        def attend_block_step(carried, inputs):
            row_top, row_total, weighted = carried
            key_block, value_block, valid_block, offset = inputs
            key_index = offset + jnp.arange(block_rows, dtype=jnp.int32)
            key_segment = segment_of(lengths, key_index)
            allowed = (query_segment[:, None] == key_segment[None, :]) & (
                (valid_block[None, :] > 0) | (query_index[:, None] == key_index[None, :])
            )
            scores = (
                jnp.einsum("qhd,khd->hqk", query_low, key_block, preferred_element_type=jnp.float32)
                * scale_factor
            )
            scores = jnp.where(allowed[None], scores, masked_score)
            new_top = jnp.maximum(row_top, jnp.max(scores, axis=2))
            weights = jnp.where(allowed[None], jnp.exp(scores - new_top[:, :, None]), 0.0)
            factor = jnp.exp(row_top - new_top)
            row_total = row_total * factor + jnp.sum(weights, axis=2)
            weighted = weighted * jnp.transpose(factor)[:, :, None] + jnp.einsum(
                "hqk,khd->qhd",
                weights.astype(jnp.bfloat16),
                value_block,
                preferred_element_type=jnp.float32,
            )
            return ((new_top, row_total, weighted), None)

        result_state, unused = lax.scan(
            attend_block_step, running, (key_blocks, value_blocks, valid_blocks, offsets)
        )
        return result_state

    return attend


def key_sweep(
    query_low, grad_attn, log_total, row_delta, query_segment, query_index, lengths, key_tuple
):
    keys_all, values_all, valid_all = key_tuple
    count_rows, head_count, head_size = query_low.shape
    scale_factor = 1.0 / math.sqrt(head_size)
    count_keys = keys_all.shape[0]
    block_rows = divisor_below(count_keys, 1024)
    block_count = count_keys // block_rows
    key_blocks = keys_all.reshape(block_count, block_rows, head_count, head_size)
    value_blocks = values_all.reshape(block_count, block_rows, head_count, head_size)
    valid_blocks = valid_all.reshape(block_count, block_rows)
    offsets = jnp.arange(block_count, dtype=jnp.int32) * block_rows
    top_shift = jnp.transpose(log_total)[:, :, None]
    delta_shift = jnp.transpose(row_delta)[:, :, None]

    def key_block_step(grad_query, inputs):
        key_block, value_block, valid_block, offset = inputs
        key_index = offset + jnp.arange(block_rows, dtype=jnp.int32)
        key_segment = segment_of(lengths, key_index)
        allowed = (query_segment[:, None] == key_segment[None, :]) & (
            (valid_block[None, :] > 0) | (query_index[:, None] == key_index[None, :])
        )
        scores = (
            jnp.einsum("qhd,khd->hqk", query_low, key_block, preferred_element_type=jnp.float32)
            * scale_factor
        )
        weights = jnp.where(allowed[None], jnp.exp(scores - top_shift), 0.0)
        grad_weights = jnp.einsum(
            "qhd,khd->hqk", grad_attn, value_block, preferred_element_type=jnp.float32
        )
        grad_scores = (weights * (grad_weights - delta_shift)).astype(jnp.bfloat16)
        grad_query = (
            grad_query
            + jnp.einsum("hqk,khd->qhd", grad_scores, key_block, preferred_element_type=jnp.float32)
            * scale_factor
        )
        grad_key = (
            jnp.einsum("hqk,qhd->khd", grad_scores, query_low, preferred_element_type=jnp.float32)
            * scale_factor
        )
        grad_value = jnp.einsum(
            "hqk,qhd->khd",
            weights.astype(jnp.bfloat16),
            grad_attn,
            preferred_element_type=jnp.float32,
        )
        return (grad_query, (grad_key, grad_value))

    start_grad = jnp.zeros((count_rows, head_count, head_size), jnp.float32)
    return lax.scan(key_block_step, start_grad, (key_blocks, value_blocks, valid_blocks, offsets))


def on_device(
    frames,
    skip,
    lengths,
    frame_mask,
    time_step,
    w_skip,
    w_ada,
    b_ada,
    w_qkv,
    w_out,
    norm_gain,
    w_up,
    b_up,
    w_down,
    b_down,
    cotangent,
):
    local_frames = frames[0]
    local_skip = skip[0]
    row_lengths = lengths[0]
    count_rows, model_width = local_frames.shape
    head_count = HEADS
    head_size = HEAD
    row_base = lax.axis_index("seq") * count_rows
    frame_index = row_base + jnp.arange(count_rows, dtype=jnp.int32)
    segment, position, member = utterance_layout(row_lengths, frame_index)
    member_float = member.astype(jnp.float32)
    embed_low = time_embedding(time_step[0], model_width).astype(jnp.bfloat16)
    ada_table = jnp.dot(embed_low, w_ada, preferred_element_type=jnp.float32) + b_ada.astype(
        jnp.float32
    )
    ada_frame = jnp.dot(member_float, ada_table, precision=precise)
    scale_part = ada_frame[:, :model_width]
    shift_part = ada_frame[:, model_width:]
    joined = jnp.concatenate([local_frames, local_skip], axis=1)
    residual_in = jnp.dot(joined, w_skip, preferred_element_type=jnp.float32)
    norm_first, first_pull = jax.vjp(normalize, residual_in)
    first_low = (norm_first * (1.0 + scale_part) + shift_part).astype(jnp.bfloat16)
    packed = jnp.dot(first_low, w_qkv, preferred_element_type=jnp.float32)
    cos_table, sin_table = rotary_tables(position, head_size)
    query_low = rotate(
        packed[:, :model_width].reshape(count_rows, head_count, head_size), cos_table, sin_table
    ).astype(jnp.bfloat16)
    keys_low = (
        rotate(
            packed[:, model_width : 2 * model_width].reshape(count_rows, head_count, head_size),
            cos_table,
            sin_table,
        )
        .astype(jnp.bfloat16)
        .reshape(count_rows, model_width)
    )
    values_low = packed[:, 2 * model_width :].astype(jnp.bfloat16)
    valid_low = frame_mask[0].astype(jnp.bfloat16)
    attend = make_attend(query_low, segment, frame_index, row_lengths)
    start_state = (
        jnp.full((head_count, count_rows), masked_score, jnp.float32),
        jnp.zeros((head_count, count_rows), jnp.float32),
        jnp.zeros((count_rows, head_count, head_size), jnp.float32),
    )
    gathered = (
        lax.all_gather(keys_low, "seq", axis=0, tiled=True),
        lax.all_gather(values_low, "seq", axis=0, tiled=True),
        lax.all_gather(valid_low, "seq", axis=0, tiled=True),
    )
    row_top, row_total, weighted = attend(start_state, gathered, 0)
    attn_sum = weighted / jnp.transpose(row_total)[:, :, None]
    log_total = jnp.transpose(row_top + jnp.log(row_total))
    attn_low = attn_sum.reshape(count_rows, model_width).astype(jnp.bfloat16)
    residual_mid = residual_in + jnp.dot(attn_low, w_out, preferred_element_type=jnp.float32)
    gain_float = norm_gain.astype(jnp.float32)
    second_float, second_pull = jax.vjp(
        lambda hidden, gain_vector: normalize(hidden) * gain_vector, residual_mid, gain_float
    )
    second_low = second_float.astype(jnp.bfloat16)
    upper_sum = jnp.dot(second_low, w_up, preferred_element_type=jnp.float32) + b_up.astype(
        jnp.float32
    )
    gated_float, gelu_pull = jax.vjp(
        lambda hidden: jax.nn.gelu(hidden, approximate=True), upper_sum
    )
    gated_low = gated_float.astype(jnp.bfloat16)
    output = (
        residual_mid
        + jnp.dot(gated_low, w_down, preferred_element_type=jnp.float32)
        + b_down.astype(jnp.float32)
    )
    grad_out = cotangent[0]
    grad_out_float = grad_out.astype(jnp.float32)
    grad_down = lax.dot_general(
        gated_low, grad_out, contract_rows, preferred_element_type=jnp.float32
    )
    grad_down_bias = jnp.sum(grad_out_float, axis=0)
    grad_gated = lax.dot_general(
        grad_out, w_down, contract_cols, preferred_element_type=jnp.float32
    )
    grad_upper = gelu_pull(grad_gated)[0].astype(jnp.bfloat16)
    grad_up = lax.dot_general(
        second_low, grad_upper, contract_rows, preferred_element_type=jnp.float32
    )
    grad_up_bias = jnp.sum(grad_upper.astype(jnp.float32), axis=0)
    grad_second = lax.dot_general(
        grad_upper, w_up, contract_cols, preferred_element_type=jnp.float32
    )
    grad_mid_norm, grad_gain = second_pull(grad_second)
    grad_mid = grad_out_float + grad_mid_norm
    grad_branch = grad_mid.astype(jnp.bfloat16)
    grad_out_weight = lax.dot_general(
        attn_low, grad_branch, contract_rows, preferred_element_type=jnp.float32
    )
    grad_attn = (
        lax.dot_general(grad_branch, w_out, contract_cols, preferred_element_type=jnp.float32)
        .astype(jnp.bfloat16)
        .reshape(count_rows, head_count, head_size)
    )
    row_delta = jnp.sum(grad_attn.astype(jnp.float32) * attn_sum, axis=2)
    grad_query, key_parts = key_sweep(
        query_low, grad_attn, log_total, row_delta, segment, frame_index, row_lengths, gathered
    )
    grad_key_all, grad_value_all = key_parts
    total_keys = grad_key_all.shape[0] * grad_key_all.shape[1]
    grad_key, grad_value = (
        lax.psum_scatter(
            grad_key_all.reshape(total_keys, model_width), "seq", scatter_dimension=0, tiled=True
        ),
        lax.psum_scatter(
            grad_value_all.reshape(total_keys, model_width), "seq", scatter_dimension=0, tiled=True
        ),
    )
    grad_key = rotate_back(
        grad_key.reshape(count_rows, head_count, head_size), cos_table, sin_table
    ).reshape(count_rows, model_width)
    grad_query = rotate_back(grad_query, cos_table, sin_table).reshape(count_rows, model_width)
    grad_packed = jnp.concatenate([grad_query, grad_key, grad_value], axis=1).astype(jnp.bfloat16)
    grad_qkv = lax.dot_general(
        first_low, grad_packed, contract_rows, preferred_element_type=jnp.float32
    )
    grad_first = lax.dot_general(
        grad_packed, w_qkv, contract_cols, preferred_element_type=jnp.float32
    )
    grad_ada_frame = jnp.concatenate([grad_first * norm_first, grad_first], axis=1)
    grad_ada_table = lax.dot_general(member_float, grad_ada_frame, contract_rows, precision=precise)
    grad_ada = lax.dot_general(
        embed_low.astype(jnp.float32), grad_ada_table, contract_rows, precision=precise
    )
    grad_ada_bias = jnp.sum(grad_ada_table, axis=0)
    grad_in = (grad_mid + first_pull(grad_first * (1.0 + scale_part))[0]).astype(jnp.bfloat16)
    grad_skip_weight = lax.dot_general(
        joined, grad_in, contract_rows, preferred_element_type=jnp.float32
    )
    grad_joined = lax.dot_general(
        grad_in, w_skip, contract_cols, preferred_element_type=jnp.float32
    )
    (
        share_skip,
        share_ada,
        share_ada_bias,
        share_qkv,
        share_out,
        share_gain,
        share_up,
        share_up_bias,
        share_down,
        share_down_bias,
    ) = (
        lax.psum_scatter(grad_skip_weight, "seq", scatter_dimension=0, tiled=True),
        lax.psum_scatter(grad_ada, "seq", scatter_dimension=0, tiled=True),
        lax.psum_scatter(grad_ada_bias, "seq", scatter_dimension=0, tiled=True),
        lax.psum_scatter(grad_qkv, "seq", scatter_dimension=0, tiled=True),
        lax.psum_scatter(grad_out_weight, "seq", scatter_dimension=0, tiled=True),
        lax.psum_scatter(grad_gain, "seq", scatter_dimension=0, tiled=True),
        lax.psum_scatter(grad_up, "seq", scatter_dimension=0, tiled=True),
        lax.psum_scatter(grad_up_bias, "seq", scatter_dimension=0, tiled=True),
        lax.psum_scatter(grad_down, "seq", scatter_dimension=0, tiled=True),
        lax.psum_scatter(grad_down_bias, "seq", scatter_dimension=0, tiled=True),
    )
    (
        total_skip,
        total_ada,
        total_ada_bias,
        total_qkv,
        total_out,
        total_gain,
        total_up,
        total_up_bias,
        total_down,
        total_down_bias,
    ) = (
        lax.psum(share_skip.astype(jnp.bfloat16), "dp").astype(jnp.float32),
        lax.psum(share_ada.astype(jnp.bfloat16), "dp").astype(jnp.float32),
        lax.psum(share_ada_bias.astype(jnp.bfloat16), "dp").astype(jnp.float32),
        lax.psum(share_qkv.astype(jnp.bfloat16), "dp").astype(jnp.float32),
        lax.psum(share_out.astype(jnp.bfloat16), "dp").astype(jnp.float32),
        lax.psum(share_gain.astype(jnp.bfloat16), "dp").astype(jnp.float32),
        lax.psum(share_up.astype(jnp.bfloat16), "dp").astype(jnp.float32),
        lax.psum(share_up_bias.astype(jnp.bfloat16), "dp").astype(jnp.float32),
        lax.psum(share_down.astype(jnp.bfloat16), "dp").astype(jnp.float32),
        lax.psum(share_down_bias.astype(jnp.bfloat16), "dp").astype(jnp.float32),
    )
    return (
        output.astype(jnp.bfloat16)[None],
        grad_joined[:, :model_width][None],
        grad_joined[:, model_width:][None],
        total_skip,
        total_ada,
        total_ada_bias,
        total_qkv,
        total_out,
        total_gain,
        total_up,
        total_up_bias,
        total_down,
        total_down_bias,
    )


RELATIVE = (0, 6, 2, 4, 1, 7, 3, 5)
PAIRS = (0, 3, 1, 2)
MESH = pl.DeviceIdType.MESH
MIB = 2**20
FAR_FIRST = (4, 5, 2, 3, 6, 7, 1)
GROUP = ((2, 0), (0, 1), (2, 1), (3, 0), (3, 1), (1, 1), (1, 0))
ROOT = math.sqrt(2.0 / math.pi)


def bit(value, place):
    return lax.rem(lax.div(value, jnp.int32(1 << place)), jnp.int32(2))


def flip(value, mask):
    out = value
    for place in range(3):
        if (mask >> place) & 1:
            out = out + (1 << place) * (1 - 2 * bit(value, place))
    return out


def exclusive(value, other):
    return sum(
        (1 << place) * lax.rem(bit(value, place) + bit(other, place), jnp.int32(2))
        for place in range(3)
    )


def columns(start, size):
    return pl.ds(pl.multiple_of(start, 128), size)


class Links:
    def __init__(self, send_sems, recv_sems, load_sems):
        self.send_sems, self.recv_sems, self.load_sems = send_sems, recv_sems, load_sems
        self.used, self.loads, self.sent = 0, 0, []
        self.dp_index, self.seq_index = lax.axis_index("dp"), lax.axis_index("seq")

    def peer(self, dp_mask, seq_mask):
        return (flip(self.dp_index, dp_mask), flip(self.seq_index, seq_mask))

    def barrier(self):
        semaphore = pltpu.get_barrier_semaphore()
        masks = [(0, mask) for mask in range(2, 8)] + list(GROUP)
        for mask in masks:
            pl.semaphore_signal(
                semaphore, inc=1, device_id=self.peer(*mask), device_id_type=MESH
            )
        return lambda: pl.semaphore_wait(semaphore, len(masks))

    def send(self, source, target, dp_mask, seq_mask):
        number = self.used
        self.used += 1
        copy = pltpu.make_async_remote_copy(
            src_ref=source,
            dst_ref=target,
            send_sem=self.send_sems.at[number],
            recv_sem=self.recv_sems.at[number],
            device_id=self.peer(dp_mask, seq_mask),
            device_id_type=MESH,
        )
        copy.start()
        self.sent.append(copy)
        return copy

    def load(self, source, target):
        copy = pltpu.make_async_copy(source, target, self.load_sems.at[self.loads])
        self.loads += 1
        copy.start()
        return copy

    def settle(self, copy):
        copy.wait()
        self.sent = [other for other in self.sent if other is not copy]

    def sent_done(self, copies):
        for copy in copies:
            copy.wait_send()
        self.sent = [other for other in self.sent if not any(other is copy for copy in copies)]

    def drain(self):
        for copy in self.sent:
            copy.wait_send()


class Share:
    def __init__(self, links, slots, near, far):
        self.links, self.slots = links, slots
        self.across = links.send(near, slots.at[2], 2, 0)
        self.beside = links.send(far, slots.at[4], 0, 1)
        self.corner = links.send(far, slots.at[6], 2, 1)
        self.waits = [links.send(near, slots.at[1], 1, 0)]

    def forward(self):
        for copy, slot in ((self.across, 2), (self.beside, 4), (self.corner, 6)):
            copy.wait_recv()
            self.waits.append(
                self.links.send(self.slots.at[slot], self.slots.at[slot + 1], 1, 0)
            )

    def wait(self):
        arrived(self.waits)


def arrived(copies):
    for copy in copies:
        copy.wait_recv()


def turn_sine_cosine(angles):
    turns = jnp.floor(angles * (0.5 / math.pi) + 0.5)
    rest = angles - turns * 6.28125
    rest = rest - turns * (2.0 * math.pi - 6.28125)
    return jnp.sin(rest), jnp.cos(rest)


def utterance_ends(lengths_ref):
    ends, total = [], jnp.int32(0)
    for number in range(lengths_ref.shape[1]):
        total = total + lengths_ref[0, number]
        ends.append(total)
    return ends


def segments(ends, index):
    return sum((index >= end).astype(jnp.int32) for end in ends)


def rotary(ends, first_row, rows, width):
    index = first_row + lax.broadcasted_iota(jnp.int32, (rows, width), 0)
    start = jnp.zeros_like(index)
    for end in ends:
        start = jnp.where(index >= end, end, start)
    lane = lax.broadcasted_iota(jnp.int32, (rows, width), 1) % HEAD
    pair = (lane % (HEAD // 2)).astype(jnp.float32)
    angles = (index - start).astype(jnp.float32) * jnp.exp(
        pair * (-2.0 * math.log(10000.0) / HEAD)
    )
    sine, cosine = turn_sine_cosine(angles)
    return cosine, jnp.where(lane < HEAD // 2, -sine, sine)


def partner(values):
    half_size = HEAD // 2
    lane = lax.broadcasted_iota(jnp.int32, values.shape, 1) % HEAD
    return jnp.where(
        lane < half_size,
        pltpu.roll(values, values.shape[1] - half_size, 1),
        pltpu.roll(values, half_size, 1),
    )


def head_mask(values, head):
    lane = lax.broadcasted_iota(jnp.int32, values.shape, 1)
    return jnp.where(lane // HEAD == head, values, jnp.zeros_like(values))


def norm_parts(values):
    centered = values - jnp.mean(values, axis=-1, keepdims=True)
    variance = jnp.mean(centered * centered, axis=-1, keepdims=True)
    factor = lax.rsqrt(variance + 1e-06)
    return centered * factor, factor


def norm_back(grad, normal, factor):
    mean_grad = jnp.mean(grad, axis=-1, keepdims=True)
    mean_product = jnp.mean(grad * normal, axis=-1, keepdims=True)
    return factor * (grad - mean_grad - normal * mean_product)


def product(left, right):
    return jnp.dot(left, right, preferred_element_type=jnp.float32)


def product_cols(left, right):
    return lax.dot_general(left, right, contract_cols, preferred_element_type=jnp.float32)


def product_rows(left, right):
    return lax.dot_general(left, right, contract_rows, preferred_element_type=jnp.float32)


def gelu_parts(upper):
    square = upper * upper
    bent = jnp.tanh(ROOT * (upper + 0.044715 * upper * square))
    value = 0.5 * upper * (1.0 + bent)
    slope = 0.5 * (1.0 + bent) + 0.5 * upper * (1.0 - bent * bent) * ROOT * (
        1.0 + 3.0 * 0.044715 * square
    )
    return value, slope


class Sum:
    def __init__(self, links, left, right, total, into_a, into_b, place=None):
        self.links, self.left, self.right, self.total = links, left, right, total
        self.into_a, self.into_b, self.place = into_a, into_b, place
        self.size = total.shape[0] // 4

    def fill(self, low, high):
        depth = self.left.shape[0] * self.left.shape[1]

        def step(number, carried):
            start = pl.multiple_of(number * 256, 256)
            source = start if self.place is None else self.place(number)
            self.total[pl.ds(start, 256), :] = product_rows(
                self.left[:, :, columns(source, 256)].reshape(depth, 256),
                self.right[...].reshape(depth, self.right.shape[2]),
            ).astype(jnp.bfloat16)
            return carried

        lax.fori_loop(low // 256, high // 256, step, 0)

    def begin(self):
        self.fill(2 * self.size, 4 * self.size)
        self.copy = self.links.send(self.total.at[2 * self.size :], self.into_a, 0, 2)

    def keep(self):
        self.fill(0, 2 * self.size)

    def second(self):
        self.links.settle(self.copy)
        both = pl.ds(0, 2 * self.size)
        self.total[both, :] = (
            self.total[both, :].astype(jnp.float32) + self.into_a[...].astype(jnp.float32)
        ).astype(jnp.bfloat16)
        self.copy = self.links.send(
            self.total.at[self.size : 2 * self.size], self.into_b, 0, 6
        )

    def third(self):
        self.copy.wait_recv()
        self.ready = self.total.at[2 * self.size : 3 * self.size]
        self.ready[...] = (
            self.total[: self.size, :].astype(jnp.float32) + self.into_b[...].astype(jnp.float32)
        ).astype(jnp.bfloat16)

    def gather(self, ready, place):
        self.target = place
        own = place(self.links.dp_index)
        self.across = self.links.send(ready, own, 2, 0)
        self.core = self.links.send(ready, own, 1, 0)
        self.own = self.links.load(ready, own)

    def spread(self):
        self.across.wait_recv()
        other = self.target(flip(self.links.dp_index, 2))
        self.far = self.links.send(other, other, 1, 0)

    def finish(self):
        self.own.wait()
        arrived([self.core, self.far])


def layer_kernel(
    lengths, steps, mask_in, frames_in, skip_frames_in, cot_in, bias_in, w_skip, w_ada, w_qkv, w_out,
    w_up, w_down,
    result, grad_frames, grad_skip, sum_skip, sum_qkv, sum_out, sum_up, sum_down, small_all,
    embed_all,
    out_buf, up_buf, down_buf, weight_buf,
    joined_all, cot_all, first_all, attn_all, second_all, gated_all, upper_all, branch_all,
    packed_all, in_all,
    frames, skip, frame_mask, biases,
    first_own, embed_own, masks, table, packed_send, packed, attn_send, attn_low,
    attn_sum, residual, scale, grad_gated, second_low, gated, upper_parts, residual_mid, normal_mid,
    grad_mid, branch, grad_heads, query_recv, pair_recv, grad_packed, grad_in, key_total,
    value_total, small, small_send, small_recv, up_ready,
    down_sum, down_a, down_b, up_sum, up_a, up_b, out_sum, out_a, out_b, skip_sum, skip_a, skip_b,
    query_sum, query_a, query_b, key_sum, key_a, key_b, value_sum, value_a, value_b,
    send_sems, recv_sems, load_sems,
):
    links = Links(send_sems, recv_sems, load_sems)
    seq_index, dp_index = links.seq_index, links.dp_index
    rows, width = frames.shape
    hidden = grad_gated.shape[1]
    float32, bfloat16 = jnp.float32, jnp.bfloat16
    odd = bit(seq_index, 0)
    load_frames = links.load(frames_in, frames)
    load_skip_frames = links.load(skip_frames_in, skip)
    load_mask = links.load(mask_in, frame_mask)
    load_bias = links.load(bias_in, biases)
    load_skip = links.load(w_skip, down_buf.at[: 2 * width])
    load_ada = links.load(w_ada, weight_buf)
    enter = links.barrier()
    load_qkv = links.load(w_qkv, up_buf.at[:, : 3 * width])
    load_cot = links.load(cot_in, cot_all.at[0])
    cotangent = cot_all.at[0]

    def relative(source, target, size):
        for number, mask in enumerate(RELATIVE):
            target[:, number * size : (number + 1) * size] = source(flip(seq_index, mask))

    def joined_block(place):
        inside = columns(lax.rem(place, jnp.int32(4)) * 256, 256)
        return jnp.where(place < 4, frames[:, inside], skip[:, inside])

    ends = utterance_ends(lengths)
    utter = lax.broadcasted_iota(jnp.int32, embed_own.shape, 0)
    flow = jnp.zeros(embed_own.shape, float32)
    for number in range(steps.shape[1]):
        flow = jnp.where(utter == number, steps[0, number].astype(float32), flow)
    lane = lax.broadcasted_iota(jnp.int32, embed_own.shape, 1)
    half = width // 2
    frequency = jnp.exp((lane % half).astype(float32) * (-math.log(10000.0) / half))
    sine, cosine = turn_sine_cosine(1000.0 * (flow / TSTEPS) * frequency)
    embed = jnp.where(lane < half, sine, cosine)
    embed_own[...] = jnp.where(utter < steps.shape[1], embed, 0.0).astype(bfloat16)
    first_row = seq_index * rows
    cos_own, sin_own = rotary(ends, first_row, rows, 256)
    load_frames.wait()
    load_skip_frames.wait()
    load_mask.wait()
    load_bias.wait()
    masks[0] = jnp.broadcast_to(frame_mask[...], masks.shape[1:])
    load_skip.wait()
    residual[...] = product(frames[...], down_buf[:width]) + product(
        skip[...], down_buf[width : 2 * width]
    )
    load_ada.wait()
    table[...] = product(embed_own[...], weight_buf[...]) + biases[:, : 2 * width].astype(float32)
    normal, unused = norm_parts(residual[...])
    row_index = first_row + lax.broadcasted_iota(jnp.int32, (rows, 1), 0)
    own_segment = segments(ends, row_index)
    spread_scale = jnp.zeros((rows, width), float32)
    spread_shift = jnp.zeros((rows, width), float32)
    for number in range(len(ends)):
        member = own_segment == number
        spread_scale = jnp.where(member, table[number : number + 1, :width], spread_scale)
        spread_shift = jnp.where(member, table[number : number + 1, width:], spread_shift)
    scale[...] = spread_scale
    second_low[...] = (normal * (1.0 + spread_scale) + spread_shift).astype(bfloat16)
    enter()
    mask_copies = [links.send(masks.at[0], masks.at[m], 0, m) for m in range(1, 8)]
    load_qkv.wait()
    packed_copies = []
    for far in (2, 1, 3, 0):
        pair = flip(lax.div(seq_index, jnp.int32(2)), far)
        parts = []
        for kind in range(3):
            part = product(second_low[...], up_buf[:, columns(kind * width + pair * 256, 256)])
            if kind < 2:
                part = part * cos_own + partner(part) * sin_own
            parts.append(part.astype(bfloat16))
        for side in range(2):
            for kind in range(3):
                packed_send[pair * 2 + side, :, kind * 128 : (kind + 1) * 128] = parts[kind][
                    :, side * 128 : (side + 1) * 128
                ]
        for mask in (2 * far, 2 * far + 1):
            if mask:
                packed_copies.append(
                    links.send(
                        packed_send.at[flip(seq_index, mask)], packed.at[seq_index], 0, mask
                    )
                )
    load_down_low = links.load(w_down.at[: 2 * width], down_buf.at[: 2 * width])
    load_down_high = links.load(w_down.at[2 * width :], down_buf.at[2 * width :])
    load_out = links.load(w_out, out_buf)
    load_up = links.load(w_up, up_buf)
    packed[seq_index] = packed_send[seq_index]
    load_cot.wait()
    cot_share = Share(links, cot_all, cotangent, cotangent)
    joined_own = grad_packed.at[:, width:]
    relative(joined_block, joined_own, 256)
    joined_all[0] = joined_own[:, :width]
    relative(lambda place: second_low[:, columns(place * 128, 128)], first_own, 128)
    first_all[0] = first_own[:, : width // 2]
    joined_share = Share(links, joined_all, joined_all.at[0], joined_own.at[:, width:])
    first_share = Share(links, first_all, first_all.at[0], first_own.at[:, width // 2 :])
    embed_copies = [links.send(embed_own, embed_all.at[dp_index], m, 0) for m in (1, 2, 3)]
    embed_load = links.load(embed_own, embed_all.at[dp_index])
    load_down_low.wait()
    load_down_high.wait()

    def gated_step(step, carried):
        part = columns(step * 512, 512)
        grad_gated[:, part] = product_cols(cotangent[...], down_buf[part, :])
        return carried

    lax.fori_loop(0, hidden // 512, gated_step, 0)
    arrived(mask_copies)
    arrived(packed_copies)
    key_index = lax.broadcasted_iota(jnp.int32, (1, 8 * rows), 1)
    key_segment = segments(ends, key_index)
    key_valid = jnp.concatenate(
        [masks[exclusive(seq_index, jnp.int32(number))][:1] for number in range(8)], axis=1
    )

    def attend(place):
        query = packed[place, :, :128]
        row_index = place * rows + lax.broadcasted_iota(jnp.int32, (rows, 1), 0)
        allowed = (segments(ends, row_index) == key_segment) & (
            (key_valid > 0) | (row_index == key_index)
        )
        keys = packed[:, :, 128:256].reshape(8 * rows, 128)
        values = packed[:, :, 256:].reshape(8 * rows, 128)
        total = jnp.zeros((rows, 128), float32)
        here = pl.ds(pl.multiple_of(place * rows, rows), rows)
        for head in range(2):
            scores = product_cols(head_mask(query, head), keys) * (1.0 / math.sqrt(HEAD))
            scores = jnp.where(allowed, scores, masked_score)
            raised = jnp.exp(scores - jnp.max(scores, axis=1, keepdims=True))
            low = (raised / jnp.sum(raised, axis=1, keepdims=True)).astype(bfloat16)
            weight_buf[here, head * 1024 : (head + 1) * 1024] = low
            total = total + product(low, head_mask(values, head))
        attn_sum[here, :] = total
        attn_send[place] = total.astype(bfloat16)

    def by_frames(source, target):
        base = links.used
        links.used += 8

        def copy_of(mask):
            place = exclusive(seq_index, mask)
            return pltpu.make_async_remote_copy(
                src_ref=source.at[place],
                dst_ref=target.at[seq_index],
                send_sem=send_sems.at[base + mask],
                recv_sem=recv_sems.at[base + mask],
                device_id=(dp_index, place),
                device_id_type=MESH,
            )

        return copy_of

    attn_copy = by_frames(attn_send, attn_low)

    def attend_step(step, carried):
        mask = lax.rem(step + 4, jnp.int32(8))
        attend(exclusive(seq_index, mask))
        attn_copy(mask).start()
        return carried

    lax.fori_loop(0, 4, attend_step, 0)
    lax.fori_loop(5, 8, attend_step, 0)
    attend(seq_index)
    attn_low[seq_index] = attn_send[seq_index]
    load_out.wait()
    for mask in range(1, 8):
        attn_copy(jnp.int32(mask)).wait()
    joined_attn = jnp.concatenate([attn_low[number] for number in range(8)], axis=1)
    residual_mid[...] = residual[...] + product(joined_attn, out_buf[...])
    normal, factor_mid = norm_parts(residual_mid[...])
    normal_mid[...] = normal
    gain_float = biases[:, 7 * width : 8 * width].astype(float32)
    second_all[0] = (normal * gain_float).astype(bfloat16)
    second_share = Share(links, second_all, second_all.at[0], second_all.at[0])
    cot_share.forward()
    joined_share.forward()
    first_share.forward()
    small[8:] = jnp.zeros((8, small.shape[1]), float32)
    load_up.wait()

    def up_step(step, carried):
        part = columns(step * 512, 512)
        upper = product(second_all[0], up_buf[:, part]) + biases[
            :, columns(2 * width + step * 512, 512)
        ].astype(float32)
        value, slope = gelu_parts(upper)
        grad_upper = (grad_gated[:, part] * slope).astype(bfloat16)
        gated[:, part] = value.astype(bfloat16)
        upper_parts[:, part] = grad_upper
        small[
            pl.ds(8 + lax.div(step, jnp.int32(4)), 1),
            columns(lax.rem(step, jnp.int32(4)) * 512, 512),
        ] = jnp.sum(grad_upper.astype(float32), axis=0, keepdims=True)
        return carried

    lax.fori_loop(0, hidden // 512, up_step, 0)

    def second_step(step, total):
        part = columns(step * 512, 512)
        return total + product_cols(upper_parts[:, part], up_buf[:, part])

    grad_second = lax.fori_loop(
        0, hidden // 512, second_step, jnp.zeros((rows, width), float32)
    )
    grad_out = cotangent[...].astype(float32)
    normal = normal_mid[...]
    small[10:11, :width] = jnp.sum(grad_second * normal, axis=0, keepdims=True)
    small[10:11, width:] = jnp.sum(grad_out, axis=0, keepdims=True)
    grad_mid[...] = grad_out + norm_back(grad_second * gain_float, normal, factor_mid)
    branch[...] = grad_mid[...].astype(bfloat16)
    grad_attn = product_cols(branch[...], out_buf[...]).astype(bfloat16)
    grad_send = attn_send
    for number in range(8):
        grad_send[number] = grad_attn[:, number * 128 : (number + 1) * 128]
    head_copies = [
        links.send(grad_send.at[flip(seq_index, m)], grad_heads.at[seq_index], 0, m)
        for m in FAR_FIRST
    ]
    grad_heads[seq_index] = grad_send[seq_index]

    def quarters(source, slots):
        size = slots.shape[2]
        slots[0] = source[:, columns(dp_index * size, size)]
        return [
            links.send(
                source.at[:, columns(flip(dp_index, m) * size, size)], slots.at[4 * v + m], m, v
            )
            for m, v in GROUP
        ]

    second_share.forward()
    branch_copies = quarters(branch, branch_all)
    attn_own = grad_packed.at[:, :width]
    relative(lambda place: attn_low[place], attn_own, 128)
    attn_all[0] = attn_own[:, : width // 2]
    attn_share = Share(links, attn_all, attn_all.at[0], attn_own.at[:, width // 2 :])
    cot_share.wait()
    second_share.wait()

    def again(first):
        units, spots = [], []
        for number in (first, first + 1):
            place = flip(seq_index, RELATIVE[number])
            units.append(place * 512 + dp_index * 128)
            spots.append(lax.div(place, jnp.int32(2)))
        weight_up = jnp.concatenate([up_buf[:, columns(unit, 128)] for unit in units], axis=1)
        weight_down = jnp.concatenate([down_buf[columns(unit, 128), :] for unit in units], axis=0)
        bias = jnp.concatenate(
            [biases[:, columns(2 * width + unit, 128)] for unit in units], axis=1
        ).astype(float32)

        def again_step(step, carried):
            both = pl.ds(2 * step, 2)
            upper = product(second_all[both].reshape(2 * rows, width), weight_up) + bias
            value, slope = gelu_parts(upper)
            grad = product_cols(cot_all[both].reshape(2 * rows, width), weight_down)
            gated_all[both, :, first * 128 : (first + 2) * 128] = value.astype(bfloat16).reshape(
                2, rows, 256
            )
            grad_upper = (grad * slope).astype(bfloat16).reshape(2, rows, 256)
            for side in range(2):
                upper_all[both, :, columns(spots[side] * 128, 128)] = grad_upper[
                    :, :, side * 128 : (side + 1) * 128
                ]
            return carried

        lax.fori_loop(0, 4, again_step, 0)

    def pair_place(number):
        base_pair = lax.div(seq_index, jnp.int32(2))
        step_a, step_b = lax.div(number, jnp.int32(2)), lax.rem(number, jnp.int32(2))
        two = jnp.int32(2)
        low_bit = lax.rem(bit(base_pair, 0) + step_a + step_b, two)
        high_bit = lax.rem(bit(base_pair, 1) + step_b, two)
        return (2 * high_bit + low_bit) * 256

    down = Sum(links, gated_all, cot_all, down_sum, down_a, down_b)
    up = Sum(links, second_all, upper_all, up_sum, up_a, up_b, pair_place)
    out = Sum(links, attn_all, branch_all, out_sum, out_a, out_b)
    query_part = Sum(links, first_all, packed_all.at[0], query_sum, query_a, query_b)
    key_part = Sum(links, first_all, packed_all.at[1], key_sum, key_a, key_b)
    value_part = Sum(links, first_all, packed_all.at[2], value_sum, value_a, value_b)
    skip_part = Sum(links, joined_all, in_all, skip_sum, skip_a, skip_b)
    again(2)
    down.begin()
    arrived(head_copies)
    links.sent_done(packed_copies)
    links.sent_done(head_copies)
    query_send = attn_send
    pair_send = packed_send.at[:, :, :256]
    query_copy = by_frames(query_send, query_recv)
    shrink = 1.0 / math.sqrt(HEAD)
    key_total[...] = jnp.zeros_like(key_total)
    value_total[...] = jnp.zeros_like(value_total)

    def back(place):
        here = pl.ds(pl.multiple_of(place * rows, rows), rows)
        grad = grad_heads[place]
        query = packed[place, :, :128]
        keys = packed[:, :, 128:256].reshape(8 * rows, 128)
        values = packed[:, :, 256:].reshape(8 * rows, 128)
        both = grad.astype(float32) * attn_sum[here, :]
        total = jnp.zeros((rows, 128), float32)
        for head in range(2):
            low = weight_buf[here, head * 1024 : (head + 1) * 1024]
            grad_head = head_mask(grad, head)
            delta = jnp.sum(head_mask(both, head), axis=1, keepdims=True)
            grad_scores = (
                low.astype(float32) * (product_cols(grad_head, values) - delta)
            ).astype(bfloat16)
            total = total + product(grad_scores, head_mask(keys, head))
            key_total[...] += product_rows(grad_scores, head_mask(query, head))
            value_total[...] += product_rows(low, grad_head)
        total = total * shrink
        cosine, sine = rotary(ends, place * rows, rows, 128)
        query_send[place] = (total * cosine - partner(total) * sine).astype(bfloat16)

    def back_step(step, carried):
        mask = lax.rem(step + 4, jnp.int32(8))
        back(exclusive(seq_index, mask))
        query_copy(mask).start()
        return carried

    lax.fori_loop(0, 4, back_step, 0)
    lax.fori_loop(5, 8, back_step, 0)
    back(seq_index)
    query_recv[seq_index] = query_send[seq_index]

    def key_step(place, carried):
        here = pl.ds(pl.multiple_of(place * rows, rows), rows)
        total = key_total[here, :] * shrink
        cosine, sine = rotary(ends, place * rows, rows, 128)
        pair_send[place, :, :128] = (total * cosine - partner(total) * sine).astype(bfloat16)
        pair_send[place, :, 128:] = value_total[here, :].astype(bfloat16)
        return carried

    lax.fori_loop(0, 8, key_step, 0)
    pair_copies = [
        links.send(pair_send.at[flip(seq_index, m)], pair_recv.at[seq_index], 0, m)
        for m in FAR_FIRST
    ]
    pair_recv[seq_index] = pair_send[seq_index]
    again(0)
    load_qkv = links.load(w_qkv, up_buf.at[:, : 3 * width])
    up.begin()
    down.keep()
    for mask in range(1, 8):
        query_copy(jnp.int32(mask)).wait()
    for share in (joined_share, attn_share):
        links.sent_done([share.beside, share.corner])
    for number in range(8):
        grad_packed[:, number * 128 : (number + 1) * 128] = query_recv[number]
    query_parts = quarters(grad_packed.at[:, :width], packed_all.at[0])
    load_qkv.wait()

    def first_step(step, total):
        part = columns(step * 512, 512)
        return total + product_cols(grad_packed[:, part], up_buf[:, part])

    grad_first = lax.fori_loop(0, 2, first_step, jnp.zeros((rows, width), float32))
    scale_normal, factor = norm_parts(residual[...])
    attn_share.forward()
    up.keep()
    down.second()
    arrived(branch_copies)
    attn_share.wait()
    out.begin()
    out.keep()

    def down_step(step, total):
        part = columns(step * 512, 512)
        return total + product(gated[:, part], down_buf[part, :])

    lower = lax.fori_loop(
        0,
        hidden // 512,
        down_step,
        residual_mid[...] + biases[:, 6 * width : 7 * width].astype(float32),
    )
    second_low[...] = lower.astype(bfloat16)
    out_loads = [links.load(second_low, result)]
    load_skip = links.load(w_skip, down_buf.at[: 2 * width])
    arrived(pair_copies)
    for number in range(8):
        for kind in (1, 2):
            grad_packed[:, kind * width + number * 128 : kind * width + (number + 1) * 128] = (
                pair_recv[number, :, (kind - 1) * 128 : kind * 128]
            )
    key_parts = quarters(grad_packed.at[:, width : 2 * width], packed_all.at[1])
    grad_first = lax.fori_loop(2, 6, first_step, grad_first)
    grad_in[...] = (
        grad_mid[...] + norm_back(grad_first * (1.0 + scale[...]), scale_normal, factor)
    ).astype(bfloat16)
    in_copies = quarters(grad_in, in_all)
    value_parts = quarters(grad_packed.at[:, 2 * width :], packed_all.at[2])
    up.second()
    out.second()
    first_share.wait()
    arrived(query_parts)
    query_part.begin()
    query_part.keep()
    scaled = grad_first * scale_normal
    for number in range(len(ends)):
        member = own_segment == number
        small[number : number + 1, :width] = jnp.sum(
            jnp.where(member, scaled, 0.0), axis=0, keepdims=True
        )
        small[number : number + 1, width:] = jnp.sum(
            jnp.where(member, grad_first, 0.0), axis=0, keepdims=True
        )

    def small_start(number, mask):
        small_send[number] = small[...].astype(bfloat16)
        return links.send(small_send.at[number], small_recv.at[number], 0, mask)

    def small_add(copy, number):
        copy.wait_recv()
        small[...] = small_send[number].astype(float32) + small_recv[number].astype(float32)

    small_copy = small_start(0, 1)
    by_rows = lambda target, size: lambda index: target.at[pl.ds(index * size, size), :]
    by_cols = lambda start, target: lambda index: target.at[:, columns(start + index * 256, 256)]
    down.third()
    down.gather(down.ready, by_rows(sum_down, 128))
    arrived(key_parts)
    key_part.begin()
    key_part.keep()
    joined_share.wait()
    arrived(in_copies)
    skip_part.begin()
    skip_part.keep()
    arrived(value_parts)
    value_part.begin()
    value_part.keep()
    small_add(small_copy, 0)
    small_copy = small_start(1, 2)
    query_part.second()
    up.third()
    up_ready[odd] = up.ready[pl.ds(pl.multiple_of(odd * 128, 128), 128), :]
    up_other = links.send(
        up.ready.at[pl.ds(pl.multiple_of((1 - odd) * 128, 128), 128), :], up_ready.at[odd], 0, 1
    )
    out.third()
    out.gather(out.ready, by_cols(0, sum_out))
    down.spread()
    load_skip.wait()
    for held, target, start in ((residual, grad_frames, 0), (normal_mid, grad_skip, width)):
        held[...] = product_cols(grad_in[...], down_buf[start : start + width, :])
        out_loads.append(links.load(held, target))
    key_part.second()
    skip_part.second()
    value_part.second()
    small_add(small_copy, 1)
    small_copy = small_start(2, 6)
    up_other.wait_recv()
    up.gather(up_ready, lambda index: sum_up.at[index])
    out.spread()
    query_part.third()
    query_part.gather(query_part.ready, by_cols(0, sum_qkv))
    key_part.third()
    key_part.gather(key_part.ready, by_cols(width, sum_qkv))
    skip_part.third()
    skip_part.gather(skip_part.ready, by_cols(0, sum_skip))
    value_part.third()
    value_part.gather(value_part.ready, by_cols(2 * width, sum_qkv))
    small_add(small_copy, 2)
    small_send[3] = small[...].astype(bfloat16)
    small_copies = [
        links.send(small_send.at[3], small_all.at[dp_index], m, 0) for m in (3, 2, 1)
    ]
    small_load = links.load(small_send.at[3], small_all.at[dp_index])
    for each in (up, query_part, key_part, skip_part, value_part):
        each.spread()
    small_load.wait()
    embed_load.wait()
    for load in out_loads:
        load.wait()
    arrived(small_copies + embed_copies)
    for each in (down, up, out, query_part, key_part, skip_part, value_part):
        each.finish()
    links.drain()


def widen_kernel(
    result_in, frames_in, skip_in, sum_skip, sum_qkv, sum_out, sum_up, sum_down, small_all, embed_all,
    result, grad_frames, grad_skip, out_skip, out_ada, out_ada_bias, out_qkv, out_out, out_gain,
    out_up, out_up_bias, out_down, out_down_bias,
    low_result, low_frames, low_skip, low_w_skip, low_qkv, low_out, low_up, low_down, low_small, low_embed,
    full_skip, full_ada, full_qkv, full_out, full_up, full_down, in_sems, out_sems,
):
    float32 = jnp.float32
    seq_index = lax.axis_index("seq")
    sources = (sum_up, sum_down, sum_qkv, sum_skip, small_all, embed_all, sum_out, result_in, frames_in, skip_in)
    inside = (low_up, low_down, low_qkv, low_w_skip, low_small, low_embed, low_out, low_result, low_frames, low_skip)
    loads = [
        pltpu.make_async_copy(source, target, in_sems.at[number])
        for number, (source, target) in enumerate(zip(sources, inside, strict=True))
    ]
    for load in loads:
        load.start()
    stores = []

    def store(source, target):
        copy = pltpu.make_async_copy(source, target, out_sems.at[len(stores)])
        copy.start()
        stores.append(copy)

    loads[0].wait()
    for quarter in range(4):
        for side in range(2):
            for level in range(4):
                start = (2 * level + side) * 512 + quarter * 128
                full_up[:, start : start + 128] = low_up[
                    quarter, side, :, level * 128 : (level + 1) * 128
                ].astype(float32)
    store(full_up, out_up)
    for number, low, full, out in (
        (1, low_down, full_down, out_down),
        (2, low_qkv, full_qkv, out_qkv),
        (3, low_w_skip, full_skip, out_skip),
    ):
        loads[number].wait()
        full[...] = low[...].astype(float32)
        store(full, out)
    loads[4].wait()
    loads[5].wait()
    size = full_ada.shape[0]
    own = low_embed[:, :, columns(seq_index * size, size)].reshape(-1, size)
    full_ada[...] = product_rows(own, low_small[...].reshape(own.shape[0], full_ada.shape[1]))
    store(full_ada, out_ada)
    loads[6].wait()
    full_out[...] = low_out[...].astype(float32)
    store(full_out, out_out)
    for number, low, out in ((7, low_result, result), (8, low_frames, grad_frames), (9, low_skip, grad_skip)):
        loads[number].wait()
        store(low, out)
    wide = low_small.shape[2]
    spot = columns(seq_index * 256, 256)
    bias = jnp.zeros((1, 256), float32)
    for number in range(4):
        bias = bias + jnp.sum(low_small[number, :8, spot].astype(float32), axis=0, keepdims=True)
    out_ada_bias[...] = bias
    upper = jnp.zeros((1, 512), float32)
    gain = jnp.zeros((1, 128), float32)
    down_bias = jnp.zeros((1, 128), float32)
    high = lax.div(seq_index, jnp.int32(4))
    for number in range(4):
        both = low_small[number, 8:, columns(lax.rem(seq_index, jnp.int32(4)) * 512, 512)].astype(float32)
        upper = upper + jnp.where(high == 0, both[:1], both[1:2])
        gain = gain + low_small[number, 8:, columns(seq_index * 128, 128)].astype(float32)[2:3]
        down_bias = down_bias + low_small[number, 8:, columns(wide // 2 + seq_index * 128, 128)].astype(float32)[2:3]
    out_up_bias[...] = upper
    out_gain[...] = gain
    out_down_bias[...] = down_bias
    for copy in stores:
        copy.wait()


def one_kernel(
    frames, skip, lengths, frame_mask, time_step, w_skip, w_ada, b_ada, w_qkv, w_out, norm_gain,
    w_up, b_up, w_down, b_down, cotangent,
):
    rows, width = frames.shape[1:]
    hidden = b_up.shape[0]
    float32, bfloat16 = jnp.float32, jnp.bfloat16
    shape = jax.ShapeDtypeStruct
    vmem = pl.BlockSpec(memory_space=pltpu.VMEM)
    smem = pl.BlockSpec(memory_space=pltpu.SMEM)
    anywhere = pl.BlockSpec(memory_space=pl.ANY)
    dma = pltpu.SemaphoreType.DMA
    low = lambda *size: pltpu.VMEM(size, bfloat16)
    full = lambda *size: pltpu.VMEM(size, float32)
    biases = jnp.concatenate([b_ada, b_up, b_down, norm_gain])[None]
    sums = ((512, 1024), (1024, 512), (512, 256), (1024, 256), (512, 256), (512, 256), (512, 256))
    sum_scratch = [low(tall // part, wide) for tall, wide in sums for part in (1, 2, 4)]
    outs = (
        (shape((rows, width), bfloat16), anywhere),
        (shape((rows, width), float32), anywhere),
        (shape((rows, width), float32), anywhere),
        (shape((2 * width // 8, width), bfloat16), anywhere),
        (shape((width // 8, 3 * width), bfloat16), anywhere),
        (shape((width // 8, width), bfloat16), anywhere),
        (shape((4, 2, width // 8, hidden // 8), bfloat16), anywhere),
        (shape((hidden // 8, width), bfloat16), anywhere),
        (shape((4, 16, 2 * width), bfloat16), anywhere),
        (shape((4, 16, width), bfloat16), anywhere),
    )
    parts = pl.pallas_call(
        layer_kernel,
        out_shape=tuple(item[0] for item in outs),
        in_specs=[smem, smem] + [anywhere] * 11,
        out_specs=tuple(item[1] for item in outs),
        scratch_shapes=[
            low(*w_out.shape), low(*w_up.shape), low(*w_down.shape), low(8 * rows, 2 * width),
            low(8, rows, width), low(8, rows, width), low(8, rows, width // 2), low(8, rows, width // 2),
            low(8, rows, width), low(8, rows, 512), low(8, rows, 512), low(8, rows, 256),
            low(3, 8, rows, 256), low(8, rows, 256),
            low(rows, width), low(rows, width), pltpu.VMEM((1, rows), jnp.int32), low(1, 8 * width),
            low(rows, width), low(16, width), pltpu.VMEM((8, 8, rows), jnp.int32),
            full(16, 2 * width), low(8, rows, 384), low(8, rows, 384), low(8, rows, 128), low(8, rows, 128),
            full(8 * rows, 128), full(rows, width), full(rows, width), full(rows, hidden), low(rows, width),
            low(rows, hidden), low(rows, hidden), full(rows, width), full(rows, width),
            full(rows, width), low(rows, width), low(8, rows, 128), low(8, rows, 128), low(8, rows, 256), low(rows, 3 * width), low(rows, width), full(8 * rows, 128),
            full(8 * rows, 128), full(16, 2 * width), low(4, 16, 2 * width), low(3, 16, 2 * width),
            low(2, rows, 512),
            *sum_scratch,
            dma((192,)), dma((192,)), dma((40,)),
        ],
        compiler_params=pltpu.CompilerParams(
            collective_id=0, has_side_effects=True, vmem_limit_bytes=60 * MIB
        ),
        name="layer",
    )(
        lengths, time_step, frame_mask, frames[0], skip[0], cotangent[0], biases, w_skip, w_ada,
        w_qkv, w_out, w_up, w_down,
    )

    last_outs = (
        (shape((rows, width), bfloat16), anywhere),
        (shape((rows, width), float32), anywhere),
        (shape((rows, width), float32), anywhere),
        (shape((2 * width // 8, width), float32), anywhere),
        (shape((width // 8, 2 * width), float32), anywhere),
        (shape((1, 2 * width // 8), float32), vmem),
        (shape((width // 8, 3 * width), float32), anywhere),
        (shape((width // 8, width), float32), anywhere),
        (shape((1, width // 8), float32), vmem),
        (shape((width // 8, hidden), float32), anywhere),
        (shape((1, hidden // 8), float32), vmem),
        (shape((hidden // 8, width), float32), anywhere),
        (shape((1, width // 8), float32), vmem),
    )
    scratch = [pltpu.VMEM(item[0].shape, item[0].dtype) for item in outs]
    scratch += [full(*last_outs[number][0].shape) for number in (3, 4, 6, 7, 9, 11)]
    widened = pl.pallas_call(
        widen_kernel,
        out_shape=tuple(item[0] for item in last_outs),
        in_specs=[anywhere] * len(outs),
        out_specs=tuple(item[1] for item in last_outs),
        scratch_shapes=[*scratch, dma((10,)), dma((12,))],
        compiler_params=pltpu.CompilerParams(vmem_limit_bytes=60 * MIB),
        name="widen",
    )(*parts)
    return tuple(
        item[None] if number < 3 else item.reshape(-1) if item.shape[0] == 1 else item
        for number, item in enumerate(widened)
    )


def solution(mesh):
    placed = (
        P("dp", "seq", None),
        P("dp", "seq", None),
        P("dp", None),
        P("dp", "seq"),
        P("dp", None),
        P(),
        P(),
        P(),
        P(),
        P(),
        P(),
        P(),
        P(),
        P(),
        P(),
        P("dp", "seq", None),
    )
    split_heads = mesh.shape["dp"] == 4 and mesh.shape["seq"] == len(RELATIVE)
    return jax.shard_map(
        one_kernel if split_heads else on_device,
        mesh=mesh,
        in_specs=placed,
        out_specs=(
            P("dp", "seq", None),
            P("dp", "seq", None),
            P("dp", "seq", None),
            P("seq", None),
            P("seq", None),
            P("seq"),
            P("seq", None),
            P("seq", None),
            P("seq"),
            P("seq", None),
            P("seq"),
            P("seq", None),
            P("seq"),
        ),
        check_vma=False,
    )
```

```python
import math

import jax
import jax.numpy as jnp
from jax import lax
from jax.experimental import pallas as pl
from jax.experimental.pallas import tpu as pltpu
from jax.sharding import PartitionSpec as P

HEADS = 16
HEAD = 64
TSTEPS = 32


precise = lax.Precision.HIGHEST
masked_score = -1e30
contract_rows = (((0,), (0,)), ((), ()))
contract_cols = (((1,), (1,)), ((), ()))


def divisor_below(count_all, upper_limit):
    size_now = min(count_all, upper_limit)
    while count_all % size_now:
        size_now -= 1
    return size_now


def normalize(values):
    centered = values - jnp.mean(values, axis=-1, keepdims=True)
    variance = jnp.mean(centered * centered, axis=-1, keepdims=True)
    return centered * lax.rsqrt(variance + 1e-06)


def segment_of(lengths, frame_index):
    utter_ends = jnp.cumsum(lengths)
    return jnp.sum((frame_index[:, None] >= utter_ends[None, :]).astype(jnp.int32), axis=1)


def utterance_layout(lengths, frame_index):
    utter_ends = jnp.cumsum(lengths)
    starts = utter_ends - lengths
    segment = segment_of(lengths, frame_index)
    member = segment[:, None] == jnp.arange(lengths.shape[0], dtype=jnp.int32)[None, :]
    position = frame_index - jnp.sum(jnp.where(member, starts[None, :], 0), axis=1)
    return (segment, position, member)


def rotary_tables(position, head_size):
    half_size = head_size // 2
    frequency = jnp.exp(
        jnp.arange(half_size, dtype=jnp.float32) * (-2.0 * math.log(10000.0) / head_size)
    )
    angles = position.astype(jnp.float32)[:, None] * frequency[None, :]
    return (jnp.cos(angles)[:, None, :], jnp.sin(angles)[:, None, :])


def rotate(values, cos_table, sin_table):
    half_size = values.shape[-1] // 2
    first_half = values[..., :half_size]
    second_half = values[..., half_size:]
    return jnp.concatenate(
        [
            first_half * cos_table - second_half * sin_table,
            second_half * cos_table + first_half * sin_table,
        ],
        axis=-1,
    )


def rotate_back(values, cos_table, sin_table):
    half_size = values.shape[-1] // 2
    first_half = values[..., :half_size]
    second_half = values[..., half_size:]
    return jnp.concatenate(
        [
            first_half * cos_table + second_half * sin_table,
            second_half * cos_table - first_half * sin_table,
        ],
        axis=-1,
    )


def time_embedding(steps, model_width):
    half_size = model_width // 2
    flow_time = steps.astype(jnp.float32) / TSTEPS
    frequency = jnp.exp(jnp.arange(half_size, dtype=jnp.float32) * (-math.log(10000.0) / half_size))
    angles = 1000.0 * flow_time[:, None] * frequency[None, :]
    return jnp.concatenate([jnp.sin(angles), jnp.cos(angles)], axis=1)


def make_attend(query_low, query_segment, query_index, lengths):
    count_rows, head_count, head_size = query_low.shape
    scale_factor = 1.0 / math.sqrt(head_size)

    def attend(running, key_piece, first_row):
        keys_part, values_part, valid_part = key_piece
        count_keys = keys_part.shape[0]
        block_rows = divisor_below(count_keys, 1024)
        block_count = count_keys // block_rows
        key_blocks = keys_part.reshape(block_count, block_rows, head_count, head_size)
        value_blocks = values_part.reshape(block_count, block_rows, head_count, head_size)
        valid_blocks = valid_part.reshape(block_count, block_rows)
        offsets = first_row + jnp.arange(block_count, dtype=jnp.int32) * block_rows

        def attend_block_step(carried, inputs):
            row_top, row_total, weighted = carried
            key_block, value_block, valid_block, offset = inputs
            key_index = offset + jnp.arange(block_rows, dtype=jnp.int32)
            key_segment = segment_of(lengths, key_index)
            allowed = (query_segment[:, None] == key_segment[None, :]) & (
                (valid_block[None, :] > 0) | (query_index[:, None] == key_index[None, :])
            )
            scores = (
                jnp.einsum("qhd,khd->hqk", query_low, key_block, preferred_element_type=jnp.float32)
                * scale_factor
            )
            scores = jnp.where(allowed[None], scores, masked_score)
            new_top = jnp.maximum(row_top, jnp.max(scores, axis=2))
            weights = jnp.where(allowed[None], jnp.exp(scores - new_top[:, :, None]), 0.0)
            factor = jnp.exp(row_top - new_top)
            row_total = row_total * factor + jnp.sum(weights, axis=2)
            weighted = weighted * jnp.transpose(factor)[:, :, None] + jnp.einsum(
                "hqk,khd->qhd",
                weights.astype(jnp.bfloat16),
                value_block,
                preferred_element_type=jnp.float32,
            )
            return ((new_top, row_total, weighted), None)

        result_state, unused = lax.scan(
            attend_block_step, running, (key_blocks, value_blocks, valid_blocks, offsets)
        )
        return result_state

    return attend


def key_sweep(
    query_low, grad_attn, log_total, row_delta, query_segment, query_index, lengths, key_tuple
):
    keys_all, values_all, valid_all = key_tuple
    count_rows, head_count, head_size = query_low.shape
    scale_factor = 1.0 / math.sqrt(head_size)
    count_keys = keys_all.shape[0]
    block_rows = divisor_below(count_keys, 1024)
    block_count = count_keys // block_rows
    key_blocks = keys_all.reshape(block_count, block_rows, head_count, head_size)
    value_blocks = values_all.reshape(block_count, block_rows, head_count, head_size)
    valid_blocks = valid_all.reshape(block_count, block_rows)
    offsets = jnp.arange(block_count, dtype=jnp.int32) * block_rows
    top_shift = jnp.transpose(log_total)[:, :, None]
    delta_shift = jnp.transpose(row_delta)[:, :, None]

    def key_block_step(grad_query, inputs):
        key_block, value_block, valid_block, offset = inputs
        key_index = offset + jnp.arange(block_rows, dtype=jnp.int32)
        key_segment = segment_of(lengths, key_index)
        allowed = (query_segment[:, None] == key_segment[None, :]) & (
            (valid_block[None, :] > 0) | (query_index[:, None] == key_index[None, :])
        )
        scores = (
            jnp.einsum("qhd,khd->hqk", query_low, key_block, preferred_element_type=jnp.float32)
            * scale_factor
        )
        weights = jnp.where(allowed[None], jnp.exp(scores - top_shift), 0.0)
        grad_weights = jnp.einsum(
            "qhd,khd->hqk", grad_attn, value_block, preferred_element_type=jnp.float32
        )
        grad_scores = (weights * (grad_weights - delta_shift)).astype(jnp.bfloat16)
        grad_query = (
            grad_query
            + jnp.einsum("hqk,khd->qhd", grad_scores, key_block, preferred_element_type=jnp.float32)
            * scale_factor
        )
        grad_key = (
            jnp.einsum("hqk,qhd->khd", grad_scores, query_low, preferred_element_type=jnp.float32)
            * scale_factor
        )
        grad_value = jnp.einsum(
            "hqk,qhd->khd",
            weights.astype(jnp.bfloat16),
            grad_attn,
            preferred_element_type=jnp.float32,
        )
        return (grad_query, (grad_key, grad_value))

    start_grad = jnp.zeros((count_rows, head_count, head_size), jnp.float32)
    return lax.scan(key_block_step, start_grad, (key_blocks, value_blocks, valid_blocks, offsets))


def on_device(
    frames,
    skip,
    lengths,
    frame_mask,
    time_step,
    w_skip,
    w_ada,
    b_ada,
    w_qkv,
    w_out,
    norm_gain,
    w_up,
    b_up,
    w_down,
    b_down,
    cotangent,
):
    local_frames = frames[0]
    local_skip = skip[0]
    row_lengths = lengths[0]
    count_rows, model_width = local_frames.shape
    head_count = HEADS
    head_size = HEAD
    row_base = lax.axis_index("seq") * count_rows
    frame_index = row_base + jnp.arange(count_rows, dtype=jnp.int32)
    segment, position, member = utterance_layout(row_lengths, frame_index)
    member_float = member.astype(jnp.float32)
    embed_low = time_embedding(time_step[0], model_width).astype(jnp.bfloat16)
    ada_table = jnp.dot(embed_low, w_ada, preferred_element_type=jnp.float32) + b_ada.astype(
        jnp.float32
    )
    ada_frame = jnp.dot(member_float, ada_table, precision=precise)
    scale_part = ada_frame[:, :model_width]
    shift_part = ada_frame[:, model_width:]
    joined = jnp.concatenate([local_frames, local_skip], axis=1)
    residual_in = jnp.dot(joined, w_skip, preferred_element_type=jnp.float32)
    norm_first, first_pull = jax.vjp(normalize, residual_in)
    first_low = (norm_first * (1.0 + scale_part) + shift_part).astype(jnp.bfloat16)
    packed = jnp.dot(first_low, w_qkv, preferred_element_type=jnp.float32)
    cos_table, sin_table = rotary_tables(position, head_size)
    query_low = rotate(
        packed[:, :model_width].reshape(count_rows, head_count, head_size), cos_table, sin_table
    ).astype(jnp.bfloat16)
    keys_low = (
        rotate(
            packed[:, model_width : 2 * model_width].reshape(count_rows, head_count, head_size),
            cos_table,
            sin_table,
        )
        .astype(jnp.bfloat16)
        .reshape(count_rows, model_width)
    )
    values_low = packed[:, 2 * model_width :].astype(jnp.bfloat16)
    valid_low = frame_mask[0].astype(jnp.bfloat16)
    attend = make_attend(query_low, segment, frame_index, row_lengths)
    start_state = (
        jnp.full((head_count, count_rows), masked_score, jnp.float32),
        jnp.zeros((head_count, count_rows), jnp.float32),
        jnp.zeros((count_rows, head_count, head_size), jnp.float32),
    )
    gathered = (
        lax.all_gather(keys_low, "seq", axis=0, tiled=True),
        lax.all_gather(values_low, "seq", axis=0, tiled=True),
        lax.all_gather(valid_low, "seq", axis=0, tiled=True),
    )
    row_top, row_total, weighted = attend(start_state, gathered, 0)
    attn_sum = weighted / jnp.transpose(row_total)[:, :, None]
    log_total = jnp.transpose(row_top + jnp.log(row_total))
    attn_low = attn_sum.reshape(count_rows, model_width).astype(jnp.bfloat16)
    residual_mid = residual_in + jnp.dot(attn_low, w_out, preferred_element_type=jnp.float32)
    gain_float = norm_gain.astype(jnp.float32)
    second_float, second_pull = jax.vjp(
        lambda hidden, gain_vector: normalize(hidden) * gain_vector, residual_mid, gain_float
    )
    second_low = second_float.astype(jnp.bfloat16)
    upper_sum = jnp.dot(second_low, w_up, preferred_element_type=jnp.float32) + b_up.astype(
        jnp.float32
    )
    gated_float, gelu_pull = jax.vjp(
        lambda hidden: jax.nn.gelu(hidden, approximate=True), upper_sum
    )
    gated_low = gated_float.astype(jnp.bfloat16)
    output = (
        residual_mid
        + jnp.dot(gated_low, w_down, preferred_element_type=jnp.float32)
        + b_down.astype(jnp.float32)
    )
    grad_out = cotangent[0]
    grad_out_float = grad_out.astype(jnp.float32)
    grad_down = lax.dot_general(
        gated_low, grad_out, contract_rows, preferred_element_type=jnp.float32
    )
    grad_down_bias = jnp.sum(grad_out_float, axis=0)
    grad_gated = lax.dot_general(
        grad_out, w_down, contract_cols, preferred_element_type=jnp.float32
    )
    grad_upper = gelu_pull(grad_gated)[0].astype(jnp.bfloat16)
    grad_up = lax.dot_general(
        second_low, grad_upper, contract_rows, preferred_element_type=jnp.float32
    )
    grad_up_bias = jnp.sum(grad_upper.astype(jnp.float32), axis=0)
    grad_second = lax.dot_general(
        grad_upper, w_up, contract_cols, preferred_element_type=jnp.float32
    )
    grad_mid_norm, grad_gain = second_pull(grad_second)
    grad_mid = grad_out_float + grad_mid_norm
    grad_branch = grad_mid.astype(jnp.bfloat16)
    grad_out_weight = lax.dot_general(
        attn_low, grad_branch, contract_rows, preferred_element_type=jnp.float32
    )
    grad_attn = (
        lax.dot_general(grad_branch, w_out, contract_cols, preferred_element_type=jnp.float32)
        .astype(jnp.bfloat16)
        .reshape(count_rows, head_count, head_size)
    )
    row_delta = jnp.sum(grad_attn.astype(jnp.float32) * attn_sum, axis=2)
    grad_query, key_parts = key_sweep(
        query_low, grad_attn, log_total, row_delta, segment, frame_index, row_lengths, gathered
    )
    grad_key_all, grad_value_all = key_parts
    total_keys = grad_key_all.shape[0] * grad_key_all.shape[1]
    grad_key, grad_value = (
        lax.psum_scatter(
            grad_key_all.reshape(total_keys, model_width), "seq", scatter_dimension=0, tiled=True
        ),
        lax.psum_scatter(
            grad_value_all.reshape(total_keys, model_width), "seq", scatter_dimension=0, tiled=True
        ),
    )
    grad_key = rotate_back(
        grad_key.reshape(count_rows, head_count, head_size), cos_table, sin_table
    ).reshape(count_rows, model_width)
    grad_query = rotate_back(grad_query, cos_table, sin_table).reshape(count_rows, model_width)
    grad_packed = jnp.concatenate([grad_query, grad_key, grad_value], axis=1).astype(jnp.bfloat16)
    grad_qkv = lax.dot_general(
        first_low, grad_packed, contract_rows, preferred_element_type=jnp.float32
    )
    grad_first = lax.dot_general(
        grad_packed, w_qkv, contract_cols, preferred_element_type=jnp.float32
    )
    grad_ada_frame = jnp.concatenate([grad_first * norm_first, grad_first], axis=1)
    grad_ada_table = lax.dot_general(member_float, grad_ada_frame, contract_rows, precision=precise)
    grad_ada = lax.dot_general(
        embed_low.astype(jnp.float32), grad_ada_table, contract_rows, precision=precise
    )
    grad_ada_bias = jnp.sum(grad_ada_table, axis=0)
    grad_in = (grad_mid + first_pull(grad_first * (1.0 + scale_part))[0]).astype(jnp.bfloat16)
    grad_skip_weight = lax.dot_general(
        joined, grad_in, contract_rows, preferred_element_type=jnp.float32
    )
    grad_joined = lax.dot_general(
        grad_in, w_skip, contract_cols, preferred_element_type=jnp.float32
    )
    (
        share_skip,
        share_ada,
        share_ada_bias,
        share_qkv,
        share_out,
        share_gain,
        share_up,
        share_up_bias,
        share_down,
        share_down_bias,
    ) = (
        lax.psum_scatter(grad_skip_weight, "seq", scatter_dimension=0, tiled=True),
        lax.psum_scatter(grad_ada, "seq", scatter_dimension=0, tiled=True),
        lax.psum_scatter(grad_ada_bias, "seq", scatter_dimension=0, tiled=True),
        lax.psum_scatter(grad_qkv, "seq", scatter_dimension=0, tiled=True),
        lax.psum_scatter(grad_out_weight, "seq", scatter_dimension=0, tiled=True),
        lax.psum_scatter(grad_gain, "seq", scatter_dimension=0, tiled=True),
        lax.psum_scatter(grad_up, "seq", scatter_dimension=0, tiled=True),
        lax.psum_scatter(grad_up_bias, "seq", scatter_dimension=0, tiled=True),
        lax.psum_scatter(grad_down, "seq", scatter_dimension=0, tiled=True),
        lax.psum_scatter(grad_down_bias, "seq", scatter_dimension=0, tiled=True),
    )
    (
        total_skip,
        total_ada,
        total_ada_bias,
        total_qkv,
        total_out,
        total_gain,
        total_up,
        total_up_bias,
        total_down,
        total_down_bias,
    ) = (
        lax.psum(share_skip.astype(jnp.bfloat16), "dp").astype(jnp.float32),
        lax.psum(share_ada.astype(jnp.bfloat16), "dp").astype(jnp.float32),
        lax.psum(share_ada_bias.astype(jnp.bfloat16), "dp").astype(jnp.float32),
        lax.psum(share_qkv.astype(jnp.bfloat16), "dp").astype(jnp.float32),
        lax.psum(share_out.astype(jnp.bfloat16), "dp").astype(jnp.float32),
        lax.psum(share_gain.astype(jnp.bfloat16), "dp").astype(jnp.float32),
        lax.psum(share_up.astype(jnp.bfloat16), "dp").astype(jnp.float32),
        lax.psum(share_up_bias.astype(jnp.bfloat16), "dp").astype(jnp.float32),
        lax.psum(share_down.astype(jnp.bfloat16), "dp").astype(jnp.float32),
        lax.psum(share_down_bias.astype(jnp.bfloat16), "dp").astype(jnp.float32),
    )
    return (
        output.astype(jnp.bfloat16)[None],
        grad_joined[:, :model_width][None],
        grad_joined[:, model_width:][None],
        total_skip,
        total_ada,
        total_ada_bias,
        total_qkv,
        total_out,
        total_gain,
        total_up,
        total_up_bias,
        total_down,
        total_down_bias,
    )


RELATIVE = (0, 6, 2, 4, 1, 7, 3, 5)
PAIRS = (0, 3, 1, 2)
MESH = pl.DeviceIdType.MESH
MIB = 2**20
FAR_FIRST = (4, 5, 2, 3, 6, 7, 1)
GROUP = ((2, 0), (0, 1), (2, 1), (3, 0), (3, 1), (1, 1), (1, 0))
ROOT = math.sqrt(2.0 / math.pi)


def bit(value, place):
    return lax.rem(lax.div(value, jnp.int32(1 << place)), jnp.int32(2))


def flip(value, mask):
    out = value
    for place in range(3):
        if (mask >> place) & 1:
            out = out + (1 << place) * (1 - 2 * bit(value, place))
    return out


def exclusive(value, other):
    return sum(
        (1 << place) * lax.rem(bit(value, place) + bit(other, place), jnp.int32(2))
        for place in range(3)
    )


def columns(start, size):
    return pl.ds(pl.multiple_of(start, 128), size)


class Links:
    def __init__(self, send_sems, recv_sems, load_sems):
        self.send_sems, self.recv_sems, self.load_sems = send_sems, recv_sems, load_sems
        self.used, self.loads, self.sent = 0, 0, []
        self.dp_index, self.seq_index = lax.axis_index("dp"), lax.axis_index("seq")

    def peer(self, dp_mask, seq_mask):
        return (flip(self.dp_index, dp_mask), flip(self.seq_index, seq_mask))

    def barrier(self):
        semaphore = pltpu.get_barrier_semaphore()
        masks = [(0, mask) for mask in range(2, 8)] + list(GROUP)
        for mask in masks:
            pl.semaphore_signal(
                semaphore, inc=1, device_id=self.peer(*mask), device_id_type=MESH
            )
        return lambda: pl.semaphore_wait(semaphore, len(masks))

    def send(self, source, target, dp_mask, seq_mask):
        number = self.used
        self.used += 1
        copy = pltpu.make_async_remote_copy(
            src_ref=source,
            dst_ref=target,
            send_sem=self.send_sems.at[number],
            recv_sem=self.recv_sems.at[number],
            device_id=self.peer(dp_mask, seq_mask),
            device_id_type=MESH,
        )
        copy.start()
        self.sent.append(copy)
        return copy

    def load(self, source, target):
        copy = pltpu.make_async_copy(source, target, self.load_sems.at[self.loads])
        self.loads += 1
        copy.start()
        return copy

    def settle(self, copy):
        copy.wait()
        self.sent = [other for other in self.sent if other is not copy]

    def sent_done(self, copies):
        for copy in copies:
            copy.wait_send()
        self.sent = [other for other in self.sent if not any(other is copy for copy in copies)]

    def drain(self):
        for copy in self.sent:
            copy.wait_send()


class Share:
    def __init__(self, links, slots, near, far):
        self.links, self.slots = links, slots
        self.across = links.send(near, slots.at[2], 2, 0)
        self.beside = links.send(far, slots.at[4], 0, 1)
        self.corner = links.send(far, slots.at[6], 2, 1)
        self.waits = [links.send(near, slots.at[1], 1, 0)]

    def forward(self):
        for copy, slot in ((self.across, 2), (self.beside, 4), (self.corner, 6)):
            copy.wait_recv()
            self.waits.append(
                self.links.send(self.slots.at[slot], self.slots.at[slot + 1], 1, 0)
            )

    def wait(self):
        arrived(self.waits)


def arrived(copies):
    for copy in copies:
        copy.wait_recv()


def turn_sine_cosine(angles):
    turns = jnp.floor(angles * (0.5 / math.pi) + 0.5)
    rest = angles - turns * 6.28125
    rest = rest - turns * (2.0 * math.pi - 6.28125)
    return jnp.sin(rest), jnp.cos(rest)


def utterance_ends(lengths_ref):
    ends, total = [], jnp.int32(0)
    for number in range(lengths_ref.shape[1]):
        total = total + lengths_ref[0, number]
        ends.append(total)
    return ends


def segments(ends, index):
    return sum((index >= end).astype(jnp.int32) for end in ends)


def rotary(ends, first_row, rows, width):
    index = first_row + lax.broadcasted_iota(jnp.int32, (rows, width), 0)
    start = jnp.zeros_like(index)
    for end in ends:
        start = jnp.where(index >= end, end, start)
    lane = lax.broadcasted_iota(jnp.int32, (rows, width), 1) % HEAD
    pair = (lane % (HEAD // 2)).astype(jnp.float32)
    angles = (index - start).astype(jnp.float32) * jnp.exp(
        pair * (-2.0 * math.log(10000.0) / HEAD)
    )
    sine, cosine = turn_sine_cosine(angles)
    return cosine, jnp.where(lane < HEAD // 2, -sine, sine)


def partner(values):
    half_size = HEAD // 2
    lane = lax.broadcasted_iota(jnp.int32, values.shape, 1) % HEAD
    return jnp.where(
        lane < half_size,
        pltpu.roll(values, values.shape[1] - half_size, 1),
        pltpu.roll(values, half_size, 1),
    )


def head_mask(values, head):
    lane = lax.broadcasted_iota(jnp.int32, values.shape, 1)
    return jnp.where(lane // HEAD == head, values, jnp.zeros_like(values))


def norm_parts(values):
    centered = values - jnp.mean(values, axis=-1, keepdims=True)
    variance = jnp.mean(centered * centered, axis=-1, keepdims=True)
    factor = lax.rsqrt(variance + 1e-06)
    return centered * factor, factor


def norm_back(grad, normal, factor):
    mean_grad = jnp.mean(grad, axis=-1, keepdims=True)
    mean_product = jnp.mean(grad * normal, axis=-1, keepdims=True)
    return factor * (grad - mean_grad - normal * mean_product)


def product(left, right):
    return jnp.dot(left, right, preferred_element_type=jnp.float32)


def product_cols(left, right):
    return lax.dot_general(left, right, contract_cols, preferred_element_type=jnp.float32)


def product_rows(left, right):
    return lax.dot_general(left, right, contract_rows, preferred_element_type=jnp.float32)


def gelu_parts(upper):
    square = upper * upper
    bent = jnp.tanh(ROOT * (upper + 0.044715 * upper * square))
    value = 0.5 * upper * (1.0 + bent)
    slope = 0.5 * (1.0 + bent) + 0.5 * upper * (1.0 - bent * bent) * ROOT * (
        1.0 + 3.0 * 0.044715 * square
    )
    return value, slope


class Sum:
    def __init__(self, links, left, right, total, into_a, into_b, place=None):
        self.links, self.left, self.right, self.total = links, left, right, total
        self.into_a, self.into_b, self.place = into_a, into_b, place
        self.size = total.shape[0] // 4

    def fill(self, low, high):
        depth = self.left.shape[0] * self.left.shape[1]

        def step(number, carried):
            start = pl.multiple_of(number * 256, 256)
            source = start if self.place is None else self.place(number)
            self.total[pl.ds(start, 256), :] = product_rows(
                self.left[:, :, columns(source, 256)].reshape(depth, 256),
                self.right[...].reshape(depth, self.right.shape[2]),
            ).astype(jnp.bfloat16)
            return carried

        lax.fori_loop(low // 256, high // 256, step, 0)

    def begin(self):
        self.fill(2 * self.size, 4 * self.size)
        self.copy = self.links.send(self.total.at[2 * self.size :], self.into_a, 0, 2)

    def keep(self):
        self.fill(0, 2 * self.size)

    def second(self):
        self.links.settle(self.copy)
        both = pl.ds(0, 2 * self.size)
        self.total[both, :] = (
            self.total[both, :].astype(jnp.float32) + self.into_a[...].astype(jnp.float32)
        ).astype(jnp.bfloat16)
        self.copy = self.links.send(
            self.total.at[self.size : 2 * self.size], self.into_b, 0, 6
        )

    def third(self):
        self.copy.wait_recv()
        self.ready = self.total.at[2 * self.size : 3 * self.size]
        self.ready[...] = (
            self.total[: self.size, :].astype(jnp.float32) + self.into_b[...].astype(jnp.float32)
        ).astype(jnp.bfloat16)

    def gather(self, ready, place):
        self.target = place
        own = place(self.links.dp_index)
        self.across = self.links.send(ready, own, 2, 0)
        self.core = self.links.send(ready, own, 1, 0)
        self.own = self.links.load(ready, own)

    def spread(self):
        self.across.wait_recv()
        other = self.target(flip(self.links.dp_index, 2))
        self.far = self.links.send(other, other, 1, 0)

    def finish(self):
        self.own.wait()
        arrived([self.core, self.far])


def layer_kernel(
    lengths, steps, mask_in, frames_in, skip_frames_in, cot_in, bias_in, w_skip, w_ada, w_qkv, w_out,
    w_up, w_down,
    result, grad_frames, grad_skip, sum_skip, sum_qkv, sum_out, sum_up, sum_down, small_all,
    embed_all,
    out_buf, up_buf, down_buf, weight_buf,
    joined_all, cot_all, first_all, attn_all, second_all, gated_all, upper_all, branch_all,
    packed_all, in_all,
    frames, skip, frame_mask, biases,
    first_own, embed_own, masks, table, packed_send, packed, attn_send, attn_low,
    attn_sum, residual, scale, grad_gated, second_low, gated, upper_parts, residual_mid, normal_mid,
    grad_mid, branch, grad_heads, query_recv, pair_recv, grad_packed, grad_in,
    query_total, small, small_send, small_recv, up_ready,
    down_sum, down_a, down_b, up_sum, up_a, up_b, out_sum, out_a, out_b, skip_sum, skip_a, skip_b,
    query_sum, query_a, query_b, key_sum, key_a, key_b, value_sum, value_a, value_b,
    send_sems, recv_sems, load_sems,
):
    links = Links(send_sems, recv_sems, load_sems)
    seq_index, dp_index = links.seq_index, links.dp_index
    rows, width = frames.shape
    hidden = grad_gated.shape[1]
    float32, bfloat16 = jnp.float32, jnp.bfloat16
    odd = bit(seq_index, 0)
    load_frames = links.load(frames_in, frames)
    load_skip_frames = links.load(skip_frames_in, skip)
    load_mask = links.load(mask_in, frame_mask)
    load_bias = links.load(bias_in, biases)
    load_skip = links.load(w_skip, down_buf.at[: 2 * width])
    load_ada = links.load(w_ada, weight_buf)
    enter = links.barrier()
    load_qkv = links.load(w_qkv, up_buf.at[:, : 3 * width])
    load_cot = links.load(cot_in, cot_all.at[0])
    cotangent = cot_all.at[0]

    def relative(source, target, size):
        for number, mask in enumerate(RELATIVE):
            target[:, number * size : (number + 1) * size] = source(flip(seq_index, mask))

    def joined_block(place):
        inside = columns(lax.rem(place, jnp.int32(4)) * 256, 256)
        return jnp.where(place < 4, frames[:, inside], skip[:, inside])

    ends = utterance_ends(lengths)
    utter = lax.broadcasted_iota(jnp.int32, embed_own.shape, 0)
    flow = jnp.zeros(embed_own.shape, float32)
    for number in range(steps.shape[1]):
        flow = jnp.where(utter == number, steps[0, number].astype(float32), flow)
    lane = lax.broadcasted_iota(jnp.int32, embed_own.shape, 1)
    half = width // 2
    frequency = jnp.exp((lane % half).astype(float32) * (-math.log(10000.0) / half))
    sine, cosine = turn_sine_cosine(1000.0 * (flow / TSTEPS) * frequency)
    embed = jnp.where(lane < half, sine, cosine)
    embed_own[...] = jnp.where(utter < steps.shape[1], embed, 0.0).astype(bfloat16)
    first_row = seq_index * rows
    cos_own, sin_own = rotary(ends, first_row, rows, 256)
    load_mask.wait()
    masks[0] = jnp.broadcast_to(frame_mask[...], masks.shape[1:])
    load_cot.wait()
    enter()
    mask_copies = [links.send(masks.at[0], masks.at[m], 0, m) for m in range(1, 8)]
    cot_share = Share(links, cot_all, cotangent, cotangent)
    load_frames.wait()
    load_skip_frames.wait()
    load_bias.wait()
    load_skip.wait()
    residual[...] = product(frames[...], down_buf[:width]) + product(
        skip[...], down_buf[width : 2 * width]
    )
    load_ada.wait()
    table[...] = product(embed_own[...], weight_buf[...]) + biases[:, : 2 * width].astype(float32)
    normal, unused = norm_parts(residual[...])
    row_index = first_row + lax.broadcasted_iota(jnp.int32, (rows, 1), 0)
    own_segment = segments(ends, row_index)
    spread_scale = jnp.zeros((rows, width), float32)
    spread_shift = jnp.zeros((rows, width), float32)
    for number in range(len(ends)):
        member = own_segment == number
        spread_scale = jnp.where(member, table[number : number + 1, :width], spread_scale)
        spread_shift = jnp.where(member, table[number : number + 1, width:], spread_shift)
    scale[...] = spread_scale
    second_low[...] = (normal * (1.0 + spread_scale) + spread_shift).astype(bfloat16)
    load_qkv.wait()
    packed_copies, later = [], []
    for far in (2, 1, 3, 0):
        pair = flip(lax.div(seq_index, jnp.int32(2)), far)
        parts = []
        for kind in range(3):
            part = product(second_low[...], up_buf[:, columns(kind * width + pair * 256, 256)])
            if kind < 2:
                part = part * cos_own + partner(part) * sin_own
            parts.append(part.astype(bfloat16))
        for side in range(2):
            for kind in range(3):
                packed_send[pair * 2 + side, :, kind * 128 : (kind + 1) * 128] = parts[kind][
                    :, side * 128 : (side + 1) * 128
                ]
        for mask in (2 * far, 2 * far + 1):
            if mask:
                place = flip(seq_index, mask)
                packed_copies.append(
                    links.send(
                        packed_send.at[place, :, :256], packed.at[seq_index, :, :256], 0, mask
                    )
                )
                later.append((place, mask))
    value_copies = [
        links.send(packed_send.at[place, :, 256:], packed.at[seq_index, :, 256:], 0, mask)
        for place, mask in later
    ]
    load_down_low = links.load(w_down.at[: 2 * width], down_buf.at[: 2 * width])
    load_down_high = links.load(w_down.at[2 * width :], down_buf.at[2 * width :])
    load_out = links.load(w_out, out_buf)
    load_up = links.load(w_up, up_buf)
    packed[seq_index] = packed_send[seq_index]
    relative(lambda place: second_low[:, columns(place * 128, 128)], first_own, 128)
    first_all[0] = first_own[:, : width // 2]
    embed_copies = [links.send(embed_own, embed_all.at[dp_index], m, 0) for m in (1, 2, 3)]
    embed_load = links.load(embed_own, embed_all.at[dp_index])
    load_down_low.wait()
    load_down_high.wait()

    def gated_step(step, carried):
        part = columns(step * 512, 512)
        grad_gated[:, part] = product_cols(cotangent[...], down_buf[part, :])
        return carried

    lax.fori_loop(0, hidden // 512, gated_step, 0)
    arrived(mask_copies)
    arrived(packed_copies)
    key_index = lax.broadcasted_iota(jnp.int32, (1, 8 * rows), 1)
    key_segment = segments(ends, key_index)
    key_valid = jnp.concatenate(
        [masks[exclusive(seq_index, jnp.int32(number))][:1] for number in range(8)], axis=1
    )

    def weigh(place, carried):
        query = packed[place, :, :128]
        row_index = place * rows + lax.broadcasted_iota(jnp.int32, (rows, 1), 0)
        allowed = (segments(ends, row_index) == key_segment) & (
            (key_valid > 0) | (row_index == key_index)
        )
        keys = packed[:, :, 128:256].reshape(8 * rows, 128)
        here = pl.ds(pl.multiple_of(place * rows, rows), rows)
        for head in range(2):
            scores = product_cols(head_mask(query, head), keys) * (1.0 / math.sqrt(HEAD))
            scores = jnp.where(allowed, scores, masked_score)
            raised = jnp.exp(scores - jnp.max(scores, axis=1, keepdims=True))
            low = (raised / jnp.sum(raised, axis=1, keepdims=True)).astype(bfloat16)
            weight_buf[here, head * 1024 : (head + 1) * 1024] = low
        return carried

    def attend(place):
        values = packed[:, :, 256:].reshape(8 * rows, 128)
        total = jnp.zeros((rows, 128), float32)
        here = pl.ds(pl.multiple_of(place * rows, rows), rows)
        for head in range(2):
            low = weight_buf[here, head * 1024 : (head + 1) * 1024]
            total = total + product(low, head_mask(values, head))
        attn_sum[here, :] = total
        attn_send[place] = total.astype(bfloat16)

    def by_frames(source, target):
        base = links.used
        links.used += 8

        def copy_of(mask):
            place = exclusive(seq_index, mask)
            return pltpu.make_async_remote_copy(
                src_ref=source.at[place],
                dst_ref=target.at[seq_index],
                send_sem=send_sems.at[base + mask],
                recv_sem=recv_sems.at[base + mask],
                device_id=(dp_index, place),
                device_id_type=MESH,
            )

        return copy_of

    attn_copy = by_frames(attn_send, attn_low)

    def attend_step(step, carried):
        mask = lax.rem(step + 4, jnp.int32(8))
        attend(exclusive(seq_index, mask))
        attn_copy(mask).start()
        return carried

    lax.fori_loop(0, 8, weigh, 0)
    arrived(value_copies)
    lax.fori_loop(0, 4, attend_step, 0)
    lax.fori_loop(5, 8, attend_step, 0)
    attend(seq_index)
    attn_low[seq_index] = attn_send[seq_index]
    load_out.wait()
    for mask in range(1, 8):
        attn_copy(jnp.int32(mask)).wait()
    joined_attn = jnp.concatenate([attn_low[number] for number in range(8)], axis=1)
    residual_mid[...] = residual[...] + product(joined_attn, out_buf[...])
    normal, factor_mid = norm_parts(residual_mid[...])
    normal_mid[...] = normal
    gain_float = biases[:, 7 * width : 8 * width].astype(float32)
    second_all[0] = (normal * gain_float).astype(bfloat16)
    second_share = Share(links, second_all, second_all.at[0], second_all.at[0])
    cot_share.forward()
    small[8:] = jnp.zeros((8, small.shape[1]), float32)
    load_up.wait()

    def up_step(step, carried):
        part = columns(step * 512, 512)
        upper = product(second_all[0], up_buf[:, part]) + biases[
            :, columns(2 * width + step * 512, 512)
        ].astype(float32)
        value, slope = gelu_parts(upper)
        grad_upper = (grad_gated[:, part] * slope).astype(bfloat16)
        gated[:, part] = value.astype(bfloat16)
        upper_parts[:, part] = grad_upper
        small[
            pl.ds(8 + lax.div(step, jnp.int32(4)), 1),
            columns(lax.rem(step, jnp.int32(4)) * 512, 512),
        ] = jnp.sum(grad_upper.astype(float32), axis=0, keepdims=True)
        return carried

    lax.fori_loop(0, hidden // 512, up_step, 0)

    def second_step(step, total):
        part = columns(step * 512, 512)
        return total + product_cols(upper_parts[:, part], up_buf[:, part])

    grad_second = lax.fori_loop(
        0, hidden // 512, second_step, jnp.zeros((rows, width), float32)
    )
    grad_out = cotangent[...].astype(float32)
    normal = normal_mid[...]
    small[10:11, :width] = jnp.sum(grad_second * normal, axis=0, keepdims=True)
    small[10:11, width:] = jnp.sum(grad_out, axis=0, keepdims=True)
    grad_mid[...] = grad_out + norm_back(grad_second * gain_float, normal, factor_mid)
    branch[...] = grad_mid[...].astype(bfloat16)
    grad_attn = product_cols(branch[...], out_buf[...]).astype(bfloat16)
    grad_send = attn_send
    for number in range(8):
        grad_send[number] = grad_attn[:, number * 128 : (number + 1) * 128]
    head_copies = [
        links.send(grad_send.at[flip(seq_index, m)], grad_heads.at[seq_index], 0, m)
        for m in FAR_FIRST
    ]
    grad_heads[seq_index] = grad_send[seq_index]

    def quarters(source, slots):
        size = slots.shape[2]
        slots[0] = source[:, columns(dp_index * size, size)]
        return [
            links.send(
                source.at[:, columns(flip(dp_index, m) * size, size)], slots.at[4 * v + m], m, v
            )
            for m, v in GROUP
        ]

    second_share.forward()
    branch_copies = quarters(branch, branch_all)
    attn_own = upper_parts.at[:, 2 * width : 3 * width]
    relative(lambda place: attn_low[place], attn_own, 128)
    attn_all[0] = attn_own[:, : width // 2]
    attn_share = Share(links, attn_all, attn_all.at[0], attn_own.at[:, width // 2 :])
    cot_share.wait()
    joined_own = upper_parts.at[:, : 2 * width]
    relative(joined_block, joined_own, 256)
    joined_all[0] = joined_own[:, :width]

    def table_step(place, carried):
        cosine, sine = rotary(ends, place * rows, rows, 128)
        grad_gated[:, columns(place * 512, 128)] = cosine
        grad_gated[:, columns(place * 512 + 128, 128)] = sine
        return carried

    lax.fori_loop(0, 8, table_step, 0)
    second_share.wait()

    def again(first):
        units, spots = [], []
        for number in (first, first + 1):
            place = flip(seq_index, RELATIVE[number])
            units.append(place * 512 + dp_index * 128)
            spots.append(lax.div(place, jnp.int32(2)))
        weight_up = jnp.concatenate([up_buf[:, columns(unit, 128)] for unit in units], axis=1)
        weight_down = jnp.concatenate([down_buf[columns(unit, 128), :] for unit in units], axis=0)
        bias = jnp.concatenate(
            [biases[:, columns(2 * width + unit, 128)] for unit in units], axis=1
        ).astype(float32)

        def again_step(step, carried):
            both = pl.ds(2 * step, 2)
            upper = product(second_all[both].reshape(2 * rows, width), weight_up) + bias
            value, slope = gelu_parts(upper)
            grad = product_cols(cot_all[both].reshape(2 * rows, width), weight_down)
            gated_all[both, :, first * 128 : (first + 2) * 128] = value.astype(bfloat16).reshape(
                2, rows, 256
            )
            grad_upper = (grad * slope).astype(bfloat16).reshape(2, rows, 256)
            for side in range(2):
                upper_all[both, :, columns(spots[side] * 128, 128)] = grad_upper[
                    :, :, side * 128 : (side + 1) * 128
                ]
            return carried

        lax.fori_loop(0, 4, again_step, 0)

    def pair_place(number):
        base_pair = lax.div(seq_index, jnp.int32(2))
        step_a, step_b = lax.div(number, jnp.int32(2)), lax.rem(number, jnp.int32(2))
        two = jnp.int32(2)
        low_bit = lax.rem(bit(base_pair, 0) + step_a + step_b, two)
        high_bit = lax.rem(bit(base_pair, 1) + step_b, two)
        return (2 * high_bit + low_bit) * 256

    down = Sum(links, gated_all, cot_all, down_sum, down_a, down_b)
    up = Sum(links, second_all, upper_all, up_sum, up_a, up_b, pair_place)
    out = Sum(links, attn_all, branch_all, out_sum, out_a, out_b)
    query_part = Sum(links, first_all, packed_all.at[0], query_sum, query_a, query_b)
    key_part = Sum(links, first_all, packed_all.at[1], key_sum, key_a, key_b)
    value_part = Sum(links, first_all, packed_all.at[2], value_sum, value_a, value_b)
    skip_part = Sum(links, joined_all, in_all, skip_sum, skip_a, skip_b)
    again(2)
    down.begin()
    arrived(head_copies)
    links.sent_done(packed_copies + value_copies)
    links.sent_done(head_copies)
    query_send = attn_send
    pair_send = packed_send.at[:, :, :256]
    first_share = Share(links, first_all, first_all.at[0], first_own.at[:, width // 2 :])
    pair_copy = by_frames(pair_send, pair_recv)
    shrink = 1.0 / math.sqrt(HEAD)
    query_total[...] = jnp.zeros_like(query_total)

    def delta_step(place, carried):
        here = pl.ds(pl.multiple_of(place * rows, rows), rows)
        both = grad_heads[place].astype(float32) * attn_sum[here, :]
        for head in range(2):
            delta = jnp.sum(head_mask(both, head), axis=1, keepdims=True)
            grad_gated[:, columns(place * 512 + 256 + head * 128, 128)] = jnp.broadcast_to(
                delta, (rows, 128)
            )
        return carried

    lax.fori_loop(0, 8, delta_step, 0)

    def turned_back(total, place):
        cosine = grad_gated[:, columns(place * 512, 128)]
        sine = grad_gated[:, columns(place * 512 + 128, 128)]
        total = total * shrink
        return (total * cosine - partner(total) * sine).astype(bfloat16)

    def back(pair):
        both = pl.ds(2 * pair, 2)
        keys = packed[both, :, 128:256].reshape(2 * rows, 128)
        values = packed[both, :, 256:].reshape(2 * rows, 128)
        queries = packed[:, :, :128].reshape(8 * rows, 128)
        grad = grad_heads[...].reshape(8 * rows, 128)
        grad_keys = jnp.zeros((2 * rows, 128), float32)
        grad_values = jnp.zeros((2 * rows, 128), float32)
        for head in range(2):
            low = weight_buf[:, columns(head * 1024 + pair * 256, 256)]
            grad_head = head_mask(grad, head)
            delta = jnp.concatenate(
                [
                    grad_gated[:, place * 512 + 256 + head * 128 : place * 512 + 384 + head * 128]
                    for place in range(8)
                ],
                axis=0,
            )
            delta = jnp.concatenate([delta, delta], axis=1)
            grad_scores = (
                low.astype(float32) * (product_cols(grad_head, values) - delta)
            ).astype(bfloat16)
            query_total[...] += product(grad_scores, head_mask(keys, head))
            grad_keys = grad_keys + product_rows(grad_scores, head_mask(queries, head))
            grad_values = grad_values + product_rows(low, grad_head)
        for side in range(2):
            place = 2 * pair + side
            part = slice(side * rows, (side + 1) * rows)
            pair_send[place, :, :128] = turned_back(grad_keys[part], place)
            pair_send[place, :, 128:] = grad_values[part].astype(bfloat16)

    own_pair = lax.div(seq_index, jnp.int32(2))

    def back_step(step, carried):
        far = step + 2 - 3 * lax.div(step, jnp.int32(2))
        back(lax.div(exclusive(seq_index, 2 * far), jnp.int32(2)))
        pair_copy(2 * far).start()
        pair_copy(2 * far + 1).start()
        return carried

    lax.fori_loop(0, 3, back_step, 0)
    back(own_pair)
    pair_copy(jnp.int32(1)).start()
    pair_recv[seq_index] = pair_send[seq_index]

    def query_step(place, carried):
        here = pl.ds(pl.multiple_of(place * rows, rows), rows)
        query_send[place] = turned_back(query_total[here, :], place)
        return carried

    lax.fori_loop(0, 8, query_step, 0)
    query_copies = [
        links.send(query_send.at[flip(seq_index, m)], query_recv.at[seq_index], 0, m)
        for m in FAR_FIRST
    ]
    query_recv[seq_index] = query_send[seq_index]
    again(0)
    load_qkv = links.load(w_qkv, up_buf.at[:, : 3 * width])
    up.begin()
    down.keep()

    def down_step(step, total):
        part = columns(step * 512, 512)
        return total + product(gated[:, part], down_buf[part, :])

    lower = lax.fori_loop(
        0,
        hidden // 512,
        down_step,
        residual_mid[...] + biases[:, 6 * width : 7 * width].astype(float32),
    )
    second_low[...] = lower.astype(bfloat16)
    out_loads = [links.load(second_low, result)]
    load_skip = links.load(w_skip, down_buf.at[: 2 * width])
    for mask in range(1, 8):
        pair_copy(jnp.int32(mask)).wait()
    for number in range(8):
        for kind in (1, 2):
            grad_packed[:, kind * width + number * 128 : kind * width + (number + 1) * 128] = (
                pair_recv[number, :, (kind - 1) * 128 : kind * 128]
            )
    key_parts = quarters(grad_packed.at[:, width : 2 * width], packed_all.at[1])
    value_parts = quarters(grad_packed.at[:, 2 * width :], packed_all.at[2])
    joined_share = Share(links, joined_all, joined_all.at[0], joined_own.at[:, width:])
    load_qkv.wait()

    def first_step(step, total):
        part = columns(step * 512, 512)
        return total + product_cols(grad_packed[:, part], up_buf[:, part])

    grad_first = lax.fori_loop(2, 6, first_step, jnp.zeros((rows, width), float32))
    scale_normal, factor = norm_parts(residual[...])
    arrived(query_copies)
    for number in range(8):
        grad_packed[:, number * 128 : (number + 1) * 128] = query_recv[number]
    query_parts = quarters(grad_packed.at[:, :width], packed_all.at[0])
    grad_first = lax.fori_loop(0, 2, first_step, grad_first)
    grad_in[...] = (
        grad_mid[...] + norm_back(grad_first * (1.0 + scale[...]), scale_normal, factor)
    ).astype(bfloat16)
    in_copies = quarters(grad_in, in_all)
    attn_share.forward()
    first_share.forward()
    up.keep()
    down.second()
    arrived(branch_copies)
    attn_share.wait()
    out.begin()
    out.keep()
    up.second()
    first_share.wait()
    arrived(key_parts)
    key_part.begin()
    key_part.keep()
    arrived(value_parts)
    value_part.begin()
    value_part.keep()
    out.second()
    scaled = grad_first * scale_normal
    for number in range(len(ends)):
        member = own_segment == number
        small[number : number + 1, :width] = jnp.sum(
            jnp.where(member, scaled, 0.0), axis=0, keepdims=True
        )
        small[number : number + 1, width:] = jnp.sum(
            jnp.where(member, grad_first, 0.0), axis=0, keepdims=True
        )

    def small_start(number, mask):
        small_send[number] = small[...].astype(bfloat16)
        return links.send(small_send.at[number], small_recv.at[number], 0, mask)

    def small_add(copy, number):
        copy.wait_recv()
        small[...] = small_send[number].astype(float32) + small_recv[number].astype(float32)

    small_copy = small_start(0, 1)
    by_rows = lambda target, size: lambda index: target.at[pl.ds(index * size, size), :]
    by_cols = lambda start, target: lambda index: target.at[:, columns(start + index * 256, 256)]
    down.third()
    down.gather(down.ready, by_rows(sum_down, 128))
    arrived(query_parts)
    query_part.begin()
    query_part.keep()
    key_part.second()
    joined_share.forward()
    joined_share.wait()
    arrived(in_copies)
    skip_part.begin()
    skip_part.keep()
    value_part.second()
    small_add(small_copy, 0)
    small_copy = small_start(1, 2)
    up.third()
    up_ready[odd] = up.ready[pl.ds(pl.multiple_of(odd * 128, 128), 128), :]
    up_other = links.send(
        up.ready.at[pl.ds(pl.multiple_of((1 - odd) * 128, 128), 128), :], up_ready.at[odd], 0, 1
    )
    out.third()
    out.gather(out.ready, by_cols(0, sum_out))
    down.spread()
    load_skip.wait()
    for held, target, start in ((residual, grad_frames, 0), (normal_mid, grad_skip, width)):
        held[...] = product_cols(grad_in[...], down_buf[start : start + width, :])
        out_loads.append(links.load(held, target))
    query_part.second()
    skip_part.second()
    small_add(small_copy, 1)
    small_copy = small_start(2, 6)
    up_other.wait_recv()
    up.gather(up_ready, lambda index: sum_up.at[index])
    out.spread()
    key_part.third()
    key_part.gather(key_part.ready, by_cols(width, sum_qkv))
    value_part.third()
    value_part.gather(value_part.ready, by_cols(2 * width, sum_qkv))
    query_part.third()
    query_part.gather(query_part.ready, by_cols(0, sum_qkv))
    skip_part.third()
    skip_part.gather(skip_part.ready, by_cols(0, sum_skip))
    small_add(small_copy, 2)
    small_send[3] = small[...].astype(bfloat16)
    small_copies = [
        links.send(small_send.at[3], small_all.at[dp_index], m, 0) for m in (3, 2, 1)
    ]
    small_load = links.load(small_send.at[3], small_all.at[dp_index])
    for each in (up, key_part, value_part, query_part, skip_part):
        each.spread()
    small_load.wait()
    embed_load.wait()
    for load in out_loads:
        load.wait()
    arrived(small_copies + embed_copies)
    for each in (down, up, out, query_part, key_part, skip_part, value_part):
        each.finish()
    links.drain()


def widen_kernel(
    result_in, frames_in, skip_in, sum_skip, sum_qkv, sum_out, sum_up, sum_down, small_all, embed_all,
    result, grad_frames, grad_skip, out_skip, out_ada, out_ada_bias, out_qkv, out_out, out_gain,
    out_up, out_up_bias, out_down, out_down_bias,
    low_result, low_frames, low_skip, low_w_skip, low_qkv, low_out, low_up, low_down, low_small, low_embed,
    full_skip, full_ada, full_qkv, full_out, full_up, full_down, in_sems, out_sems,
):
    float32 = jnp.float32
    seq_index = lax.axis_index("seq")
    sources = (sum_up, sum_down, sum_qkv, sum_skip, small_all, embed_all, sum_out, result_in, frames_in, skip_in)
    inside = (low_up, low_down, low_qkv, low_w_skip, low_small, low_embed, low_out, low_result, low_frames, low_skip)
    loads = [
        pltpu.make_async_copy(source, target, in_sems.at[number])
        for number, (source, target) in enumerate(zip(sources, inside, strict=True))
    ]
    for load in loads:
        load.start()
    stores = []

    def store(source, target):
        copy = pltpu.make_async_copy(source, target, out_sems.at[len(stores)])
        copy.start()
        stores.append(copy)

    loads[0].wait()
    for quarter in range(4):
        for side in range(2):
            for level in range(4):
                start = (2 * level + side) * 512 + quarter * 128
                full_up[:, start : start + 128] = low_up[
                    quarter, side, :, level * 128 : (level + 1) * 128
                ].astype(float32)
    store(full_up, out_up)
    for number, low, full, out in (
        (1, low_down, full_down, out_down),
        (2, low_qkv, full_qkv, out_qkv),
        (3, low_w_skip, full_skip, out_skip),
    ):
        loads[number].wait()
        full[...] = low[...].astype(float32)
        store(full, out)
    loads[4].wait()
    loads[5].wait()
    size = full_ada.shape[0]
    own = low_embed[:, :, columns(seq_index * size, size)].reshape(-1, size)
    full_ada[...] = product_rows(own, low_small[...].reshape(own.shape[0], full_ada.shape[1]))
    store(full_ada, out_ada)
    loads[6].wait()
    full_out[...] = low_out[...].astype(float32)
    store(full_out, out_out)
    for number, low, out in ((7, low_result, result), (8, low_frames, grad_frames), (9, low_skip, grad_skip)):
        loads[number].wait()
        store(low, out)
    wide = low_small.shape[2]
    spot = columns(seq_index * 256, 256)
    bias = jnp.zeros((1, 256), float32)
    for number in range(4):
        bias = bias + jnp.sum(low_small[number, :8, spot].astype(float32), axis=0, keepdims=True)
    out_ada_bias[...] = bias
    upper = jnp.zeros((1, 512), float32)
    gain = jnp.zeros((1, 128), float32)
    down_bias = jnp.zeros((1, 128), float32)
    high = lax.div(seq_index, jnp.int32(4))
    for number in range(4):
        both = low_small[number, 8:, columns(lax.rem(seq_index, jnp.int32(4)) * 512, 512)].astype(float32)
        upper = upper + jnp.where(high == 0, both[:1], both[1:2])
        gain = gain + low_small[number, 8:, columns(seq_index * 128, 128)].astype(float32)[2:3]
        down_bias = down_bias + low_small[number, 8:, columns(wide // 2 + seq_index * 128, 128)].astype(float32)[2:3]
    out_up_bias[...] = upper
    out_gain[...] = gain
    out_down_bias[...] = down_bias
    for copy in stores:
        copy.wait()


def one_kernel(
    frames, skip, lengths, frame_mask, time_step, w_skip, w_ada, b_ada, w_qkv, w_out, norm_gain,
    w_up, b_up, w_down, b_down, cotangent,
):
    rows, width = frames.shape[1:]
    hidden = b_up.shape[0]
    float32, bfloat16 = jnp.float32, jnp.bfloat16
    shape = jax.ShapeDtypeStruct
    vmem = pl.BlockSpec(memory_space=pltpu.VMEM)
    smem = pl.BlockSpec(memory_space=pltpu.SMEM)
    anywhere = pl.BlockSpec(memory_space=pl.ANY)
    dma = pltpu.SemaphoreType.DMA
    low = lambda *size: pltpu.VMEM(size, bfloat16)
    full = lambda *size: pltpu.VMEM(size, float32)
    biases = jnp.concatenate([b_ada, b_up, b_down, norm_gain])[None]
    sums = ((512, 1024), (1024, 512), (512, 256), (1024, 256), (512, 256), (512, 256), (512, 256))
    sum_scratch = [low(tall // part, wide) for tall, wide in sums for part in (1, 2, 4)]
    outs = (
        (shape((rows, width), bfloat16), anywhere),
        (shape((rows, width), float32), anywhere),
        (shape((rows, width), float32), anywhere),
        (shape((2 * width // 8, width), bfloat16), anywhere),
        (shape((width // 8, 3 * width), bfloat16), anywhere),
        (shape((width // 8, width), bfloat16), anywhere),
        (shape((4, 2, width // 8, hidden // 8), bfloat16), anywhere),
        (shape((hidden // 8, width), bfloat16), anywhere),
        (shape((4, 16, 2 * width), bfloat16), anywhere),
        (shape((4, 16, width), bfloat16), anywhere),
    )
    parts = pl.pallas_call(
        layer_kernel,
        out_shape=tuple(item[0] for item in outs),
        in_specs=[smem, smem] + [anywhere] * 11,
        out_specs=tuple(item[1] for item in outs),
        scratch_shapes=[
            low(*w_out.shape), low(*w_up.shape), low(*w_down.shape), low(8 * rows, 2 * width),
            low(8, rows, width), low(8, rows, width), low(8, rows, width // 2), low(8, rows, width // 2),
            low(8, rows, width), low(8, rows, 512), low(8, rows, 512), low(8, rows, 256),
            low(3, 8, rows, 256), low(8, rows, 256),
            low(rows, width), low(rows, width), pltpu.VMEM((1, rows), jnp.int32), low(1, 8 * width),
            low(rows, width), low(16, width), pltpu.VMEM((8, 8, rows), jnp.int32),
            full(16, 2 * width), low(8, rows, 384), low(8, rows, 384), low(8, rows, 128), low(8, rows, 128),
            full(8 * rows, 128), full(rows, width), full(rows, width), full(rows, hidden), low(rows, width),
            low(rows, hidden), low(rows, hidden), full(rows, width), full(rows, width),
            full(rows, width), low(rows, width), low(8, rows, 128), low(8, rows, 128), low(8, rows, 256), low(rows, 3 * width), low(rows, width), full(8 * rows, 128),
            full(16, 2 * width), low(4, 16, 2 * width), low(3, 16, 2 * width),
            low(2, rows, 512),
            *sum_scratch,
            dma((168,)), dma((168,)), dma((28,)),
        ],
        compiler_params=pltpu.CompilerParams(
            collective_id=0, has_side_effects=True, vmem_limit_bytes=60 * MIB
        ),
        name="layer",
    )(
        lengths, time_step, frame_mask, frames[0], skip[0], cotangent[0], biases, w_skip, w_ada,
        w_qkv, w_out, w_up, w_down,
    )

    last_outs = (
        (shape((rows, width), bfloat16), anywhere),
        (shape((rows, width), float32), anywhere),
        (shape((rows, width), float32), anywhere),
        (shape((2 * width // 8, width), float32), anywhere),
        (shape((width // 8, 2 * width), float32), anywhere),
        (shape((1, 2 * width // 8), float32), vmem),
        (shape((width // 8, 3 * width), float32), anywhere),
        (shape((width // 8, width), float32), anywhere),
        (shape((1, width // 8), float32), vmem),
        (shape((width // 8, hidden), float32), anywhere),
        (shape((1, hidden // 8), float32), vmem),
        (shape((hidden // 8, width), float32), anywhere),
        (shape((1, width // 8), float32), vmem),
    )
    scratch = [pltpu.VMEM(item[0].shape, item[0].dtype) for item in outs]
    scratch += [full(*last_outs[number][0].shape) for number in (3, 4, 6, 7, 9, 11)]
    widened = pl.pallas_call(
        widen_kernel,
        out_shape=tuple(item[0] for item in last_outs),
        in_specs=[anywhere] * len(outs),
        out_specs=tuple(item[1] for item in last_outs),
        scratch_shapes=[*scratch, dma((10,)), dma((12,))],
        compiler_params=pltpu.CompilerParams(vmem_limit_bytes=60 * MIB),
        name="widen",
    )(*parts)
    return tuple(
        item[None] if number < 3 else item.reshape(-1) if item.shape[0] == 1 else item
        for number, item in enumerate(widened)
    )


def solution(mesh):
    placed = (
        P("dp", "seq", None),
        P("dp", "seq", None),
        P("dp", None),
        P("dp", "seq"),
        P("dp", None),
        P(),
        P(),
        P(),
        P(),
        P(),
        P(),
        P(),
        P(),
        P(),
        P(),
        P("dp", "seq", None),
    )
    split_heads = mesh.shape["dp"] == 4 and mesh.shape["seq"] == len(RELATIVE)
    return jax.shard_map(
        one_kernel if split_heads else on_device,
        mesh=mesh,
        in_specs=placed,
        out_specs=(
            P("dp", "seq", None),
            P("dp", "seq", None),
            P("dp", "seq", None),
            P("seq", None),
            P("seq", None),
            P("seq"),
            P("seq", None),
            P("seq", None),
            P("seq"),
            P("seq", None),
            P("seq"),
            P("seq", None),
            P("seq"),
        ),
        check_vma=False,
    )
```

```python
import math

import jax
import jax.numpy as jnp
from jax import lax
from jax.experimental import pallas as pl
from jax.experimental.pallas import tpu as pltpu
from jax.sharding import PartitionSpec as P

HEADS = 16
HEAD = 64
TSTEPS = 32


precise = lax.Precision.HIGHEST
masked_score = -1e30
contract_rows = (((0,), (0,)), ((), ()))
contract_cols = (((1,), (1,)), ((), ()))


def divisor_below(count_all, upper_limit):
    size_now = min(count_all, upper_limit)
    while count_all % size_now:
        size_now -= 1
    return size_now


def normalize(values):
    centered = values - jnp.mean(values, axis=-1, keepdims=True)
    variance = jnp.mean(centered * centered, axis=-1, keepdims=True)
    return centered * lax.rsqrt(variance + 1e-06)


def segment_of(lengths, frame_index):
    utter_ends = jnp.cumsum(lengths)
    return jnp.sum((frame_index[:, None] >= utter_ends[None, :]).astype(jnp.int32), axis=1)


def utterance_layout(lengths, frame_index):
    utter_ends = jnp.cumsum(lengths)
    starts = utter_ends - lengths
    segment = segment_of(lengths, frame_index)
    member = segment[:, None] == jnp.arange(lengths.shape[0], dtype=jnp.int32)[None, :]
    position = frame_index - jnp.sum(jnp.where(member, starts[None, :], 0), axis=1)
    return (segment, position, member)


def rotary_tables(position, head_size):
    half_size = head_size // 2
    frequency = jnp.exp(
        jnp.arange(half_size, dtype=jnp.float32) * (-2.0 * math.log(10000.0) / head_size)
    )
    angles = position.astype(jnp.float32)[:, None] * frequency[None, :]
    return (jnp.cos(angles)[:, None, :], jnp.sin(angles)[:, None, :])


def rotate(values, cos_table, sin_table):
    half_size = values.shape[-1] // 2
    first_half = values[..., :half_size]
    second_half = values[..., half_size:]
    return jnp.concatenate(
        [
            first_half * cos_table - second_half * sin_table,
            second_half * cos_table + first_half * sin_table,
        ],
        axis=-1,
    )


def rotate_back(values, cos_table, sin_table):
    half_size = values.shape[-1] // 2
    first_half = values[..., :half_size]
    second_half = values[..., half_size:]
    return jnp.concatenate(
        [
            first_half * cos_table + second_half * sin_table,
            second_half * cos_table - first_half * sin_table,
        ],
        axis=-1,
    )


def time_embedding(steps, model_width):
    half_size = model_width // 2
    flow_time = steps.astype(jnp.float32) / TSTEPS
    frequency = jnp.exp(jnp.arange(half_size, dtype=jnp.float32) * (-math.log(10000.0) / half_size))
    angles = 1000.0 * flow_time[:, None] * frequency[None, :]
    return jnp.concatenate([jnp.sin(angles), jnp.cos(angles)], axis=1)


def make_attend(query_low, query_segment, query_index, lengths):
    count_rows, head_count, head_size = query_low.shape
    scale_factor = 1.0 / math.sqrt(head_size)

    def attend(running, key_piece, first_row):
        keys_part, values_part, valid_part = key_piece
        count_keys = keys_part.shape[0]
        block_rows = divisor_below(count_keys, 1024)
        block_count = count_keys // block_rows
        key_blocks = keys_part.reshape(block_count, block_rows, head_count, head_size)
        value_blocks = values_part.reshape(block_count, block_rows, head_count, head_size)
        valid_blocks = valid_part.reshape(block_count, block_rows)
        offsets = first_row + jnp.arange(block_count, dtype=jnp.int32) * block_rows

        def attend_block_step(carried, inputs):
            row_top, row_total, weighted = carried
            key_block, value_block, valid_block, offset = inputs
            key_index = offset + jnp.arange(block_rows, dtype=jnp.int32)
            key_segment = segment_of(lengths, key_index)
            allowed = (query_segment[:, None] == key_segment[None, :]) & (
                (valid_block[None, :] > 0) | (query_index[:, None] == key_index[None, :])
            )
            scores = (
                jnp.einsum("qhd,khd->hqk", query_low, key_block, preferred_element_type=jnp.float32)
                * scale_factor
            )
            scores = jnp.where(allowed[None], scores, masked_score)
            new_top = jnp.maximum(row_top, jnp.max(scores, axis=2))
            weights = jnp.where(allowed[None], jnp.exp(scores - new_top[:, :, None]), 0.0)
            factor = jnp.exp(row_top - new_top)
            row_total = row_total * factor + jnp.sum(weights, axis=2)
            weighted = weighted * jnp.transpose(factor)[:, :, None] + jnp.einsum(
                "hqk,khd->qhd",
                weights.astype(jnp.bfloat16),
                value_block,
                preferred_element_type=jnp.float32,
            )
            return ((new_top, row_total, weighted), None)

        result_state, unused = lax.scan(
            attend_block_step, running, (key_blocks, value_blocks, valid_blocks, offsets)
        )
        return result_state

    return attend


def key_sweep(
    query_low, grad_attn, log_total, row_delta, query_segment, query_index, lengths, key_tuple
):
    keys_all, values_all, valid_all = key_tuple
    count_rows, head_count, head_size = query_low.shape
    scale_factor = 1.0 / math.sqrt(head_size)
    count_keys = keys_all.shape[0]
    block_rows = divisor_below(count_keys, 1024)
    block_count = count_keys // block_rows
    key_blocks = keys_all.reshape(block_count, block_rows, head_count, head_size)
    value_blocks = values_all.reshape(block_count, block_rows, head_count, head_size)
    valid_blocks = valid_all.reshape(block_count, block_rows)
    offsets = jnp.arange(block_count, dtype=jnp.int32) * block_rows
    top_shift = jnp.transpose(log_total)[:, :, None]
    delta_shift = jnp.transpose(row_delta)[:, :, None]

    def key_block_step(grad_query, inputs):
        key_block, value_block, valid_block, offset = inputs
        key_index = offset + jnp.arange(block_rows, dtype=jnp.int32)
        key_segment = segment_of(lengths, key_index)
        allowed = (query_segment[:, None] == key_segment[None, :]) & (
            (valid_block[None, :] > 0) | (query_index[:, None] == key_index[None, :])
        )
        scores = (
            jnp.einsum("qhd,khd->hqk", query_low, key_block, preferred_element_type=jnp.float32)
            * scale_factor
        )
        weights = jnp.where(allowed[None], jnp.exp(scores - top_shift), 0.0)
        grad_weights = jnp.einsum(
            "qhd,khd->hqk", grad_attn, value_block, preferred_element_type=jnp.float32
        )
        grad_scores = (weights * (grad_weights - delta_shift)).astype(jnp.bfloat16)
        grad_query = (
            grad_query
            + jnp.einsum("hqk,khd->qhd", grad_scores, key_block, preferred_element_type=jnp.float32)
            * scale_factor
        )
        grad_key = (
            jnp.einsum("hqk,qhd->khd", grad_scores, query_low, preferred_element_type=jnp.float32)
            * scale_factor
        )
        grad_value = jnp.einsum(
            "hqk,qhd->khd",
            weights.astype(jnp.bfloat16),
            grad_attn,
            preferred_element_type=jnp.float32,
        )
        return (grad_query, (grad_key, grad_value))

    start_grad = jnp.zeros((count_rows, head_count, head_size), jnp.float32)
    return lax.scan(key_block_step, start_grad, (key_blocks, value_blocks, valid_blocks, offsets))


def on_device(
    frames,
    skip,
    lengths,
    frame_mask,
    time_step,
    w_skip,
    w_ada,
    b_ada,
    w_qkv,
    w_out,
    norm_gain,
    w_up,
    b_up,
    w_down,
    b_down,
    cotangent,
):
    local_frames = frames[0]
    local_skip = skip[0]
    row_lengths = lengths[0]
    count_rows, model_width = local_frames.shape
    head_count = HEADS
    head_size = HEAD
    row_base = lax.axis_index("seq") * count_rows
    frame_index = row_base + jnp.arange(count_rows, dtype=jnp.int32)
    segment, position, member = utterance_layout(row_lengths, frame_index)
    member_float = member.astype(jnp.float32)
    embed_low = time_embedding(time_step[0], model_width).astype(jnp.bfloat16)
    ada_table = jnp.dot(embed_low, w_ada, preferred_element_type=jnp.float32) + b_ada.astype(
        jnp.float32
    )
    ada_frame = jnp.dot(member_float, ada_table, precision=precise)
    scale_part = ada_frame[:, :model_width]
    shift_part = ada_frame[:, model_width:]
    joined = jnp.concatenate([local_frames, local_skip], axis=1)
    residual_in = jnp.dot(joined, w_skip, preferred_element_type=jnp.float32)
    norm_first, first_pull = jax.vjp(normalize, residual_in)
    first_low = (norm_first * (1.0 + scale_part) + shift_part).astype(jnp.bfloat16)
    packed = jnp.dot(first_low, w_qkv, preferred_element_type=jnp.float32)
    cos_table, sin_table = rotary_tables(position, head_size)
    query_low = rotate(
        packed[:, :model_width].reshape(count_rows, head_count, head_size), cos_table, sin_table
    ).astype(jnp.bfloat16)
    keys_low = (
        rotate(
            packed[:, model_width : 2 * model_width].reshape(count_rows, head_count, head_size),
            cos_table,
            sin_table,
        )
        .astype(jnp.bfloat16)
        .reshape(count_rows, model_width)
    )
    values_low = packed[:, 2 * model_width :].astype(jnp.bfloat16)
    valid_low = frame_mask[0].astype(jnp.bfloat16)
    attend = make_attend(query_low, segment, frame_index, row_lengths)
    start_state = (
        jnp.full((head_count, count_rows), masked_score, jnp.float32),
        jnp.zeros((head_count, count_rows), jnp.float32),
        jnp.zeros((count_rows, head_count, head_size), jnp.float32),
    )
    gathered = (
        lax.all_gather(keys_low, "seq", axis=0, tiled=True),
        lax.all_gather(values_low, "seq", axis=0, tiled=True),
        lax.all_gather(valid_low, "seq", axis=0, tiled=True),
    )
    row_top, row_total, weighted = attend(start_state, gathered, 0)
    attn_sum = weighted / jnp.transpose(row_total)[:, :, None]
    log_total = jnp.transpose(row_top + jnp.log(row_total))
    attn_low = attn_sum.reshape(count_rows, model_width).astype(jnp.bfloat16)
    residual_mid = residual_in + jnp.dot(attn_low, w_out, preferred_element_type=jnp.float32)
    gain_float = norm_gain.astype(jnp.float32)
    second_float, second_pull = jax.vjp(
        lambda hidden, gain_vector: normalize(hidden) * gain_vector, residual_mid, gain_float
    )
    second_low = second_float.astype(jnp.bfloat16)
    upper_sum = jnp.dot(second_low, w_up, preferred_element_type=jnp.float32) + b_up.astype(
        jnp.float32
    )
    gated_float, gelu_pull = jax.vjp(
        lambda hidden: jax.nn.gelu(hidden, approximate=True), upper_sum
    )
    gated_low = gated_float.astype(jnp.bfloat16)
    output = (
        residual_mid
        + jnp.dot(gated_low, w_down, preferred_element_type=jnp.float32)
        + b_down.astype(jnp.float32)
    )
    grad_out = cotangent[0]
    grad_out_float = grad_out.astype(jnp.float32)
    grad_down = lax.dot_general(
        gated_low, grad_out, contract_rows, preferred_element_type=jnp.float32
    )
    grad_down_bias = jnp.sum(grad_out_float, axis=0)
    grad_gated = lax.dot_general(
        grad_out, w_down, contract_cols, preferred_element_type=jnp.float32
    )
    grad_upper = gelu_pull(grad_gated)[0].astype(jnp.bfloat16)
    grad_up = lax.dot_general(
        second_low, grad_upper, contract_rows, preferred_element_type=jnp.float32
    )
    grad_up_bias = jnp.sum(grad_upper.astype(jnp.float32), axis=0)
    grad_second = lax.dot_general(
        grad_upper, w_up, contract_cols, preferred_element_type=jnp.float32
    )
    grad_mid_norm, grad_gain = second_pull(grad_second)
    grad_mid = grad_out_float + grad_mid_norm
    grad_branch = grad_mid.astype(jnp.bfloat16)
    grad_out_weight = lax.dot_general(
        attn_low, grad_branch, contract_rows, preferred_element_type=jnp.float32
    )
    grad_attn = (
        lax.dot_general(grad_branch, w_out, contract_cols, preferred_element_type=jnp.float32)
        .astype(jnp.bfloat16)
        .reshape(count_rows, head_count, head_size)
    )
    row_delta = jnp.sum(grad_attn.astype(jnp.float32) * attn_sum, axis=2)
    grad_query, key_parts = key_sweep(
        query_low, grad_attn, log_total, row_delta, segment, frame_index, row_lengths, gathered
    )
    grad_key_all, grad_value_all = key_parts
    total_keys = grad_key_all.shape[0] * grad_key_all.shape[1]
    grad_key, grad_value = (
        lax.psum_scatter(
            grad_key_all.reshape(total_keys, model_width), "seq", scatter_dimension=0, tiled=True
        ),
        lax.psum_scatter(
            grad_value_all.reshape(total_keys, model_width), "seq", scatter_dimension=0, tiled=True
        ),
    )
    grad_key = rotate_back(
        grad_key.reshape(count_rows, head_count, head_size), cos_table, sin_table
    ).reshape(count_rows, model_width)
    grad_query = rotate_back(grad_query, cos_table, sin_table).reshape(count_rows, model_width)
    grad_packed = jnp.concatenate([grad_query, grad_key, grad_value], axis=1).astype(jnp.bfloat16)
    grad_qkv = lax.dot_general(
        first_low, grad_packed, contract_rows, preferred_element_type=jnp.float32
    )
    grad_first = lax.dot_general(
        grad_packed, w_qkv, contract_cols, preferred_element_type=jnp.float32
    )
    grad_ada_frame = jnp.concatenate([grad_first * norm_first, grad_first], axis=1)
    grad_ada_table = lax.dot_general(member_float, grad_ada_frame, contract_rows, precision=precise)
    grad_ada = lax.dot_general(
        embed_low.astype(jnp.float32), grad_ada_table, contract_rows, precision=precise
    )
    grad_ada_bias = jnp.sum(grad_ada_table, axis=0)
    grad_in = (grad_mid + first_pull(grad_first * (1.0 + scale_part))[0]).astype(jnp.bfloat16)
    grad_skip_weight = lax.dot_general(
        joined, grad_in, contract_rows, preferred_element_type=jnp.float32
    )
    grad_joined = lax.dot_general(
        grad_in, w_skip, contract_cols, preferred_element_type=jnp.float32
    )
    (
        share_skip,
        share_ada,
        share_ada_bias,
        share_qkv,
        share_out,
        share_gain,
        share_up,
        share_up_bias,
        share_down,
        share_down_bias,
    ) = (
        lax.psum_scatter(grad_skip_weight, "seq", scatter_dimension=0, tiled=True),
        lax.psum_scatter(grad_ada, "seq", scatter_dimension=0, tiled=True),
        lax.psum_scatter(grad_ada_bias, "seq", scatter_dimension=0, tiled=True),
        lax.psum_scatter(grad_qkv, "seq", scatter_dimension=0, tiled=True),
        lax.psum_scatter(grad_out_weight, "seq", scatter_dimension=0, tiled=True),
        lax.psum_scatter(grad_gain, "seq", scatter_dimension=0, tiled=True),
        lax.psum_scatter(grad_up, "seq", scatter_dimension=0, tiled=True),
        lax.psum_scatter(grad_up_bias, "seq", scatter_dimension=0, tiled=True),
        lax.psum_scatter(grad_down, "seq", scatter_dimension=0, tiled=True),
        lax.psum_scatter(grad_down_bias, "seq", scatter_dimension=0, tiled=True),
    )
    (
        total_skip,
        total_ada,
        total_ada_bias,
        total_qkv,
        total_out,
        total_gain,
        total_up,
        total_up_bias,
        total_down,
        total_down_bias,
    ) = (
        lax.psum(share_skip.astype(jnp.bfloat16), "dp").astype(jnp.float32),
        lax.psum(share_ada.astype(jnp.bfloat16), "dp").astype(jnp.float32),
        lax.psum(share_ada_bias.astype(jnp.bfloat16), "dp").astype(jnp.float32),
        lax.psum(share_qkv.astype(jnp.bfloat16), "dp").astype(jnp.float32),
        lax.psum(share_out.astype(jnp.bfloat16), "dp").astype(jnp.float32),
        lax.psum(share_gain.astype(jnp.bfloat16), "dp").astype(jnp.float32),
        lax.psum(share_up.astype(jnp.bfloat16), "dp").astype(jnp.float32),
        lax.psum(share_up_bias.astype(jnp.bfloat16), "dp").astype(jnp.float32),
        lax.psum(share_down.astype(jnp.bfloat16), "dp").astype(jnp.float32),
        lax.psum(share_down_bias.astype(jnp.bfloat16), "dp").astype(jnp.float32),
    )
    return (
        output.astype(jnp.bfloat16)[None],
        grad_joined[:, :model_width][None],
        grad_joined[:, model_width:][None],
        total_skip,
        total_ada,
        total_ada_bias,
        total_qkv,
        total_out,
        total_gain,
        total_up,
        total_up_bias,
        total_down,
        total_down_bias,
    )


RELATIVE = (0, 6, 2, 4, 1, 7, 3, 5)
PAIRS = (0, 3, 1, 2)
MESH = pl.DeviceIdType.MESH
MIB = 2**20
FAR_FIRST = (4, 5, 2, 3, 6, 7, 1)
GROUP = ((2, 0), (0, 1), (2, 1), (3, 0), (3, 1), (1, 1), (1, 0))
ROOT = math.sqrt(2.0 / math.pi)


def bit(value, place):
    return lax.rem(lax.div(value, jnp.int32(1 << place)), jnp.int32(2))


def flip(value, mask):
    out = value
    for place in range(3):
        if (mask >> place) & 1:
            out = out + (1 << place) * (1 - 2 * bit(value, place))
    return out


def exclusive(value, other):
    return sum(
        (1 << place) * lax.rem(bit(value, place) + bit(other, place), jnp.int32(2))
        for place in range(3)
    )


def columns(start, size):
    return pl.ds(pl.multiple_of(start, 128), size)


class Links:
    def __init__(self, send_sems, recv_sems, load_sems):
        self.send_sems, self.recv_sems, self.load_sems = send_sems, recv_sems, load_sems
        self.used, self.loads, self.sent = 0, 0, []
        self.dp_index, self.seq_index = lax.axis_index("dp"), lax.axis_index("seq")

    def peer(self, dp_mask, seq_mask):
        return (flip(self.dp_index, dp_mask), flip(self.seq_index, seq_mask))

    def barrier(self):
        semaphore = pltpu.get_barrier_semaphore()
        masks = [(0, mask) for mask in range(2, 8)] + list(GROUP)
        for mask in masks:
            pl.semaphore_signal(
                semaphore, inc=1, device_id=self.peer(*mask), device_id_type=MESH
            )
        return lambda: pl.semaphore_wait(semaphore, len(masks))

    def send(self, source, target, dp_mask, seq_mask):
        number = self.used
        self.used += 1
        copy = pltpu.make_async_remote_copy(
            src_ref=source,
            dst_ref=target,
            send_sem=self.send_sems.at[number],
            recv_sem=self.recv_sems.at[number],
            device_id=self.peer(dp_mask, seq_mask),
            device_id_type=MESH,
        )
        copy.start()
        self.sent.append(copy)
        return copy

    def load(self, source, target):
        copy = pltpu.make_async_copy(source, target, self.load_sems.at[self.loads])
        self.loads += 1
        copy.start()
        return copy

    def settle(self, copy):
        copy.wait()
        self.sent = [other for other in self.sent if other is not copy]

    def sent_done(self, copies):
        for copy in copies:
            copy.wait_send()
        self.sent = [other for other in self.sent if not any(other is copy for copy in copies)]

    def drain(self):
        for copy in self.sent:
            copy.wait_send()


class Share:
    def __init__(self, links, slots, near, far):
        self.links, self.slots = links, slots
        self.across = links.send(near, slots.at[2], 2, 0)
        self.beside = links.send(far, slots.at[4], 0, 1)
        self.corner = links.send(far, slots.at[6], 2, 1)
        self.waits = [links.send(near, slots.at[1], 1, 0)]

    def forward(self):
        for copy, slot in ((self.across, 2), (self.beside, 4), (self.corner, 6)):
            copy.wait_recv()
            self.waits.append(
                self.links.send(self.slots.at[slot], self.slots.at[slot + 1], 1, 0)
            )

    def wait(self):
        arrived(self.waits)


def arrived(copies):
    for copy in copies:
        copy.wait_recv()


def turn_sine_cosine(angles):
    turns = jnp.floor(angles * (0.5 / math.pi) + 0.5)
    rest = angles - turns * 6.28125
    rest = rest - turns * (2.0 * math.pi - 6.28125)
    return jnp.sin(rest), jnp.cos(rest)


def utterance_ends(lengths_ref):
    ends, total = [], jnp.int32(0)
    for number in range(lengths_ref.shape[1]):
        total = total + lengths_ref[0, number]
        ends.append(total)
    return ends


def segments(ends, index):
    return sum((index >= end).astype(jnp.int32) for end in ends)


def rotary(ends, first_row, rows, width):
    index = first_row + lax.broadcasted_iota(jnp.int32, (rows, width), 0)
    start = jnp.zeros_like(index)
    for end in ends:
        start = jnp.where(index >= end, end, start)
    lane = lax.broadcasted_iota(jnp.int32, (rows, width), 1) % HEAD
    pair = (lane % (HEAD // 2)).astype(jnp.float32)
    angles = (index - start).astype(jnp.float32) * jnp.exp(
        pair * (-2.0 * math.log(10000.0) / HEAD)
    )
    sine, cosine = turn_sine_cosine(angles)
    return cosine, jnp.where(lane < HEAD // 2, -sine, sine)


def partner(values):
    half_size = HEAD // 2
    lane = lax.broadcasted_iota(jnp.int32, values.shape, 1) % HEAD
    return jnp.where(
        lane < half_size,
        pltpu.roll(values, values.shape[1] - half_size, 1),
        pltpu.roll(values, half_size, 1),
    )


def head_mask(values, head):
    lane = lax.broadcasted_iota(jnp.int32, values.shape, 1)
    return jnp.where(lane // HEAD == head, values, jnp.zeros_like(values))


def norm_parts(values):
    centered = values - jnp.mean(values, axis=-1, keepdims=True)
    variance = jnp.mean(centered * centered, axis=-1, keepdims=True)
    factor = lax.rsqrt(variance + 1e-06)
    return centered * factor, factor


def norm_back(grad, normal, factor):
    mean_grad = jnp.mean(grad, axis=-1, keepdims=True)
    mean_product = jnp.mean(grad * normal, axis=-1, keepdims=True)
    return factor * (grad - mean_grad - normal * mean_product)


def product(left, right):
    return jnp.dot(left, right, preferred_element_type=jnp.float32)


def product_cols(left, right):
    return lax.dot_general(left, right, contract_cols, preferred_element_type=jnp.float32)


def product_rows(left, right):
    return lax.dot_general(left, right, contract_rows, preferred_element_type=jnp.float32)


def gelu_parts(upper):
    square = upper * upper
    bent = jnp.tanh(ROOT * (upper + 0.044715 * upper * square))
    value = 0.5 * upper * (1.0 + bent)
    slope = 0.5 * (1.0 + bent) + 0.5 * upper * (1.0 - bent * bent) * ROOT * (
        1.0 + 3.0 * 0.044715 * square
    )
    return value, slope


class Sum:
    def __init__(
        self, links, left, right, total, into_a, into_b, place=None, beside=None
    ):
        self.links, self.left, self.right, self.total = links, left, right, total
        self.into_a, self.into_b, self.place, self.beside = into_a, into_b, place, beside
        self.size = total.shape[0] // 4

    def piece(self, source):
        depth = self.left.shape[0] * self.left.shape[1]
        return product_rows(
            self.left[:, :, columns(source, 256)].reshape(depth, 256),
            self.right[...].reshape(depth, self.right.shape[2]),
        )

    def fill(self, low, high):
        def step(number, carried):
            start = pl.multiple_of(number * 256, 256)
            source = start if self.place is None else self.place(number)
            made = self.piece(source)
            if self.beside is not None:
                made = made + self.beside[1][pl.ds(start, 256), :].astype(jnp.float32)
            self.total[pl.ds(start, 256), :] = made.astype(jnp.bfloat16)
            return carried

        lax.fori_loop(low // 256, high // 256, step, 0)

    def begin_beside(self):
        out, into = self.beside

        def step(number, carried):
            start = pl.multiple_of(number * 256, 256)
            out[pl.ds(start, 256), :] = self.piece(4 * self.size + start).astype(jnp.bfloat16)
            return carried

        lax.fori_loop(0, 4 * self.size // 256, step, 0)
        self.beside_copy = self.links.send(out, into, 0, 1)

    def begin(self):
        if self.beside is not None:
            self.beside_copy.wait_recv()
        self.fill(2 * self.size, 4 * self.size)
        self.copy = self.links.send(self.total.at[2 * self.size :], self.into_a, 0, 2)

    def keep(self):
        self.fill(0, 2 * self.size)

    def second(self):
        self.links.settle(self.copy)
        both = pl.ds(0, 2 * self.size)
        self.total[both, :] = (
            self.total[both, :].astype(jnp.float32) + self.into_a[...].astype(jnp.float32)
        ).astype(jnp.bfloat16)
        self.copy = self.links.send(
            self.total.at[self.size : 2 * self.size], self.into_b, 0, 6
        )

    def third(self):
        self.copy.wait_recv()
        self.ready = self.total.at[2 * self.size : 3 * self.size]
        self.ready[...] = (
            self.total[: self.size, :].astype(jnp.float32) + self.into_b[...].astype(jnp.float32)
        ).astype(jnp.bfloat16)

    def gather(self, ready, place):
        self.target = place
        own = place(self.links.dp_index)
        self.across = self.links.send(ready, own, 2, 0)
        self.core = self.links.send(ready, own, 1, 0)
        self.own = self.links.load(ready, own)

    def spread(self):
        self.across.wait_recv()
        other = self.target(flip(self.links.dp_index, 2))
        self.far = self.links.send(other, other, 1, 0)

    def finish(self):
        self.own.wait()
        arrived([self.core, self.far])


def layer_kernel(
    lengths, steps, mask_in, frames_in, skip_frames_in, cot_in, bias_in, w_skip, w_ada, w_qkv, w_out,
    w_up, w_down,
    result, grad_frames, grad_skip, sum_skip, sum_qkv, sum_out, sum_up, sum_down, small_all,
    embed_all,
    out_buf, up_buf, down_buf, weight_buf,
    joined_all, cot_all, first_all, attn_all, second_all, gated_all, upper_all, branch_all,
    packed_all, in_all,
    frames, skip, frame_mask, biases,
    first_own, embed_own, masks, table, packed_send, packed, attn_send, attn_low,
    attn_sum, residual, scale, grad_gated, second_low, gated, upper_parts, residual_mid, normal_mid,
    grad_mid, branch, grad_heads, query_recv, pair_recv, grad_packed, grad_in,
    query_total, turns, small, small_send, small_recv, up_ready,
    down_sum, down_a, down_b, up_sum, up_a, up_b, out_sum, out_a, out_b, skip_sum, skip_a, skip_b, skip_out, skip_beside,
    query_sum, query_a, query_b, key_sum, key_a, key_b, value_sum, value_a, value_b,
    send_sems, recv_sems, load_sems,
):
    links = Links(send_sems, recv_sems, load_sems)
    seq_index, dp_index = links.seq_index, links.dp_index
    rows, width = frames.shape
    hidden = grad_gated.shape[1]
    float32, bfloat16 = jnp.float32, jnp.bfloat16
    odd = bit(seq_index, 0)
    load_frames = links.load(frames_in, frames)
    load_skip_frames = links.load(skip_frames_in, skip)
    load_mask = links.load(mask_in, frame_mask)
    load_bias = links.load(bias_in, biases)
    load_skip = links.load(w_skip, down_buf.at[: 2 * width])
    load_ada = links.load(w_ada, weight_buf)
    enter = links.barrier()
    load_qkv = links.load(w_qkv, up_buf.at[:, : 3 * width])
    load_cot = links.load(cot_in, cot_all.at[0])
    cotangent = cot_all.at[0]

    def relative(source, target, size):
        for number, mask in enumerate(RELATIVE):
            target[:, number * size : (number + 1) * size] = source(flip(seq_index, mask))

    def joined_block(place):
        inside = columns(lax.rem(place, jnp.int32(4)) * 256, 256)
        return jnp.where(place < 4, frames[:, inside], skip[:, inside])

    ends = utterance_ends(lengths)
    utter = lax.broadcasted_iota(jnp.int32, embed_own.shape, 0)
    flow = jnp.zeros(embed_own.shape, float32)
    for number in range(steps.shape[1]):
        flow = jnp.where(utter == number, steps[0, number].astype(float32), flow)
    lane = lax.broadcasted_iota(jnp.int32, embed_own.shape, 1)
    half = width // 2
    frequency = jnp.exp((lane % half).astype(float32) * (-math.log(10000.0) / half))
    sine, cosine = turn_sine_cosine(1000.0 * (flow / TSTEPS) * frequency)
    embed = jnp.where(lane < half, sine, cosine)
    embed_own[...] = jnp.where(utter < steps.shape[1], embed, 0.0).astype(bfloat16)
    first_row = seq_index * rows
    cos_own, sin_own = rotary(ends, first_row, rows, 256)
    load_frames.wait()
    load_skip_frames.wait()
    relative(joined_block, joined_all.at[0], 256)
    load_mask.wait()
    masks[0] = jnp.broadcast_to(frame_mask[...], masks.shape[1:])
    load_cot.wait()
    enter()
    mask_copies = [links.send(masks.at[0], masks.at[m], 0, m) for m in range(1, 8)]
    cot_share = Share(links, cot_all, cotangent, cotangent)
    joined_across = links.send(joined_all.at[0], joined_all.at[2], 2, 0)
    joined_core = links.send(joined_all.at[0], joined_all.at[1], 1, 0)
    load_bias.wait()
    load_skip.wait()
    residual[...] = product(frames[...], down_buf[:width]) + product(
        skip[...], down_buf[width : 2 * width]
    )
    load_ada.wait()
    table[...] = product(embed_own[...], weight_buf[...]) + biases[:, : 2 * width].astype(float32)
    normal, unused = norm_parts(residual[...])
    row_index = first_row + lax.broadcasted_iota(jnp.int32, (rows, 1), 0)
    own_segment = segments(ends, row_index)
    spread_scale = jnp.zeros((rows, width), float32)
    spread_shift = jnp.zeros((rows, width), float32)
    for number in range(len(ends)):
        member = own_segment == number
        spread_scale = jnp.where(member, table[number : number + 1, :width], spread_scale)
        spread_shift = jnp.where(member, table[number : number + 1, width:], spread_shift)
    scale[...] = spread_scale
    second_low[...] = (normal * (1.0 + spread_scale) + spread_shift).astype(bfloat16)
    load_qkv.wait()
    packed_copies, later = [], []
    for far in (2, 1, 3, 0):
        pair = flip(lax.div(seq_index, jnp.int32(2)), far)
        parts = []
        for kind in range(3):
            part = product(second_low[...], up_buf[:, columns(kind * width + pair * 256, 256)])
            if kind < 2:
                part = part * cos_own + partner(part) * sin_own
            parts.append(part.astype(bfloat16))
        for side in range(2):
            for kind in range(3):
                packed_send[pair * 2 + side, :, kind * 128 : (kind + 1) * 128] = parts[kind][
                    :, side * 128 : (side + 1) * 128
                ]
        for mask in (2 * far, 2 * far + 1):
            if mask:
                place = flip(seq_index, mask)
                packed_copies.append(
                    links.send(
                        packed_send.at[place, :, :256], packed.at[seq_index, :, :256], 0, mask
                    )
                )
                later.append((place, mask))
    value_copies = [
        links.send(packed_send.at[place, :, 256:], packed.at[seq_index, :, 256:], 0, mask)
        for place, mask in later
    ]
    load_down_low = links.load(w_down.at[: 2 * width], down_buf.at[: 2 * width])
    load_down_high = links.load(w_down.at[2 * width :], down_buf.at[2 * width :])
    load_out = links.load(w_out, out_buf)
    load_up = links.load(w_up, up_buf)
    packed[seq_index] = packed_send[seq_index]
    relative(lambda place: second_low[:, columns(place * 128, 128)], first_own, 128)
    first_all[0] = first_own[:, : width // 2]
    embed_copies = [links.send(embed_own, embed_all.at[dp_index], m, 0) for m in (1, 2, 3)]
    embed_load = links.load(embed_own, embed_all.at[dp_index])
    load_down_low.wait()
    load_down_high.wait()

    def gated_step(step, carried):
        part = columns(step * 512, 512)
        grad_gated[:, part] = product_cols(cotangent[...], down_buf[part, :])
        return carried

    lax.fori_loop(0, hidden // 512, gated_step, 0)

    def table_step(place, carried):
        here = pl.ds(pl.multiple_of(place * rows, rows), rows)
        cosine, sine = rotary(ends, place * rows, rows, 128)
        turns[here, :128] = cosine
        turns[here, 128:] = sine
        return carried

    lax.fori_loop(0, 8, table_step, 0)
    arrived(mask_copies)
    arrived(packed_copies)
    key_index = lax.broadcasted_iota(jnp.int32, (1, 8 * rows), 1)
    key_segment = segments(ends, key_index)
    key_valid = jnp.concatenate(
        [masks[exclusive(seq_index, jnp.int32(number))][:1] for number in range(8)], axis=1
    )

    def weigh(place, carried):
        query = packed[place, :, :128]
        row_index = place * rows + lax.broadcasted_iota(jnp.int32, (rows, 1), 0)
        allowed = (segments(ends, row_index) == key_segment) & (
            (key_valid > 0) | (row_index == key_index)
        )
        keys = packed[:, :, 128:256].reshape(8 * rows, 128)
        here = pl.ds(pl.multiple_of(place * rows, rows), rows)
        for head in range(2):
            scores = product_cols(head_mask(query, head), keys) * (1.0 / math.sqrt(HEAD))
            scores = jnp.where(allowed, scores, masked_score)
            raised = jnp.exp(scores - jnp.max(scores, axis=1, keepdims=True))
            low = (raised / jnp.sum(raised, axis=1, keepdims=True)).astype(bfloat16)
            weight_buf[here, head * 1024 : (head + 1) * 1024] = low
        return carried

    def attend(place):
        values = packed[:, :, 256:].reshape(8 * rows, 128)
        total = jnp.zeros((rows, 128), float32)
        here = pl.ds(pl.multiple_of(place * rows, rows), rows)
        for head in range(2):
            low = weight_buf[here, head * 1024 : (head + 1) * 1024]
            total = total + product(low, head_mask(values, head))
        attn_sum[here, :] = total
        attn_send[place] = total.astype(bfloat16)

    def by_frames(source, target):
        base = links.used
        links.used += 8

        def copy_of(mask):
            place = exclusive(seq_index, mask)
            return pltpu.make_async_remote_copy(
                src_ref=source.at[place],
                dst_ref=target.at[seq_index],
                send_sem=send_sems.at[base + mask],
                recv_sem=recv_sems.at[base + mask],
                device_id=(dp_index, place),
                device_id_type=MESH,
            )

        return copy_of

    attn_copy = by_frames(attn_send, attn_low)

    def attend_step(step, carried):
        mask = lax.rem(step + 4, jnp.int32(8))
        attend(exclusive(seq_index, mask))
        attn_copy(mask).start()
        return carried

    lax.fori_loop(0, 8, weigh, 0)
    arrived(value_copies)
    lax.fori_loop(0, 4, attend_step, 0)
    lax.fori_loop(5, 8, attend_step, 0)
    attend(seq_index)
    attn_low[seq_index] = attn_send[seq_index]
    load_out.wait()
    for mask in range(1, 8):
        attn_copy(jnp.int32(mask)).wait()
    joined_attn = jnp.concatenate([attn_low[number] for number in range(8)], axis=1)
    residual_mid[...] = residual[...] + product(joined_attn, out_buf[...])
    normal, factor_mid = norm_parts(residual_mid[...])
    normal_mid[...] = normal
    gain_float = biases[:, 7 * width : 8 * width].astype(float32)
    second_all[0] = (normal * gain_float).astype(bfloat16)
    second_share = Share(links, second_all, second_all.at[0], second_all.at[0])
    cot_share.forward()
    small[8:] = jnp.zeros((8, small.shape[1]), float32)
    load_up.wait()

    def up_step(step, carried):
        part = columns(step * 512, 512)
        upper = product(second_all[0], up_buf[:, part]) + biases[
            :, columns(2 * width + step * 512, 512)
        ].astype(float32)
        value, slope = gelu_parts(upper)
        grad_upper = (grad_gated[:, part] * slope).astype(bfloat16)
        gated[:, part] = value.astype(bfloat16)
        upper_parts[:, part] = grad_upper
        small[
            pl.ds(8 + lax.div(step, jnp.int32(4)), 1),
            columns(lax.rem(step, jnp.int32(4)) * 512, 512),
        ] = jnp.sum(grad_upper.astype(float32), axis=0, keepdims=True)
        return carried

    lax.fori_loop(0, hidden // 512, up_step, 0)

    def second_step(step, total):
        part = columns(step * 512, 512)
        return total + product_cols(upper_parts[:, part], up_buf[:, part])

    grad_second = lax.fori_loop(
        0, hidden // 512, second_step, jnp.zeros((rows, width), float32)
    )
    grad_out = cotangent[...].astype(float32)
    normal = normal_mid[...]
    small[10:11, :width] = jnp.sum(grad_second * normal, axis=0, keepdims=True)
    small[10:11, width:] = jnp.sum(grad_out, axis=0, keepdims=True)
    grad_mid[...] = grad_out + norm_back(grad_second * gain_float, normal, factor_mid)
    branch[...] = grad_mid[...].astype(bfloat16)
    grad_attn = product_cols(branch[...], out_buf[...]).astype(bfloat16)
    grad_send = attn_send
    for number in range(8):
        grad_send[number] = grad_attn[:, number * 128 : (number + 1) * 128]
    head_copies = [
        links.send(grad_send.at[flip(seq_index, m)], grad_heads.at[seq_index], 0, m)
        for m in FAR_FIRST
    ]
    grad_heads[seq_index] = grad_send[seq_index]

    def quarters(source, slots, group=GROUP):
        size = slots.shape[2]
        slots[0] = source[:, columns(dp_index * size, size)]
        return [
            links.send(
                source.at[:, columns(flip(dp_index, m) * size, size)], slots.at[4 * v + m], m, v
            )
            for m, v in group
        ]

    second_share.forward()
    branch_copies = quarters(branch, branch_all)
    attn_own = upper_parts.at[:, 2 * width : 3 * width]
    relative(lambda place: attn_low[place], attn_own, 128)
    attn_all[0] = attn_own[:, : width // 2]
    attn_share = Share(links, attn_all, attn_all.at[0], attn_own.at[:, width // 2 :])
    cot_share.wait()
    joined_across.wait_recv()
    joined_far = links.send(joined_all.at[2], joined_all.at[3], 1, 0)
    second_share.wait()

    def again(first):
        units, spots = [], []
        for number in (first, first + 1):
            place = flip(seq_index, RELATIVE[number])
            units.append(place * 512 + dp_index * 128)
            spots.append(lax.div(place, jnp.int32(2)))
        weight_up = jnp.concatenate([up_buf[:, columns(unit, 128)] for unit in units], axis=1)
        weight_down = jnp.concatenate([down_buf[columns(unit, 128), :] for unit in units], axis=0)
        bias = jnp.concatenate(
            [biases[:, columns(2 * width + unit, 128)] for unit in units], axis=1
        ).astype(float32)

        def again_step(step, carried):
            both = pl.ds(2 * step, 2)
            upper = product(second_all[both].reshape(2 * rows, width), weight_up) + bias
            value, slope = gelu_parts(upper)
            grad = product_cols(cot_all[both].reshape(2 * rows, width), weight_down)
            gated_all[both, :, first * 128 : (first + 2) * 128] = value.astype(bfloat16).reshape(
                2, rows, 256
            )
            grad_upper = (grad * slope).astype(bfloat16).reshape(2, rows, 256)
            for side in range(2):
                upper_all[both, :, columns(spots[side] * 128, 128)] = grad_upper[
                    :, :, side * 128 : (side + 1) * 128
                ]
            return carried

        lax.fori_loop(0, 4, again_step, 0)

    def pair_place(number):
        base_pair = lax.div(seq_index, jnp.int32(2))
        step_a, step_b = lax.div(number, jnp.int32(2)), lax.rem(number, jnp.int32(2))
        two = jnp.int32(2)
        low_bit = lax.rem(bit(base_pair, 0) + step_a + step_b, two)
        high_bit = lax.rem(bit(base_pair, 1) + step_b, two)
        return (2 * high_bit + low_bit) * 256

    down = Sum(links, gated_all, cot_all, down_sum, down_a, down_b)
    up = Sum(links, second_all, upper_all, up_sum, up_a, up_b, pair_place)
    out = Sum(links, attn_all, branch_all, out_sum, out_a, out_b)
    query_part = Sum(links, first_all, packed_all.at[0], query_sum, query_a, query_b)
    key_part = Sum(links, first_all, packed_all.at[1], key_sum, key_a, key_b)
    value_part = Sum(links, first_all, packed_all.at[2], value_sum, value_a, value_b)
    skip_part = Sum(
        links, joined_all, in_all, skip_sum, skip_a, skip_b, beside=(skip_out, skip_beside)
    )
    again(2)
    down.begin()
    arrived(head_copies)
    links.sent_done(packed_copies + value_copies)
    links.sent_done(head_copies)
    query_send = attn_send
    pair_send = packed_send.at[:, :, :256]
    first_share = Share(links, first_all, first_all.at[0], first_own.at[:, width // 2 :])
    pair_copy = by_frames(pair_send, pair_recv)
    shrink = 1.0 / math.sqrt(HEAD)
    query_total[...] = jnp.zeros_like(query_total)

    def delta_step(place, carried):
        here = pl.ds(pl.multiple_of(place * rows, rows), rows)
        both = grad_heads[place].astype(float32) * attn_sum[here, :]
        for head in range(2):
            delta = jnp.sum(head_mask(both, head), axis=1, keepdims=True)
            grad_gated[:, columns(place * 512 + 256 + head * 128, 128)] = jnp.broadcast_to(
                delta, (rows, 128)
            )
        return carried

    lax.fori_loop(0, 8, delta_step, 0)

    def turned_back(total, place):
        here = pl.ds(pl.multiple_of(place * rows, rows), rows)
        cosine, sine = turns[here, :128], turns[here, 128:]
        total = total * shrink
        return (total * cosine - partner(total) * sine).astype(bfloat16)

    def back(pair):
        both = pl.ds(2 * pair, 2)
        keys = packed[both, :, 128:256].reshape(2 * rows, 128)
        values = packed[both, :, 256:].reshape(2 * rows, 128)
        queries = packed[:, :, :128].reshape(8 * rows, 128)
        grad = grad_heads[...].reshape(8 * rows, 128)
        grad_keys = jnp.zeros((2 * rows, 128), float32)
        grad_values = jnp.zeros((2 * rows, 128), float32)
        for head in range(2):
            low = weight_buf[:, columns(head * 1024 + pair * 256, 256)]
            grad_head = head_mask(grad, head)
            delta = jnp.concatenate(
                [
                    grad_gated[:, place * 512 + 256 + head * 128 : place * 512 + 384 + head * 128]
                    for place in range(8)
                ],
                axis=0,
            )
            delta = jnp.concatenate([delta, delta], axis=1)
            grad_scores = (
                low.astype(float32) * (product_cols(grad_head, values) - delta)
            ).astype(bfloat16)
            query_total[...] += product(grad_scores, head_mask(keys, head))
            grad_keys = grad_keys + product_rows(grad_scores, head_mask(queries, head))
            grad_values = grad_values + product_rows(low, grad_head)
        for side in range(2):
            place = 2 * pair + side
            part = slice(side * rows, (side + 1) * rows)
            pair_send[place, :, :128] = turned_back(grad_keys[part], place)
            pair_send[place, :, 128:] = grad_values[part].astype(bfloat16)

    own_pair = lax.div(seq_index, jnp.int32(2))

    def back_step(step, carried):
        far = step + 2 - 3 * lax.div(step, jnp.int32(2))
        back(lax.div(exclusive(seq_index, 2 * far), jnp.int32(2)))
        pair_copy(2 * far).start()
        pair_copy(2 * far + 1).start()
        return carried

    lax.fori_loop(0, 3, back_step, 0)
    back(own_pair)
    pair_copy(jnp.int32(1)).start()
    pair_recv[seq_index] = pair_send[seq_index]

    def query_step(place, carried):
        here = pl.ds(pl.multiple_of(place * rows, rows), rows)
        query_send[place] = turned_back(query_total[here, :], place)
        return carried

    lax.fori_loop(0, 8, query_step, 0)
    query_copies = [
        links.send(query_send.at[flip(seq_index, m)], query_recv.at[seq_index], 0, m)
        for m in FAR_FIRST
    ]
    query_recv[seq_index] = query_send[seq_index]
    again(0)
    load_qkv = links.load(w_qkv, up_buf.at[:, : 3 * width])
    up.begin()
    down.keep()

    def down_step(step, total):
        part = columns(step * 512, 512)
        return total + product(gated[:, part], down_buf[part, :])

    lower = lax.fori_loop(
        0,
        hidden // 512,
        down_step,
        residual_mid[...] + biases[:, 6 * width : 7 * width].astype(float32),
    )
    second_low[...] = lower.astype(bfloat16)
    out_loads = [links.load(second_low, result)]
    load_skip = links.load(w_skip, down_buf.at[: 2 * width])
    for mask in range(1, 8):
        pair_copy(jnp.int32(mask)).wait()
    for number in range(8):
        for kind in (1, 2):
            grad_packed[:, kind * width + number * 128 : kind * width + (number + 1) * 128] = (
                pair_recv[number, :, (kind - 1) * 128 : kind * 128]
            )
    key_parts = quarters(grad_packed.at[:, width : 2 * width], packed_all.at[1])
    value_parts = quarters(grad_packed.at[:, 2 * width :], packed_all.at[2])
    load_qkv.wait()

    def first_step(step, total):
        part = columns(step * 512, 512)
        return total + product_cols(grad_packed[:, part], up_buf[:, part])

    grad_first = lax.fori_loop(2, 6, first_step, jnp.zeros((rows, width), float32))
    scale_normal, factor = norm_parts(residual[...])
    down.second()
    arrived(query_copies)
    for number in range(8):
        grad_packed[:, number * 128 : (number + 1) * 128] = query_recv[number]
    grad_first = lax.fori_loop(0, 2, first_step, grad_first)
    grad_in[...] = (
        grad_mid[...] + norm_back(grad_first * (1.0 + scale[...]), scale_normal, factor)
    ).astype(bfloat16)
    in_copies = quarters(grad_in, in_all, ((2, 0), (3, 0), (1, 0)))
    query_parts = quarters(grad_packed.at[:, :width], packed_all.at[0])
    attn_share.forward()
    first_share.forward()
    up.keep()
    arrived(branch_copies)
    attn_share.wait()
    out.begin()
    out.keep()
    up.second()
    first_share.wait()
    arrived([joined_core, joined_far] + in_copies)
    skip_part.begin_beside()
    arrived(key_parts)
    key_part.begin()
    key_part.keep()
    arrived(value_parts)
    value_part.begin()
    value_part.keep()
    out.second()
    scaled = grad_first * scale_normal
    for number in range(len(ends)):
        member = own_segment == number
        small[number : number + 1, :width] = jnp.sum(
            jnp.where(member, scaled, 0.0), axis=0, keepdims=True
        )
        small[number : number + 1, width:] = jnp.sum(
            jnp.where(member, grad_first, 0.0), axis=0, keepdims=True
        )

    def small_start(number, mask):
        small_send[number] = small[...].astype(bfloat16)
        return links.send(small_send.at[number], small_recv.at[number], 0, mask)

    def small_add(copy, number):
        copy.wait_recv()
        small[...] = small_send[number].astype(float32) + small_recv[number].astype(float32)

    small_copy = small_start(0, 1)
    by_rows = lambda target, size: lambda index: target.at[pl.ds(index * size, size), :]
    by_cols = lambda start, target: lambda index: target.at[:, columns(start + index * 256, 256)]
    down.third()
    down.gather(down.ready, by_rows(sum_down, 128))
    arrived(query_parts)
    query_part.begin()
    query_part.keep()
    key_part.second()
    skip_part.begin()
    skip_part.keep()
    value_part.second()
    small_add(small_copy, 0)
    small_copy = small_start(1, 2)
    up.third()
    up_ready[odd] = up.ready[pl.ds(pl.multiple_of(odd * 128, 128), 128), :]
    up_other = links.send(
        up.ready.at[pl.ds(pl.multiple_of((1 - odd) * 128, 128), 128), :], up_ready.at[odd], 0, 1
    )
    out.third()
    out.gather(out.ready, by_cols(0, sum_out))
    down.spread()
    load_skip.wait()
    for held, target, start in ((residual, grad_frames, 0), (normal_mid, grad_skip, width)):
        held[...] = product_cols(grad_in[...], down_buf[start : start + width, :])
        out_loads.append(links.load(held, target))
    query_part.second()
    skip_part.second()
    small_add(small_copy, 1)
    small_copy = small_start(2, 6)
    up_other.wait_recv()
    up.gather(up_ready, lambda index: sum_up.at[index])
    out.spread()
    key_part.third()
    key_part.gather(key_part.ready, by_cols(width, sum_qkv))
    value_part.third()
    value_part.gather(value_part.ready, by_cols(2 * width, sum_qkv))
    query_part.third()
    query_part.gather(query_part.ready, by_cols(0, sum_qkv))
    skip_part.third()
    skip_part.gather(skip_part.ready, by_cols(0, sum_skip))
    small_add(small_copy, 2)
    small_send[3] = small[...].astype(bfloat16)
    small_copies = [
        links.send(small_send.at[3], small_all.at[dp_index], m, 0) for m in (3, 2, 1)
    ]
    small_load = links.load(small_send.at[3], small_all.at[dp_index])
    for each in (up, key_part, value_part, query_part, skip_part):
        each.spread()
    small_load.wait()
    embed_load.wait()
    for load in out_loads:
        load.wait()
    arrived(small_copies + embed_copies)
    for each in (down, up, out, query_part, key_part, skip_part, value_part):
        each.finish()
    links.drain()


def widen_kernel(
    result_in, frames_in, skip_in, sum_skip, sum_qkv, sum_out, sum_up, sum_down, small_all, embed_all,
    result, grad_frames, grad_skip, out_skip, out_ada, out_ada_bias, out_qkv, out_out, out_gain,
    out_up, out_up_bias, out_down, out_down_bias,
    low_result, low_frames, low_skip, low_w_skip, low_qkv, low_out, low_up, low_down, low_small, low_embed,
    full_skip, full_ada, full_qkv, full_out, full_up, full_down, in_sems, out_sems,
):
    float32 = jnp.float32
    seq_index = lax.axis_index("seq")
    sources = (sum_up, sum_down, sum_qkv, sum_skip, small_all, embed_all, sum_out, result_in, frames_in, skip_in)
    inside = (low_up, low_down, low_qkv, low_w_skip, low_small, low_embed, low_out, low_result, low_frames, low_skip)
    loads = [
        pltpu.make_async_copy(source, target, in_sems.at[number])
        for number, (source, target) in enumerate(zip(sources, inside, strict=True))
    ]
    for load in loads:
        load.start()
    stores = []

    def store(source, target):
        copy = pltpu.make_async_copy(source, target, out_sems.at[len(stores)])
        copy.start()
        stores.append(copy)

    loads[0].wait()
    for quarter in range(4):
        for side in range(2):
            for level in range(4):
                start = (2 * level + side) * 512 + quarter * 128
                full_up[:, start : start + 128] = low_up[
                    quarter, side, :, level * 128 : (level + 1) * 128
                ].astype(float32)
    store(full_up, out_up)
    for number, low, full, out in (
        (1, low_down, full_down, out_down),
        (2, low_qkv, full_qkv, out_qkv),
        (3, low_w_skip, full_skip, out_skip),
    ):
        loads[number].wait()
        full[...] = low[...].astype(float32)
        store(full, out)
    loads[4].wait()
    loads[5].wait()
    size = full_ada.shape[0]
    own = low_embed[:, :, columns(seq_index * size, size)].reshape(-1, size)
    full_ada[...] = product_rows(own, low_small[...].reshape(own.shape[0], full_ada.shape[1]))
    store(full_ada, out_ada)
    loads[6].wait()
    full_out[...] = low_out[...].astype(float32)
    store(full_out, out_out)
    for number, low, out in ((7, low_result, result), (8, low_frames, grad_frames), (9, low_skip, grad_skip)):
        loads[number].wait()
        store(low, out)
    wide = low_small.shape[2]
    spot = columns(seq_index * 256, 256)
    bias = jnp.zeros((1, 256), float32)
    for number in range(4):
        bias = bias + jnp.sum(low_small[number, :8, spot].astype(float32), axis=0, keepdims=True)
    out_ada_bias[...] = bias
    upper = jnp.zeros((1, 512), float32)
    gain = jnp.zeros((1, 128), float32)
    down_bias = jnp.zeros((1, 128), float32)
    high = lax.div(seq_index, jnp.int32(4))
    for number in range(4):
        both = low_small[number, 8:, columns(lax.rem(seq_index, jnp.int32(4)) * 512, 512)].astype(float32)
        upper = upper + jnp.where(high == 0, both[:1], both[1:2])
        gain = gain + low_small[number, 8:, columns(seq_index * 128, 128)].astype(float32)[2:3]
        down_bias = down_bias + low_small[number, 8:, columns(wide // 2 + seq_index * 128, 128)].astype(float32)[2:3]
    out_up_bias[...] = upper
    out_gain[...] = gain
    out_down_bias[...] = down_bias
    for copy in stores:
        copy.wait()


def one_kernel(
    frames, skip, lengths, frame_mask, time_step, w_skip, w_ada, b_ada, w_qkv, w_out, norm_gain,
    w_up, b_up, w_down, b_down, cotangent,
):
    rows, width = frames.shape[1:]
    hidden = b_up.shape[0]
    float32, bfloat16 = jnp.float32, jnp.bfloat16
    shape = jax.ShapeDtypeStruct
    vmem = pl.BlockSpec(memory_space=pltpu.VMEM)
    smem = pl.BlockSpec(memory_space=pltpu.SMEM)
    anywhere = pl.BlockSpec(memory_space=pl.ANY)
    dma = pltpu.SemaphoreType.DMA
    low = lambda *size: pltpu.VMEM(size, bfloat16)
    full = lambda *size: pltpu.VMEM(size, float32)
    biases = jnp.concatenate([b_ada, b_up, b_down, norm_gain])[None]
    sums = ((512, 1024), (1024, 512), (512, 256), (1024, 256), (512, 256), (512, 256), (512, 256))
    sum_scratch = [low(tall // part, wide) for tall, wide in sums for part in (1, 2, 4)]
    sum_scratch[12:12] = [low(1024, 256), low(1024, 256)]
    outs = (
        (shape((rows, width), bfloat16), anywhere),
        (shape((rows, width), float32), anywhere),
        (shape((rows, width), float32), anywhere),
        (shape((2 * width // 8, width), bfloat16), anywhere),
        (shape((width // 8, 3 * width), bfloat16), anywhere),
        (shape((width // 8, width), bfloat16), anywhere),
        (shape((4, 2, width // 8, hidden // 8), bfloat16), anywhere),
        (shape((hidden // 8, width), bfloat16), anywhere),
        (shape((4, 16, 2 * width), bfloat16), anywhere),
        (shape((4, 16, width), bfloat16), anywhere),
    )
    parts = pl.pallas_call(
        layer_kernel,
        out_shape=tuple(item[0] for item in outs),
        in_specs=[smem, smem] + [anywhere] * 11,
        out_specs=tuple(item[1] for item in outs),
        scratch_shapes=[
            low(*w_out.shape), low(*w_up.shape), low(*w_down.shape), low(8 * rows, 2 * width),
            low(4, rows, 2 * width), low(8, rows, width), low(8, rows, width // 2), low(8, rows, width // 2),
            low(8, rows, width), low(8, rows, 512), low(8, rows, 512), low(8, rows, 256),
            low(3, 8, rows, 256), low(4, rows, 256),
            low(rows, width), low(rows, width), pltpu.VMEM((1, rows), jnp.int32), low(1, 8 * width),
            low(rows, width), low(16, width), pltpu.VMEM((8, 8, rows), jnp.int32),
            full(16, 2 * width), low(8, rows, 384), low(8, rows, 384), low(8, rows, 128), low(8, rows, 128),
            full(8 * rows, 128), full(rows, width), full(rows, width), full(rows, hidden), low(rows, width),
            low(rows, hidden), low(rows, hidden), full(rows, width), full(rows, width),
            full(rows, width), low(rows, width), low(8, rows, 128), low(8, rows, 128), low(8, rows, 256), low(rows, 3 * width), low(rows, width), full(8 * rows, 128), full(8 * rows, 256),
            full(16, 2 * width), low(4, 16, 2 * width), low(3, 16, 2 * width),
            low(2, rows, 512),
            *sum_scratch,
            dma((168,)), dma((168,)), dma((28,)),
        ],
        compiler_params=pltpu.CompilerParams(
            collective_id=0, has_side_effects=True, vmem_limit_bytes=62 * MIB
        ),
        name="layer",
    )(
        lengths, time_step, frame_mask, frames[0], skip[0], cotangent[0], biases, w_skip, w_ada,
        w_qkv, w_out, w_up, w_down,
    )

    last_outs = (
        (shape((rows, width), bfloat16), anywhere),
        (shape((rows, width), float32), anywhere),
        (shape((rows, width), float32), anywhere),
        (shape((2 * width // 8, width), float32), anywhere),
        (shape((width // 8, 2 * width), float32), anywhere),
        (shape((1, 2 * width // 8), float32), vmem),
        (shape((width // 8, 3 * width), float32), anywhere),
        (shape((width // 8, width), float32), anywhere),
        (shape((1, width // 8), float32), vmem),
        (shape((width // 8, hidden), float32), anywhere),
        (shape((1, hidden // 8), float32), vmem),
        (shape((hidden // 8, width), float32), anywhere),
        (shape((1, width // 8), float32), vmem),
    )
    scratch = [pltpu.VMEM(item[0].shape, item[0].dtype) for item in outs]
    scratch += [full(*last_outs[number][0].shape) for number in (3, 4, 6, 7, 9, 11)]
    widened = pl.pallas_call(
        widen_kernel,
        out_shape=tuple(item[0] for item in last_outs),
        in_specs=[anywhere] * len(outs),
        out_specs=tuple(item[1] for item in last_outs),
        scratch_shapes=[*scratch, dma((10,)), dma((12,))],
        compiler_params=pltpu.CompilerParams(vmem_limit_bytes=60 * MIB),
        name="widen",
    )(*parts)
    return tuple(
        item[None] if number < 3 else item.reshape(-1) if item.shape[0] == 1 else item
        for number, item in enumerate(widened)
    )


def solution(mesh):
    placed = (
        P("dp", "seq", None),
        P("dp", "seq", None),
        P("dp", None),
        P("dp", "seq"),
        P("dp", None),
        P(),
        P(),
        P(),
        P(),
        P(),
        P(),
        P(),
        P(),
        P(),
        P(),
        P("dp", "seq", None),
    )
    split_heads = mesh.shape["dp"] == 4 and mesh.shape["seq"] == len(RELATIVE)
    return jax.shard_map(
        one_kernel if split_heads else on_device,
        mesh=mesh,
        in_specs=placed,
        out_specs=(
            P("dp", "seq", None),
            P("dp", "seq", None),
            P("dp", "seq", None),
            P("seq", None),
            P("seq", None),
            P("seq"),
            P("seq", None),
            P("seq", None),
            P("seq"),
            P("seq", None),
            P("seq"),
            P("seq", None),
            P("seq"),
        ),
        check_vma=False,
    )
```

```python
import math

import jax
import jax.numpy as jnp
from jax import lax
from jax.experimental import pallas as pl
from jax.experimental.pallas import tpu as pltpu
from jax.sharding import PartitionSpec as P

HEADS = 16
HEAD = 64
TSTEPS = 32


precise = lax.Precision.HIGHEST
masked_score = -1e30
contract_rows = (((0,), (0,)), ((), ()))
contract_cols = (((1,), (1,)), ((), ()))


def divisor_below(count_all, upper_limit):
    size_now = min(count_all, upper_limit)
    while count_all % size_now:
        size_now -= 1
    return size_now


def normalize(values):
    centered = values - jnp.mean(values, axis=-1, keepdims=True)
    variance = jnp.mean(centered * centered, axis=-1, keepdims=True)
    return centered * lax.rsqrt(variance + 1e-06)


def segment_of(lengths, frame_index):
    utter_ends = jnp.cumsum(lengths)
    return jnp.sum((frame_index[:, None] >= utter_ends[None, :]).astype(jnp.int32), axis=1)


def utterance_layout(lengths, frame_index):
    utter_ends = jnp.cumsum(lengths)
    starts = utter_ends - lengths
    segment = segment_of(lengths, frame_index)
    member = segment[:, None] == jnp.arange(lengths.shape[0], dtype=jnp.int32)[None, :]
    position = frame_index - jnp.sum(jnp.where(member, starts[None, :], 0), axis=1)
    return (segment, position, member)


def rotary_tables(position, head_size):
    half_size = head_size // 2
    frequency = jnp.exp(
        jnp.arange(half_size, dtype=jnp.float32) * (-2.0 * math.log(10000.0) / head_size)
    )
    angles = position.astype(jnp.float32)[:, None] * frequency[None, :]
    return (jnp.cos(angles)[:, None, :], jnp.sin(angles)[:, None, :])


def rotate(values, cos_table, sin_table):
    half_size = values.shape[-1] // 2
    first_half = values[..., :half_size]
    second_half = values[..., half_size:]
    return jnp.concatenate(
        [
            first_half * cos_table - second_half * sin_table,
            second_half * cos_table + first_half * sin_table,
        ],
        axis=-1,
    )


def rotate_back(values, cos_table, sin_table):
    half_size = values.shape[-1] // 2
    first_half = values[..., :half_size]
    second_half = values[..., half_size:]
    return jnp.concatenate(
        [
            first_half * cos_table + second_half * sin_table,
            second_half * cos_table - first_half * sin_table,
        ],
        axis=-1,
    )


def time_embedding(steps, model_width):
    half_size = model_width // 2
    flow_time = steps.astype(jnp.float32) / TSTEPS
    frequency = jnp.exp(jnp.arange(half_size, dtype=jnp.float32) * (-math.log(10000.0) / half_size))
    angles = 1000.0 * flow_time[:, None] * frequency[None, :]
    return jnp.concatenate([jnp.sin(angles), jnp.cos(angles)], axis=1)


def make_attend(query_low, query_segment, query_index, lengths):
    count_rows, head_count, head_size = query_low.shape
    scale_factor = 1.0 / math.sqrt(head_size)

    def attend(running, key_piece, first_row):
        keys_part, values_part, valid_part = key_piece
        count_keys = keys_part.shape[0]
        block_rows = divisor_below(count_keys, 1024)
        block_count = count_keys // block_rows
        key_blocks = keys_part.reshape(block_count, block_rows, head_count, head_size)
        value_blocks = values_part.reshape(block_count, block_rows, head_count, head_size)
        valid_blocks = valid_part.reshape(block_count, block_rows)
        offsets = first_row + jnp.arange(block_count, dtype=jnp.int32) * block_rows

        def attend_block_step(carried, inputs):
            row_top, row_total, weighted = carried
            key_block, value_block, valid_block, offset = inputs
            key_index = offset + jnp.arange(block_rows, dtype=jnp.int32)
            key_segment = segment_of(lengths, key_index)
            allowed = (query_segment[:, None] == key_segment[None, :]) & (
                (valid_block[None, :] > 0) | (query_index[:, None] == key_index[None, :])
            )
            scores = (
                jnp.einsum("qhd,khd->hqk", query_low, key_block, preferred_element_type=jnp.float32)
                * scale_factor
            )
            scores = jnp.where(allowed[None], scores, masked_score)
            new_top = jnp.maximum(row_top, jnp.max(scores, axis=2))
            weights = jnp.where(allowed[None], jnp.exp(scores - new_top[:, :, None]), 0.0)
            factor = jnp.exp(row_top - new_top)
            row_total = row_total * factor + jnp.sum(weights, axis=2)
            weighted = weighted * jnp.transpose(factor)[:, :, None] + jnp.einsum(
                "hqk,khd->qhd",
                weights.astype(jnp.bfloat16),
                value_block,
                preferred_element_type=jnp.float32,
            )
            return ((new_top, row_total, weighted), None)

        result_state, unused = lax.scan(
            attend_block_step, running, (key_blocks, value_blocks, valid_blocks, offsets)
        )
        return result_state

    return attend


def key_sweep(
    query_low, grad_attn, log_total, row_delta, query_segment, query_index, lengths, key_tuple
):
    keys_all, values_all, valid_all = key_tuple
    count_rows, head_count, head_size = query_low.shape
    scale_factor = 1.0 / math.sqrt(head_size)
    count_keys = keys_all.shape[0]
    block_rows = divisor_below(count_keys, 1024)
    block_count = count_keys // block_rows
    key_blocks = keys_all.reshape(block_count, block_rows, head_count, head_size)
    value_blocks = values_all.reshape(block_count, block_rows, head_count, head_size)
    valid_blocks = valid_all.reshape(block_count, block_rows)
    offsets = jnp.arange(block_count, dtype=jnp.int32) * block_rows
    top_shift = jnp.transpose(log_total)[:, :, None]
    delta_shift = jnp.transpose(row_delta)[:, :, None]

    def key_block_step(grad_query, inputs):
        key_block, value_block, valid_block, offset = inputs
        key_index = offset + jnp.arange(block_rows, dtype=jnp.int32)
        key_segment = segment_of(lengths, key_index)
        allowed = (query_segment[:, None] == key_segment[None, :]) & (
            (valid_block[None, :] > 0) | (query_index[:, None] == key_index[None, :])
        )
        scores = (
            jnp.einsum("qhd,khd->hqk", query_low, key_block, preferred_element_type=jnp.float32)
            * scale_factor
        )
        weights = jnp.where(allowed[None], jnp.exp(scores - top_shift), 0.0)
        grad_weights = jnp.einsum(
            "qhd,khd->hqk", grad_attn, value_block, preferred_element_type=jnp.float32
        )
        grad_scores = (weights * (grad_weights - delta_shift)).astype(jnp.bfloat16)
        grad_query = (
            grad_query
            + jnp.einsum("hqk,khd->qhd", grad_scores, key_block, preferred_element_type=jnp.float32)
            * scale_factor
        )
        grad_key = (
            jnp.einsum("hqk,qhd->khd", grad_scores, query_low, preferred_element_type=jnp.float32)
            * scale_factor
        )
        grad_value = jnp.einsum(
            "hqk,qhd->khd",
            weights.astype(jnp.bfloat16),
            grad_attn,
            preferred_element_type=jnp.float32,
        )
        return (grad_query, (grad_key, grad_value))

    start_grad = jnp.zeros((count_rows, head_count, head_size), jnp.float32)
    return lax.scan(key_block_step, start_grad, (key_blocks, value_blocks, valid_blocks, offsets))


def on_device(
    frames,
    skip,
    lengths,
    frame_mask,
    time_step,
    w_skip,
    w_ada,
    b_ada,
    w_qkv,
    w_out,
    norm_gain,
    w_up,
    b_up,
    w_down,
    b_down,
    cotangent,
):
    local_frames = frames[0]
    local_skip = skip[0]
    row_lengths = lengths[0]
    count_rows, model_width = local_frames.shape
    head_count = HEADS
    head_size = HEAD
    row_base = lax.axis_index("seq") * count_rows
    frame_index = row_base + jnp.arange(count_rows, dtype=jnp.int32)
    segment, position, member = utterance_layout(row_lengths, frame_index)
    member_float = member.astype(jnp.float32)
    embed_low = time_embedding(time_step[0], model_width).astype(jnp.bfloat16)
    ada_table = jnp.dot(embed_low, w_ada, preferred_element_type=jnp.float32) + b_ada.astype(
        jnp.float32
    )
    ada_frame = jnp.dot(member_float, ada_table, precision=precise)
    scale_part = ada_frame[:, :model_width]
    shift_part = ada_frame[:, model_width:]
    joined = jnp.concatenate([local_frames, local_skip], axis=1)
    residual_in = jnp.dot(joined, w_skip, preferred_element_type=jnp.float32)
    norm_first, first_pull = jax.vjp(normalize, residual_in)
    first_low = (norm_first * (1.0 + scale_part) + shift_part).astype(jnp.bfloat16)
    packed = jnp.dot(first_low, w_qkv, preferred_element_type=jnp.float32)
    cos_table, sin_table = rotary_tables(position, head_size)
    query_low = rotate(
        packed[:, :model_width].reshape(count_rows, head_count, head_size), cos_table, sin_table
    ).astype(jnp.bfloat16)
    keys_low = (
        rotate(
            packed[:, model_width : 2 * model_width].reshape(count_rows, head_count, head_size),
            cos_table,
            sin_table,
        )
        .astype(jnp.bfloat16)
        .reshape(count_rows, model_width)
    )
    values_low = packed[:, 2 * model_width :].astype(jnp.bfloat16)
    valid_low = frame_mask[0].astype(jnp.bfloat16)
    attend = make_attend(query_low, segment, frame_index, row_lengths)
    start_state = (
        jnp.full((head_count, count_rows), masked_score, jnp.float32),
        jnp.zeros((head_count, count_rows), jnp.float32),
        jnp.zeros((count_rows, head_count, head_size), jnp.float32),
    )
    gathered = (
        lax.all_gather(keys_low, "seq", axis=0, tiled=True),
        lax.all_gather(values_low, "seq", axis=0, tiled=True),
        lax.all_gather(valid_low, "seq", axis=0, tiled=True),
    )
    row_top, row_total, weighted = attend(start_state, gathered, 0)
    attn_sum = weighted / jnp.transpose(row_total)[:, :, None]
    log_total = jnp.transpose(row_top + jnp.log(row_total))
    attn_low = attn_sum.reshape(count_rows, model_width).astype(jnp.bfloat16)
    residual_mid = residual_in + jnp.dot(attn_low, w_out, preferred_element_type=jnp.float32)
    gain_float = norm_gain.astype(jnp.float32)
    second_float, second_pull = jax.vjp(
        lambda hidden, gain_vector: normalize(hidden) * gain_vector, residual_mid, gain_float
    )
    second_low = second_float.astype(jnp.bfloat16)
    upper_sum = jnp.dot(second_low, w_up, preferred_element_type=jnp.float32) + b_up.astype(
        jnp.float32
    )
    gated_float, gelu_pull = jax.vjp(
        lambda hidden: jax.nn.gelu(hidden, approximate=True), upper_sum
    )
    gated_low = gated_float.astype(jnp.bfloat16)
    output = (
        residual_mid
        + jnp.dot(gated_low, w_down, preferred_element_type=jnp.float32)
        + b_down.astype(jnp.float32)
    )
    grad_out = cotangent[0]
    grad_out_float = grad_out.astype(jnp.float32)
    grad_down = lax.dot_general(
        gated_low, grad_out, contract_rows, preferred_element_type=jnp.float32
    )
    grad_down_bias = jnp.sum(grad_out_float, axis=0)
    grad_gated = lax.dot_general(
        grad_out, w_down, contract_cols, preferred_element_type=jnp.float32
    )
    grad_upper = gelu_pull(grad_gated)[0].astype(jnp.bfloat16)
    grad_up = lax.dot_general(
        second_low, grad_upper, contract_rows, preferred_element_type=jnp.float32
    )
    grad_up_bias = jnp.sum(grad_upper.astype(jnp.float32), axis=0)
    grad_second = lax.dot_general(
        grad_upper, w_up, contract_cols, preferred_element_type=jnp.float32
    )
    grad_mid_norm, grad_gain = second_pull(grad_second)
    grad_mid = grad_out_float + grad_mid_norm
    grad_branch = grad_mid.astype(jnp.bfloat16)
    grad_out_weight = lax.dot_general(
        attn_low, grad_branch, contract_rows, preferred_element_type=jnp.float32
    )
    grad_attn = (
        lax.dot_general(grad_branch, w_out, contract_cols, preferred_element_type=jnp.float32)
        .astype(jnp.bfloat16)
        .reshape(count_rows, head_count, head_size)
    )
    row_delta = jnp.sum(grad_attn.astype(jnp.float32) * attn_sum, axis=2)
    grad_query, key_parts = key_sweep(
        query_low, grad_attn, log_total, row_delta, segment, frame_index, row_lengths, gathered
    )
    grad_key_all, grad_value_all = key_parts
    total_keys = grad_key_all.shape[0] * grad_key_all.shape[1]
    grad_key, grad_value = (
        lax.psum_scatter(
            grad_key_all.reshape(total_keys, model_width), "seq", scatter_dimension=0, tiled=True
        ),
        lax.psum_scatter(
            grad_value_all.reshape(total_keys, model_width), "seq", scatter_dimension=0, tiled=True
        ),
    )
    grad_key = rotate_back(
        grad_key.reshape(count_rows, head_count, head_size), cos_table, sin_table
    ).reshape(count_rows, model_width)
    grad_query = rotate_back(grad_query, cos_table, sin_table).reshape(count_rows, model_width)
    grad_packed = jnp.concatenate([grad_query, grad_key, grad_value], axis=1).astype(jnp.bfloat16)
    grad_qkv = lax.dot_general(
        first_low, grad_packed, contract_rows, preferred_element_type=jnp.float32
    )
    grad_first = lax.dot_general(
        grad_packed, w_qkv, contract_cols, preferred_element_type=jnp.float32
    )
    grad_ada_frame = jnp.concatenate([grad_first * norm_first, grad_first], axis=1)
    grad_ada_table = lax.dot_general(member_float, grad_ada_frame, contract_rows, precision=precise)
    grad_ada = lax.dot_general(
        embed_low.astype(jnp.float32), grad_ada_table, contract_rows, precision=precise
    )
    grad_ada_bias = jnp.sum(grad_ada_table, axis=0)
    grad_in = (grad_mid + first_pull(grad_first * (1.0 + scale_part))[0]).astype(jnp.bfloat16)
    grad_skip_weight = lax.dot_general(
        joined, grad_in, contract_rows, preferred_element_type=jnp.float32
    )
    grad_joined = lax.dot_general(
        grad_in, w_skip, contract_cols, preferred_element_type=jnp.float32
    )
    (
        share_skip,
        share_ada,
        share_ada_bias,
        share_qkv,
        share_out,
        share_gain,
        share_up,
        share_up_bias,
        share_down,
        share_down_bias,
    ) = (
        lax.psum_scatter(grad_skip_weight, "seq", scatter_dimension=0, tiled=True),
        lax.psum_scatter(grad_ada, "seq", scatter_dimension=0, tiled=True),
        lax.psum_scatter(grad_ada_bias, "seq", scatter_dimension=0, tiled=True),
        lax.psum_scatter(grad_qkv, "seq", scatter_dimension=0, tiled=True),
        lax.psum_scatter(grad_out_weight, "seq", scatter_dimension=0, tiled=True),
        lax.psum_scatter(grad_gain, "seq", scatter_dimension=0, tiled=True),
        lax.psum_scatter(grad_up, "seq", scatter_dimension=0, tiled=True),
        lax.psum_scatter(grad_up_bias, "seq", scatter_dimension=0, tiled=True),
        lax.psum_scatter(grad_down, "seq", scatter_dimension=0, tiled=True),
        lax.psum_scatter(grad_down_bias, "seq", scatter_dimension=0, tiled=True),
    )
    (
        total_skip,
        total_ada,
        total_ada_bias,
        total_qkv,
        total_out,
        total_gain,
        total_up,
        total_up_bias,
        total_down,
        total_down_bias,
    ) = (
        lax.psum(share_skip.astype(jnp.bfloat16), "dp").astype(jnp.float32),
        lax.psum(share_ada.astype(jnp.bfloat16), "dp").astype(jnp.float32),
        lax.psum(share_ada_bias.astype(jnp.bfloat16), "dp").astype(jnp.float32),
        lax.psum(share_qkv.astype(jnp.bfloat16), "dp").astype(jnp.float32),
        lax.psum(share_out.astype(jnp.bfloat16), "dp").astype(jnp.float32),
        lax.psum(share_gain.astype(jnp.bfloat16), "dp").astype(jnp.float32),
        lax.psum(share_up.astype(jnp.bfloat16), "dp").astype(jnp.float32),
        lax.psum(share_up_bias.astype(jnp.bfloat16), "dp").astype(jnp.float32),
        lax.psum(share_down.astype(jnp.bfloat16), "dp").astype(jnp.float32),
        lax.psum(share_down_bias.astype(jnp.bfloat16), "dp").astype(jnp.float32),
    )
    return (
        output.astype(jnp.bfloat16)[None],
        grad_joined[:, :model_width][None],
        grad_joined[:, model_width:][None],
        total_skip,
        total_ada,
        total_ada_bias,
        total_qkv,
        total_out,
        total_gain,
        total_up,
        total_up_bias,
        total_down,
        total_down_bias,
    )


RELATIVE = (0, 6, 2, 4, 1, 7, 3, 5)
PAIRS = (0, 3, 1, 2)
MESH = pl.DeviceIdType.MESH
MIB = 2**20
FAR_FIRST = (4, 5, 2, 3, 6, 7, 1)
GROUP = ((2, 0), (0, 1), (2, 1), (3, 0), (3, 1), (1, 1), (1, 0))
ROOT = math.sqrt(2.0 / math.pi)


def bit(value, place):
    return lax.rem(lax.div(value, jnp.int32(1 << place)), jnp.int32(2))


def flip(value, mask):
    out = value
    for place in range(3):
        if (mask >> place) & 1:
            out = out + (1 << place) * (1 - 2 * bit(value, place))
    return out


def exclusive(value, other):
    return sum(
        (1 << place) * lax.rem(bit(value, place) + bit(other, place), jnp.int32(2))
        for place in range(3)
    )


def columns(start, size):
    return pl.ds(pl.multiple_of(start, 128), size)


class Links:
    def __init__(self, send_sems, recv_sems, load_sems):
        self.send_sems, self.recv_sems, self.load_sems = send_sems, recv_sems, load_sems
        self.used, self.loads, self.sent = 0, 0, []
        self.dp_index, self.seq_index = lax.axis_index("dp"), lax.axis_index("seq")

    def peer(self, dp_mask, seq_mask):
        return (flip(self.dp_index, dp_mask), flip(self.seq_index, seq_mask))

    def barrier(self):
        semaphore = pltpu.get_barrier_semaphore()
        masks = [(0, mask) for mask in range(2, 8)] + list(GROUP)
        for mask in masks:
            pl.semaphore_signal(
                semaphore, inc=1, device_id=self.peer(*mask), device_id_type=MESH
            )
        return lambda: pl.semaphore_wait(semaphore, len(masks))

    def send(self, source, target, dp_mask, seq_mask):
        number = self.used
        self.used += 1
        copy = pltpu.make_async_remote_copy(
            src_ref=source,
            dst_ref=target,
            send_sem=self.send_sems.at[number],
            recv_sem=self.recv_sems.at[number],
            device_id=self.peer(dp_mask, seq_mask),
            device_id_type=MESH,
        )
        copy.start()
        self.sent.append(copy)
        return copy

    def load(self, source, target):
        copy = pltpu.make_async_copy(source, target, self.load_sems.at[self.loads])
        self.loads += 1
        copy.start()
        return copy

    def settle(self, copy):
        copy.wait()
        self.sent = [other for other in self.sent if other is not copy]

    def sent_done(self, copies):
        for copy in copies:
            copy.wait_send()
        self.sent = [other for other in self.sent if not any(other is copy for copy in copies)]

    def drain(self):
        for copy in self.sent:
            copy.wait_send()


class Share:
    def __init__(self, links, slots, near, far):
        self.links, self.slots = links, slots
        self.across = links.send(near, slots.at[2], 2, 0)
        self.beside = links.send(far, slots.at[4], 0, 1)
        self.corner = links.send(far, slots.at[6], 2, 1)
        self.waits = [links.send(near, slots.at[1], 1, 0)]

    def forward(self):
        for copy, slot in ((self.across, 2), (self.beside, 4), (self.corner, 6)):
            copy.wait_recv()
            self.waits.append(
                self.links.send(self.slots.at[slot], self.slots.at[slot + 1], 1, 0)
            )

    def wait(self):
        arrived(self.waits)


def arrived(copies):
    for copy in copies:
        copy.wait_recv()


def turn_sine_cosine(angles):
    turns = jnp.floor(angles * (0.5 / math.pi) + 0.5)
    rest = angles - turns * 6.28125
    rest = rest - turns * (2.0 * math.pi - 6.28125)
    return jnp.sin(rest), jnp.cos(rest)


def utterance_ends(lengths_ref):
    ends, total = [], jnp.int32(0)
    for number in range(lengths_ref.shape[1]):
        total = total + lengths_ref[0, number]
        ends.append(total)
    return ends


def segments(ends, index):
    return sum((index >= end).astype(jnp.int32) for end in ends)


def rotary(ends, first_row, rows, width):
    index = first_row + lax.broadcasted_iota(jnp.int32, (rows, width), 0)
    start = jnp.zeros_like(index)
    for end in ends:
        start = jnp.where(index >= end, end, start)
    lane = lax.broadcasted_iota(jnp.int32, (rows, width), 1) % HEAD
    pair = (lane % (HEAD // 2)).astype(jnp.float32)
    angles = (index - start).astype(jnp.float32) * jnp.exp(
        pair * (-2.0 * math.log(10000.0) / HEAD)
    )
    sine, cosine = turn_sine_cosine(angles)
    return cosine, jnp.where(lane < HEAD // 2, -sine, sine)


def partner(values):
    half_size = HEAD // 2
    lane = lax.broadcasted_iota(jnp.int32, values.shape, 1) % HEAD
    return jnp.where(
        lane < half_size,
        pltpu.roll(values, values.shape[1] - half_size, 1),
        pltpu.roll(values, half_size, 1),
    )


def head_mask(values, head):
    lane = lax.broadcasted_iota(jnp.int32, values.shape, 1)
    return jnp.where(lane // HEAD == head, values, jnp.zeros_like(values))


def norm_parts(values):
    centered = values - jnp.mean(values, axis=-1, keepdims=True)
    variance = jnp.mean(centered * centered, axis=-1, keepdims=True)
    factor = lax.rsqrt(variance + 1e-06)
    return centered * factor, factor


def norm_back(grad, normal, factor):
    mean_grad = jnp.mean(grad, axis=-1, keepdims=True)
    mean_product = jnp.mean(grad * normal, axis=-1, keepdims=True)
    return factor * (grad - mean_grad - normal * mean_product)


def product(left, right):
    return jnp.dot(left, right, preferred_element_type=jnp.float32)


def product_cols(left, right):
    return lax.dot_general(left, right, contract_cols, preferred_element_type=jnp.float32)


def product_rows(left, right):
    return lax.dot_general(left, right, contract_rows, preferred_element_type=jnp.float32)


def gelu_parts(upper):
    square = upper * upper
    bent = jnp.tanh(ROOT * (upper + 0.044715 * upper * square))
    value = 0.5 * upper * (1.0 + bent)
    slope = 0.5 * (1.0 + bent) + 0.5 * upper * (1.0 - bent * bent) * ROOT * (
        1.0 + 3.0 * 0.044715 * square
    )
    return value, slope


class Sum:
    def __init__(
        self, links, left, right, total, into_a, into_b, place=None, beside=None
    ):
        self.links, self.left, self.right, self.total = links, left, right, total
        self.into_a, self.into_b, self.place, self.beside = into_a, into_b, place, beside
        self.size = total.shape[0] // 4

    def piece(self, source):
        depth = self.left.shape[0] * self.left.shape[1]
        return product_rows(
            self.left[:, :, columns(source, 256)].reshape(depth, 256),
            self.right[...].reshape(depth, self.right.shape[2]),
        )

    def fill(self, low, high):
        def step(number, carried):
            start = pl.multiple_of(number * 256, 256)
            source = start if self.place is None else self.place(number)
            made = self.piece(source)
            if self.beside is not None:
                made = made + self.beside[1][pl.ds(start, 256), :].astype(jnp.float32)
            self.total[pl.ds(start, 256), :] = made.astype(jnp.bfloat16)
            return carried

        lax.fori_loop(low // 256, high // 256, step, 0)

    def begin_beside(self):
        out, into = self.beside

        def step(number, carried):
            start = pl.multiple_of(number * 256, 256)
            out[pl.ds(start, 256), :] = self.piece(4 * self.size + start).astype(jnp.bfloat16)
            return carried

        lax.fori_loop(0, 4 * self.size // 256, step, 0)
        self.beside_copy = self.links.send(out, into, 0, 1)

    def begin(self):
        if self.beside is not None:
            self.beside_copy.wait_recv()
        self.fill(2 * self.size, 4 * self.size)
        self.copy = self.links.send(self.total.at[2 * self.size :], self.into_a, 0, 2)

    def keep(self):
        self.fill(0, 2 * self.size)

    def second(self):
        self.links.settle(self.copy)
        both = pl.ds(0, 2 * self.size)
        self.total[both, :] = (
            self.total[both, :].astype(jnp.float32) + self.into_a[...].astype(jnp.float32)
        ).astype(jnp.bfloat16)
        self.copy = self.links.send(
            self.total.at[self.size : 2 * self.size], self.into_b, 0, 6
        )

    def third(self):
        self.copy.wait_recv()
        self.ready = self.total.at[2 * self.size : 3 * self.size]
        self.ready[...] = (
            self.total[: self.size, :].astype(jnp.float32) + self.into_b[...].astype(jnp.float32)
        ).astype(jnp.bfloat16)

    def gather(self, ready, place):
        self.target = place
        own = place(self.links.dp_index)
        self.across = self.links.send(ready, own, 2, 0)
        self.core = self.links.send(ready, own, 1, 0)
        self.own = self.links.load(ready, own)

    def spread(self):
        self.across.wait_recv()
        other = self.target(flip(self.links.dp_index, 2))
        self.far = self.links.send(other, other, 1, 0)

    def finish(self):
        self.own.wait()
        arrived([self.core, self.far])


def layer_kernel(
    lengths, steps, mask_in, frames_in, skip_frames_in, cot_in, bias_in, w_skip, w_ada, w_qkv, w_out,
    w_up, w_down,
    result, grad_frames, grad_skip, sum_skip, sum_qkv, sum_out, sum_up, sum_down, small_all,
    embed_all,
    out_buf, up_buf, down_buf, weight_buf,
    joined_all, cot_all, first_all, attn_all, second_all, gated_all, upper_all, branch_all,
    packed_all, in_all,
    frames, skip, frame_mask, biases,
    first_own, embed_own, masks, table, packed_send, packed, attn_send, attn_low,
    attn_sum, residual, scale, grad_gated, second_low, gated, upper_parts, residual_mid, normal_mid,
    grad_mid, branch, grad_heads, query_recv, pair_recv, grad_packed, grad_in,
    query_total, turns, small, small_send, small_recv, up_ready,
    down_sum, down_a, down_b, up_sum, up_a, up_b, out_sum, out_a, out_b, skip_sum, skip_a, skip_b, skip_out, skip_beside,
    query_sum, query_a, query_b, key_sum, key_a, key_b, value_sum, value_a, value_b,
    send_sems, recv_sems, load_sems,
):
    links = Links(send_sems, recv_sems, load_sems)
    seq_index, dp_index = links.seq_index, links.dp_index
    rows, width = frames.shape
    hidden = grad_gated.shape[1]
    float32, bfloat16 = jnp.float32, jnp.bfloat16
    odd = bit(seq_index, 0)
    load_frames = links.load(frames_in, frames)
    load_skip_frames = links.load(skip_frames_in, skip)
    load_mask = links.load(mask_in, frame_mask)
    load_bias = links.load(bias_in, biases)
    load_skip = links.load(w_skip, down_buf.at[: 2 * width])
    load_ada = links.load(w_ada, weight_buf)
    enter = links.barrier()
    load_qkv = links.load(w_qkv, up_buf.at[:, : 3 * width])
    load_cot = links.load(cot_in, cot_all.at[0])
    cotangent = cot_all.at[0]

    def relative(source, target, size):
        for number, mask in enumerate(RELATIVE):
            target[:, number * size : (number + 1) * size] = source(flip(seq_index, mask))

    def joined_block(place):
        inside = columns(lax.rem(place, jnp.int32(4)) * 256, 256)
        return jnp.where(place < 4, frames[:, inside], skip[:, inside])

    ends = utterance_ends(lengths)
    utter = lax.broadcasted_iota(jnp.int32, embed_own.shape, 0)
    flow = jnp.zeros(embed_own.shape, float32)
    for number in range(steps.shape[1]):
        flow = jnp.where(utter == number, steps[0, number].astype(float32), flow)
    lane = lax.broadcasted_iota(jnp.int32, embed_own.shape, 1)
    half = width // 2
    frequency = jnp.exp((lane % half).astype(float32) * (-math.log(10000.0) / half))
    sine, cosine = turn_sine_cosine(1000.0 * (flow / TSTEPS) * frequency)
    embed = jnp.where(lane < half, sine, cosine)
    embed_own[...] = jnp.where(utter < steps.shape[1], embed, 0.0).astype(bfloat16)
    first_row = seq_index * rows
    cos_own, sin_own = rotary(ends, first_row, rows, 256)
    load_frames.wait()
    load_skip_frames.wait()
    relative(joined_block, joined_all.at[0], 256)
    load_mask.wait()
    masks[0] = jnp.broadcast_to(frame_mask[...], masks.shape[1:])
    load_cot.wait()
    enter()
    mask_copies = [links.send(masks.at[0], masks.at[m], 0, m) for m in range(1, 8)]
    cot_share = Share(links, cot_all, cotangent, cotangent)
    joined_across = links.send(joined_all.at[0], joined_all.at[2], 2, 0)
    joined_core = links.send(joined_all.at[0], joined_all.at[1], 1, 0)
    load_bias.wait()
    load_skip.wait()
    residual[...] = product(frames[...], down_buf[:width]) + product(
        skip[...], down_buf[width : 2 * width]
    )
    load_ada.wait()
    table[...] = product(embed_own[...], weight_buf[...]) + biases[:, : 2 * width].astype(float32)
    normal, unused = norm_parts(residual[...])
    row_index = first_row + lax.broadcasted_iota(jnp.int32, (rows, 1), 0)
    own_segment = segments(ends, row_index)
    spread_scale = jnp.zeros((rows, width), float32)
    spread_shift = jnp.zeros((rows, width), float32)
    for number in range(len(ends)):
        member = own_segment == number
        spread_scale = jnp.where(member, table[number : number + 1, :width], spread_scale)
        spread_shift = jnp.where(member, table[number : number + 1, width:], spread_shift)
    scale[...] = spread_scale
    second_low[...] = (normal * (1.0 + spread_scale) + spread_shift).astype(bfloat16)
    load_qkv.wait()
    packed_copies, later = [], []
    for far in (2, 1, 3, 0):
        pair = flip(lax.div(seq_index, jnp.int32(2)), far)
        parts = []
        for kind in range(3):
            part = product(second_low[...], up_buf[:, columns(kind * width + pair * 256, 256)])
            if kind < 2:
                part = part * cos_own + partner(part) * sin_own
            parts.append(part.astype(bfloat16))
        for side in range(2):
            for kind in range(3):
                packed_send[pair * 2 + side, :, kind * 128 : (kind + 1) * 128] = parts[kind][
                    :, side * 128 : (side + 1) * 128
                ]
        for mask in (2 * far, 2 * far + 1):
            if mask:
                place = flip(seq_index, mask)
                packed_copies.append(
                    links.send(
                        packed_send.at[place, :, :256], packed.at[seq_index, :, :256], 0, mask
                    )
                )
                later.append((place, mask))
    value_copies = [
        links.send(packed_send.at[place, :, 256:], packed.at[seq_index, :, 256:], 0, mask)
        for place, mask in later
    ]
    load_down_low = links.load(w_down.at[: 2 * width], down_buf.at[: 2 * width])
    load_down_high = links.load(w_down.at[2 * width :], down_buf.at[2 * width :])
    load_out = links.load(w_out, out_buf)
    load_up = links.load(w_up, up_buf)
    packed[seq_index] = packed_send[seq_index]
    relative(lambda place: second_low[:, columns(place * 128, 128)], first_own, 128)
    first_all[0] = first_own[:, : width // 2]
    embed_copies = [links.send(embed_own, embed_all.at[dp_index], m, 0) for m in (1, 2, 3)]
    embed_load = links.load(embed_own, embed_all.at[dp_index])
    load_down_low.wait()
    load_down_high.wait()

    def gated_step(step, carried):
        part = columns(step * 512, 512)
        grad_gated[:, part] = product_cols(cotangent[...], down_buf[part, :])
        return carried

    lax.fori_loop(0, hidden // 512, gated_step, 0)

    def table_step(place, carried):
        here = pl.ds(pl.multiple_of(place * rows, rows), rows)
        cosine, sine = rotary(ends, place * rows, rows, 128)
        turns[here, :128] = cosine
        turns[here, 128:] = sine
        return carried

    lax.fori_loop(0, 8, table_step, 0)
    arrived(mask_copies)
    arrived(packed_copies)
    key_index = lax.broadcasted_iota(jnp.int32, (1, 8 * rows), 1)
    key_segment = segments(ends, key_index)
    key_valid = jnp.concatenate(
        [masks[exclusive(seq_index, jnp.int32(number))][:1] for number in range(8)], axis=1
    )

    def weigh(place, carried):
        query = packed[place, :, :128]
        row_index = place * rows + lax.broadcasted_iota(jnp.int32, (rows, 1), 0)
        allowed = (segments(ends, row_index) == key_segment) & (
            (key_valid > 0) | (row_index == key_index)
        )
        keys = packed[:, :, 128:256].reshape(8 * rows, 128)
        here = pl.ds(pl.multiple_of(place * rows, rows), rows)
        for head in range(2):
            scores = product_cols(head_mask(query, head), keys) * (1.0 / math.sqrt(HEAD))
            scores = jnp.where(allowed, scores, masked_score)
            raised = jnp.exp(scores - jnp.max(scores, axis=1, keepdims=True))
            low = (raised / jnp.sum(raised, axis=1, keepdims=True)).astype(bfloat16)
            weight_buf[here, head * 1024 : (head + 1) * 1024] = low
        return carried

    def attend(place):
        values = packed[:, :, 256:].reshape(8 * rows, 128)
        total = jnp.zeros((rows, 128), float32)
        here = pl.ds(pl.multiple_of(place * rows, rows), rows)
        for head in range(2):
            low = weight_buf[here, head * 1024 : (head + 1) * 1024]
            total = total + product(low, head_mask(values, head))
        attn_sum[here, :] = total
        attn_send[place] = total.astype(bfloat16)

    def by_frames(source, target):
        base = links.used
        links.used += 8

        def copy_of(mask):
            place = exclusive(seq_index, mask)
            return pltpu.make_async_remote_copy(
                src_ref=source.at[place],
                dst_ref=target.at[seq_index],
                send_sem=send_sems.at[base + mask],
                recv_sem=recv_sems.at[base + mask],
                device_id=(dp_index, place),
                device_id_type=MESH,
            )

        return copy_of

    attn_copy = by_frames(attn_send, attn_low)

    def attend_step(step, carried):
        mask = lax.rem(step + 4, jnp.int32(8))
        attend(exclusive(seq_index, mask))
        attn_copy(mask).start()
        return carried

    lax.fori_loop(0, 8, weigh, 0)
    arrived(value_copies)
    lax.fori_loop(0, 4, attend_step, 0)
    lax.fori_loop(5, 8, attend_step, 0)
    attend(seq_index)
    attn_low[seq_index] = attn_send[seq_index]
    load_out.wait()
    for mask in range(1, 8):
        attn_copy(jnp.int32(mask)).wait()
    joined_attn = jnp.concatenate([attn_low[number] for number in range(8)], axis=1)
    residual_mid[...] = residual[...] + product(joined_attn, out_buf[...])
    normal, factor_mid = norm_parts(residual_mid[...])
    normal_mid[...] = normal
    gain_float = biases[:, 7 * width : 8 * width].astype(float32)
    second_all[0] = (normal * gain_float).astype(bfloat16)
    second_share = Share(links, second_all, second_all.at[0], second_all.at[0])
    cot_share.forward()
    small[8:] = jnp.zeros((8, small.shape[1]), float32)
    load_up.wait()

    def up_step(step, carried):
        part = columns(step * 512, 512)
        upper = product(second_all[0], up_buf[:, part]) + biases[
            :, columns(2 * width + step * 512, 512)
        ].astype(float32)
        value, slope = gelu_parts(upper)
        grad_upper = (grad_gated[:, part] * slope).astype(bfloat16)
        gated[:, part] = value.astype(bfloat16)
        upper_parts[:, part] = grad_upper
        small[
            pl.ds(8 + lax.div(step, jnp.int32(4)), 1),
            columns(lax.rem(step, jnp.int32(4)) * 512, 512),
        ] = jnp.sum(grad_upper.astype(float32), axis=0, keepdims=True)
        return carried

    lax.fori_loop(0, hidden // 512, up_step, 0)

    def second_step(step, total):
        part = columns(step * 512, 512)
        return total + product_cols(upper_parts[:, part], up_buf[:, part])

    grad_second = lax.fori_loop(
        0, hidden // 512, second_step, jnp.zeros((rows, width), float32)
    )
    grad_out = cotangent[...].astype(float32)
    normal = normal_mid[...]
    small[10:11, :width] = jnp.sum(grad_second * normal, axis=0, keepdims=True)
    small[10:11, width:] = jnp.sum(grad_out, axis=0, keepdims=True)
    grad_mid[...] = grad_out + norm_back(grad_second * gain_float, normal, factor_mid)
    branch[...] = grad_mid[...].astype(bfloat16)
    grad_attn = product_cols(branch[...], out_buf[...]).astype(bfloat16)
    grad_send = attn_send
    for number in range(8):
        grad_send[number] = grad_attn[:, number * 128 : (number + 1) * 128]
    head_copies = [
        links.send(grad_send.at[flip(seq_index, m)], grad_heads.at[seq_index], 0, m)
        for m in FAR_FIRST
    ]
    grad_heads[seq_index] = grad_send[seq_index]

    def quarters(source, slots, group=GROUP):
        size = slots.shape[2]
        slots[0] = source[:, columns(dp_index * size, size)]
        return [
            links.send(
                source.at[:, columns(flip(dp_index, m) * size, size)], slots.at[4 * v + m], m, v
            )
            for m, v in group
        ]

    second_share.forward()
    branch_copies = quarters(branch, branch_all)
    attn_own = upper_parts.at[:, 2 * width : 3 * width]
    relative(lambda place: attn_low[place], attn_own, 128)
    attn_all[0] = attn_own[:, : width // 2]
    attn_share = Share(links, attn_all, attn_all.at[0], attn_own.at[:, width // 2 :])
    cot_share.wait()
    joined_across.wait_recv()
    joined_far = links.send(joined_all.at[2], joined_all.at[3], 1, 0)
    second_share.wait()

    def again(first):
        units, spots = [], []
        for number in (first, first + 1):
            place = flip(seq_index, RELATIVE[number])
            units.append(place * 512 + dp_index * 128)
            spots.append(lax.div(place, jnp.int32(2)))
        weight_up = jnp.concatenate([up_buf[:, columns(unit, 128)] for unit in units], axis=1)
        weight_down = jnp.concatenate([down_buf[columns(unit, 128), :] for unit in units], axis=0)
        bias = jnp.concatenate(
            [biases[:, columns(2 * width + unit, 128)] for unit in units], axis=1
        ).astype(float32)

        def again_step(step, carried):
            both = pl.ds(2 * step, 2)
            upper = product(second_all[both].reshape(2 * rows, width), weight_up) + bias
            value, slope = gelu_parts(upper)
            grad = product_cols(cot_all[both].reshape(2 * rows, width), weight_down)
            gated_all[both, :, first * 128 : (first + 2) * 128] = value.astype(bfloat16).reshape(
                2, rows, 256
            )
            grad_upper = (grad * slope).astype(bfloat16).reshape(2, rows, 256)
            for side in range(2):
                upper_all[both, :, columns(spots[side] * 128, 128)] = grad_upper[
                    :, :, side * 128 : (side + 1) * 128
                ]
            return carried

        lax.fori_loop(0, 4, again_step, 0)

    def pair_place(number):
        base_pair = lax.div(seq_index, jnp.int32(2))
        step_a, step_b = lax.div(number, jnp.int32(2)), lax.rem(number, jnp.int32(2))
        two = jnp.int32(2)
        low_bit = lax.rem(bit(base_pair, 0) + step_a + step_b, two)
        high_bit = lax.rem(bit(base_pair, 1) + step_b, two)
        return (2 * high_bit + low_bit) * 256

    down = Sum(links, gated_all, cot_all, down_sum, down_a, down_b)
    up = Sum(links, second_all, upper_all, up_sum, up_a, up_b, pair_place)
    out = Sum(links, attn_all, branch_all, out_sum, out_a, out_b)
    query_part = Sum(links, first_all, packed_all.at[0], query_sum, query_a, query_b)
    key_part = Sum(links, first_all, packed_all.at[1], key_sum, key_a, key_b)
    value_part = Sum(links, first_all, packed_all.at[2], value_sum, value_a, value_b)
    skip_part = Sum(
        links, joined_all, in_all, skip_sum, skip_a, skip_b, beside=(skip_out, skip_beside)
    )
    again(2)
    down.begin()
    arrived(head_copies)
    links.sent_done(packed_copies + value_copies)
    links.sent_done(head_copies)
    query_send = attn_send
    pair_send = packed_send.at[:, :, :256]
    first_share = Share(links, first_all, first_all.at[0], first_own.at[:, width // 2 :])
    pair_copy = by_frames(pair_send, pair_recv)
    shrink = 1.0 / math.sqrt(HEAD)
    query_total[...] = jnp.zeros_like(query_total)

    def delta_step(place, carried):
        here = pl.ds(pl.multiple_of(place * rows, rows), rows)
        both = grad_heads[place].astype(float32) * attn_sum[here, :]
        for head in range(2):
            delta = jnp.sum(head_mask(both, head), axis=1, keepdims=True)
            grad_gated[:, columns(place * 512 + 256 + head * 128, 128)] = jnp.broadcast_to(
                delta, (rows, 128)
            )
        return carried

    lax.fori_loop(0, 8, delta_step, 0)

    def turned_back(total, place):
        here = pl.ds(pl.multiple_of(place * rows, rows), rows)
        cosine, sine = turns[here, :128], turns[here, 128:]
        total = total * shrink
        return (total * cosine - partner(total) * sine).astype(bfloat16)

    def back(pair):
        both = pl.ds(2 * pair, 2)
        keys = packed[both, :, 128:256].reshape(2 * rows, 128)
        values = packed[both, :, 256:].reshape(2 * rows, 128)
        queries = packed[:, :, :128].reshape(8 * rows, 128)
        grad = grad_heads[...].reshape(8 * rows, 128)
        grad_keys = jnp.zeros((2 * rows, 128), float32)
        grad_values = jnp.zeros((2 * rows, 128), float32)
        for head in range(2):
            low = weight_buf[:, columns(head * 1024 + pair * 256, 256)]
            grad_head = head_mask(grad, head)
            delta = jnp.concatenate(
                [
                    grad_gated[:, place * 512 + 256 + head * 128 : place * 512 + 384 + head * 128]
                    for place in range(8)
                ],
                axis=0,
            )
            delta = jnp.concatenate([delta, delta], axis=1)
            grad_scores = (
                low.astype(float32) * (product_cols(grad_head, values) - delta)
            ).astype(bfloat16)
            query_total[...] += product(grad_scores, head_mask(keys, head))
            grad_keys = grad_keys + product_rows(grad_scores, head_mask(queries, head))
            grad_values = grad_values + product_rows(low, grad_head)
        for side in range(2):
            place = 2 * pair + side
            part = slice(side * rows, (side + 1) * rows)
            pair_send[place, :, :128] = turned_back(grad_keys[part], place)
            pair_send[place, :, 128:] = grad_values[part].astype(bfloat16)

    own_pair = lax.div(seq_index, jnp.int32(2))

    def back_step(step, carried):
        far = step + 2 - 3 * lax.div(step, jnp.int32(2))
        back(lax.div(exclusive(seq_index, 2 * far), jnp.int32(2)))
        pair_copy(2 * far).start()
        pair_copy(2 * far + 1).start()
        return carried

    lax.fori_loop(0, 3, back_step, 0)
    back(own_pair)
    pair_copy(jnp.int32(1)).start()
    pair_recv[seq_index] = pair_send[seq_index]

    def query_step(place, carried):
        here = pl.ds(pl.multiple_of(place * rows, rows), rows)
        query_send[place] = turned_back(query_total[here, :], place)
        return carried

    lax.fori_loop(0, 8, query_step, 0)
    query_copies = [
        links.send(query_send.at[flip(seq_index, m)], query_recv.at[seq_index], 0, m)
        for m in FAR_FIRST
    ]
    query_recv[seq_index] = query_send[seq_index]
    again(0)
    load_qkv = links.load(w_qkv, up_buf.at[:, : 3 * width])
    up.begin()
    down.keep()

    def down_step(step, total):
        part = columns(step * 512, 512)
        return total + product(gated[:, part], down_buf[part, :])

    lower = lax.fori_loop(
        0,
        hidden // 512,
        down_step,
        residual_mid[...] + biases[:, 6 * width : 7 * width].astype(float32),
    )
    second_low[...] = lower.astype(bfloat16)
    out_loads = [links.load(second_low, result)]
    load_skip = links.load(w_skip, down_buf.at[: 2 * width])
    for mask in range(1, 8):
        pair_copy(jnp.int32(mask)).wait()
    for number in range(8):
        for kind in (1, 2):
            grad_packed[:, kind * width + number * 128 : kind * width + (number + 1) * 128] = (
                pair_recv[number, :, (kind - 1) * 128 : kind * 128]
            )
    key_parts = quarters(grad_packed.at[:, width : 2 * width], packed_all.at[1])
    value_parts = quarters(grad_packed.at[:, 2 * width :], packed_all.at[2])
    load_qkv.wait()

    def first_step(step, total):
        part = columns(step * 512, 512)
        return total + product_cols(grad_packed[:, part], up_buf[:, part])

    grad_first = lax.fori_loop(2, 6, first_step, jnp.zeros((rows, width), float32))
    scale_normal, factor = norm_parts(residual[...])
    down.second()
    arrived(query_copies)
    for number in range(8):
        grad_packed[:, number * 128 : (number + 1) * 128] = query_recv[number]
    grad_first = lax.fori_loop(0, 2, first_step, grad_first)
    grad_in[...] = (
        grad_mid[...] + norm_back(grad_first * (1.0 + scale[...]), scale_normal, factor)
    ).astype(bfloat16)
    in_copies = quarters(grad_in, in_all, ((2, 0), (3, 0), (1, 0)))
    query_parts = quarters(grad_packed.at[:, :width], packed_all.at[0])
    attn_share.forward()
    first_share.forward()
    up.keep()
    arrived(branch_copies)
    attn_share.wait()
    out.begin()
    out.keep()
    up.second()
    first_share.wait()
    arrived([joined_core, joined_far] + in_copies)
    skip_part.begin_beside()
    arrived(key_parts)
    key_part.begin()
    key_part.keep()
    arrived(value_parts)
    value_part.begin()
    value_part.keep()
    out.second()
    scaled = grad_first * scale_normal
    for number in range(len(ends)):
        member = own_segment == number
        small[number : number + 1, :width] = jnp.sum(
            jnp.where(member, scaled, 0.0), axis=0, keepdims=True
        )
        small[number : number + 1, width:] = jnp.sum(
            jnp.where(member, grad_first, 0.0), axis=0, keepdims=True
        )

    def small_start(number, mask):
        small_send[number] = small[...].astype(bfloat16)
        return links.send(small_send.at[number], small_recv.at[number], 0, mask)

    def small_add(copy, number):
        copy.wait_recv()
        small[...] = small_send[number].astype(float32) + small_recv[number].astype(float32)

    small_copy = small_start(0, 1)
    by_rows = lambda target, size: lambda index: target.at[pl.ds(index * size, size), :]
    by_cols = lambda start, target: lambda index: target.at[:, columns(start + index * 256, 256)]
    down.third()
    down.gather(down.ready, by_rows(sum_down, 128))
    arrived(query_parts)
    query_part.begin()
    query_part.keep()
    key_part.second()
    skip_part.begin()
    skip_part.keep()
    value_part.second()
    small_add(small_copy, 0)
    small_copy = small_start(1, 2)
    up.third()
    up_ready[odd] = up.ready[pl.ds(pl.multiple_of(odd * 128, 128), 128), :]
    up_other = links.send(
        up.ready.at[pl.ds(pl.multiple_of((1 - odd) * 128, 128), 128), :], up_ready.at[odd], 0, 1
    )
    out.third()
    out.gather(out.ready, by_cols(0, sum_out))
    down.spread()
    load_skip.wait()
    for held, target, start in ((residual, grad_frames, 0), (normal_mid, grad_skip, width)):
        held[...] = product_cols(grad_in[...], down_buf[start : start + width, :])
        out_loads.append(links.load(held, target))
    query_part.second()
    skip_part.second()
    small_add(small_copy, 1)
    small_copy = small_start(2, 6)
    up_other.wait_recv()
    up.gather(up_ready, lambda index: sum_up.at[index])
    out.spread()
    key_part.third()
    key_part.gather(key_part.ready, by_cols(width, sum_qkv))
    value_part.third()
    value_part.gather(value_part.ready, by_cols(2 * width, sum_qkv))
    query_part.third()
    query_part.gather(query_part.ready, by_cols(0, sum_qkv))
    skip_part.third()
    skip_part.gather(skip_part.ready, by_cols(0, sum_skip))
    small_add(small_copy, 2)
    small_send[3] = small[...].astype(bfloat16)
    small_copies = [
        links.send(small_send.at[3], small_all.at[dp_index], m, 0) for m in (3, 2, 1)
    ]
    small_load = links.load(small_send.at[3], small_all.at[dp_index])
    for each in (up, key_part, value_part, query_part, skip_part):
        each.spread()
    small_load.wait()
    embed_load.wait()
    for load in out_loads:
        load.wait()
    arrived(small_copies + embed_copies)
    for each in (down, up, out, query_part, key_part, skip_part, value_part):
        each.finish()
    links.drain()


def widen_kernel(
    result_in, frames_in, skip_in, sum_skip, sum_qkv, sum_out, sum_up, sum_down, small_all, embed_all,
    result, grad_frames, grad_skip, out_skip, out_ada, out_ada_bias, out_qkv, out_out, out_gain,
    out_up, out_up_bias, out_down, out_down_bias,
    low_result, low_frames, low_skip, low_w_skip, low_qkv, low_out, low_up, low_down, low_small, low_embed,
    full_skip, full_ada, full_qkv, full_out, full_up, full_down, in_sems, out_sems,
):
    float32 = jnp.float32
    seq_index = lax.axis_index("seq")
    sources = (sum_up, sum_down, sum_qkv, sum_skip, small_all, embed_all, sum_out)
    inside = (low_up, low_down, low_qkv, low_w_skip, low_small, low_embed, low_out)
    loads = [
        pltpu.make_async_copy(source, target, in_sems.at[number])
        for number, (source, target) in enumerate(zip(sources, inside, strict=True))
    ]
    for number in (6, 3, 2, 1, 0, 4, 5):
        loads[number].start()
    stores = []

    def store(source, target):
        copy = pltpu.make_async_copy(source, target, out_sems.at[len(stores)])
        copy.start()
        stores.append(copy)

    for whole, out in ((frames_in, grad_frames), (skip_in, grad_skip), (result_in, result)):
        store(whole, out)
    for number, low, full, out in (
        (6, low_out, full_out, out_out),
        (3, low_w_skip, full_skip, out_skip),
        (2, low_qkv, full_qkv, out_qkv),
        (1, low_down, full_down, out_down),
    ):
        loads[number].wait()
        full[...] = low[...].astype(float32)
        store(full, out)
    loads[0].wait()
    for quarter in range(4):
        for side in range(2):
            for level in range(4):
                start = (2 * level + side) * 512 + quarter * 128
                full_up[:, start : start + 128] = low_up[
                    quarter, side, :, level * 128 : (level + 1) * 128
                ].astype(float32)
    store(full_up, out_up)
    loads[4].wait()
    loads[5].wait()
    size = full_ada.shape[0]
    own = low_embed[:, :, columns(seq_index * size, size)].reshape(-1, size)
    full_ada[...] = product_rows(own, low_small[...].reshape(own.shape[0], full_ada.shape[1]))
    store(full_ada, out_ada)
    wide = low_small.shape[2]
    spot = columns(seq_index * 256, 256)
    bias = jnp.zeros((1, 256), float32)
    for number in range(4):
        bias = bias + jnp.sum(low_small[number, :8, spot].astype(float32), axis=0, keepdims=True)
    out_ada_bias[...] = bias
    upper = jnp.zeros((1, 512), float32)
    gain = jnp.zeros((1, 128), float32)
    down_bias = jnp.zeros((1, 128), float32)
    high = lax.div(seq_index, jnp.int32(4))
    for number in range(4):
        both = low_small[number, 8:, columns(lax.rem(seq_index, jnp.int32(4)) * 512, 512)].astype(float32)
        upper = upper + jnp.where(high == 0, both[:1], both[1:2])
        gain = gain + low_small[number, 8:, columns(seq_index * 128, 128)].astype(float32)[2:3]
        down_bias = down_bias + low_small[number, 8:, columns(wide // 2 + seq_index * 128, 128)].astype(float32)[2:3]
    out_up_bias[...] = upper
    out_gain[...] = gain
    out_down_bias[...] = down_bias
    for copy in stores:
        copy.wait()


def one_kernel(
    frames, skip, lengths, frame_mask, time_step, w_skip, w_ada, b_ada, w_qkv, w_out, norm_gain,
    w_up, b_up, w_down, b_down, cotangent,
):
    rows, width = frames.shape[1:]
    hidden = b_up.shape[0]
    float32, bfloat16 = jnp.float32, jnp.bfloat16
    shape = jax.ShapeDtypeStruct
    vmem = pl.BlockSpec(memory_space=pltpu.VMEM)
    smem = pl.BlockSpec(memory_space=pltpu.SMEM)
    anywhere = pl.BlockSpec(memory_space=pl.ANY)
    dma = pltpu.SemaphoreType.DMA
    low = lambda *size: pltpu.VMEM(size, bfloat16)
    full = lambda *size: pltpu.VMEM(size, float32)
    biases = jnp.concatenate([b_ada, b_up, b_down, norm_gain])[None]
    sums = ((512, 1024), (1024, 512), (512, 256), (1024, 256), (512, 256), (512, 256), (512, 256))
    sum_scratch = [low(tall // part, wide) for tall, wide in sums for part in (1, 2, 4)]
    sum_scratch[12:12] = [low(1024, 256), low(1024, 256)]
    outs = (
        (shape((rows, width), bfloat16), anywhere),
        (shape((rows, width), float32), anywhere),
        (shape((rows, width), float32), anywhere),
        (shape((2 * width // 8, width), bfloat16), anywhere),
        (shape((width // 8, 3 * width), bfloat16), anywhere),
        (shape((width // 8, width), bfloat16), anywhere),
        (shape((4, 2, width // 8, hidden // 8), bfloat16), anywhere),
        (shape((hidden // 8, width), bfloat16), anywhere),
        (shape((4, 16, 2 * width), bfloat16), anywhere),
        (shape((4, 16, width), bfloat16), anywhere),
    )
    parts = pl.pallas_call(
        layer_kernel,
        out_shape=tuple(item[0] for item in outs),
        in_specs=[smem, smem] + [anywhere] * 11,
        out_specs=tuple(item[1] for item in outs),
        scratch_shapes=[
            low(*w_out.shape), low(*w_up.shape), low(*w_down.shape), low(8 * rows, 2 * width),
            low(4, rows, 2 * width), low(8, rows, width), low(8, rows, width // 2), low(8, rows, width // 2),
            low(8, rows, width), low(8, rows, 512), low(8, rows, 512), low(8, rows, 256),
            low(3, 8, rows, 256), low(4, rows, 256),
            low(rows, width), low(rows, width), pltpu.VMEM((1, rows), jnp.int32), low(1, 8 * width),
            low(rows, width), low(16, width), pltpu.VMEM((8, 8, rows), jnp.int32),
            full(16, 2 * width), low(8, rows, 384), low(8, rows, 384), low(8, rows, 128), low(8, rows, 128),
            full(8 * rows, 128), full(rows, width), full(rows, width), full(rows, hidden), low(rows, width),
            low(rows, hidden), low(rows, hidden), full(rows, width), full(rows, width),
            full(rows, width), low(rows, width), low(8, rows, 128), low(8, rows, 128), low(8, rows, 256), low(rows, 3 * width), low(rows, width), full(8 * rows, 128), full(8 * rows, 256),
            full(16, 2 * width), low(4, 16, 2 * width), low(3, 16, 2 * width),
            low(2, rows, 512),
            *sum_scratch,
            dma((168,)), dma((168,)), dma((28,)),
        ],
        compiler_params=pltpu.CompilerParams(
            collective_id=0, has_side_effects=True, vmem_limit_bytes=62 * MIB
        ),
        name="layer",
    )(
        lengths, time_step, frame_mask, frames[0], skip[0], cotangent[0], biases, w_skip, w_ada,
        w_qkv, w_out, w_up, w_down,
    )

    last_outs = (
        (shape((rows, width), bfloat16), anywhere),
        (shape((rows, width), float32), anywhere),
        (shape((rows, width), float32), anywhere),
        (shape((2 * width // 8, width), float32), anywhere),
        (shape((width // 8, 2 * width), float32), anywhere),
        (shape((1, 2 * width // 8), float32), vmem),
        (shape((width // 8, 3 * width), float32), anywhere),
        (shape((width // 8, width), float32), anywhere),
        (shape((1, width // 8), float32), vmem),
        (shape((width // 8, hidden), float32), anywhere),
        (shape((1, hidden // 8), float32), vmem),
        (shape((hidden // 8, width), float32), anywhere),
        (shape((1, width // 8), float32), vmem),
    )
    scratch = [pltpu.VMEM(item[0].shape, item[0].dtype) for item in outs]
    scratch += [full(*last_outs[number][0].shape) for number in (3, 4, 6, 7, 9, 11)]
    widened = pl.pallas_call(
        widen_kernel,
        out_shape=tuple(item[0] for item in last_outs),
        in_specs=[anywhere] * len(outs),
        out_specs=tuple(item[1] for item in last_outs),
        scratch_shapes=[*scratch, dma((10,)), dma((12,))],
        compiler_params=pltpu.CompilerParams(vmem_limit_bytes=60 * MIB),
        name="widen",
    )(*parts)
    return tuple(
        item[None] if number < 3 else item.reshape(-1) if item.shape[0] == 1 else item
        for number, item in enumerate(widened)
    )


def solution(mesh):
    placed = (
        P("dp", "seq", None),
        P("dp", "seq", None),
        P("dp", None),
        P("dp", "seq"),
        P("dp", None),
        P(),
        P(),
        P(),
        P(),
        P(),
        P(),
        P(),
        P(),
        P(),
        P(),
        P("dp", "seq", None),
    )
    split_heads = mesh.shape["dp"] == 4 and mesh.shape["seq"] == len(RELATIVE)
    return jax.shard_map(
        one_kernel if split_heads else on_device,
        mesh=mesh,
        in_specs=placed,
        out_specs=(
            P("dp", "seq", None),
            P("dp", "seq", None),
            P("dp", "seq", None),
            P("seq", None),
            P("seq", None),
            P("seq"),
            P("seq", None),
            P("seq", None),
            P("seq"),
            P("seq", None),
            P("seq"),
            P("seq", None),
            P("seq"),
        ),
        check_vma=False,
    )
```
